32 devices in a mesh: dp: 8 (over z, x), blk: 4 (over y, core).
Axes of the slice: x: 2, y: 2, z: 4, core: 2. Of those that a mesh axis runs over, the one named last changes fastest.
Arguments:
- hidden_in: bfloat16 [32, 512, 768], P('dp', 'blk'), may hold values from -6 to 6
- pad_mask: int32 [32, 512], P('dp', 'blk'), may hold values from 0 to 1, as said below
- masked_flag: int32 [32, 512], P('dp', 'blk'), may hold values 0 or 1
- replaced_flag: int32 [32, 512], P('dp', 'blk'), may hold values 0 or 1
- mask_vector: float32 [768], replicated, may hold values from -4 to 4
- replace_vector: float32 [768], replicated, may hold values from -3 to 3
- w_query: bfloat16 [768, 768], replicated, may hold values from -0.3125 to 0.3125
- b_query: float32 [768], replicated, may hold values from -2 to 2
- w_key: bfloat16 [768, 768], replicated, may hold values from -0.3125 to 0.3125
- w_value: bfloat16 [768, 768], replicated, may hold values from -0.21875 to 0.21875
- b_value: float32 [768], replicated, may hold values from -2 to 2
- w_out: bfloat16 [768, 768], replicated, may hold values from -1.25 to 1.25
- b_out: float32 [768], replicated, may hold values from -3 to 3
- gain_one: float32 [768], replicated, may hold values from 0.1 to 1.9
- shift_one: float32 [768], replicated, may hold values from -3 to 3
- w_up: bfloat16 [768, 3072], replicated, may hold values from -0.21875 to 0.21875
- b_up: float32 [3072], replicated, may hold values from -3 to 3
- w_down: bfloat16 [3072, 768], replicated, may hold values from -0.15625 to 0.15625
- b_down: float32 [768], replicated, may hold values from -3 to 3
- gain_two: float32 [768], replicated, may hold values from 0.1 to 1.9
- shift_two: float32 [768], replicated, may hold values from -3 to 3
- out_grad: bfloat16 [32, 512, 768], P('dp', 'blk'), may hold values from -6 to 6
Outputs:
- hidden_out: bfloat16 [32, 512, 768], P('dp', 'blk')
- grad_in: bfloat16 [32, 512, 768], P('dp', 'blk')
- grad_mask_vector: float32 [768], replicated
- grad_replace_vector: float32 [768], replicated
- grad_w_query: float32 [768, 768], P('dp', 'blk')
- grad_b_query: float32 [768], replicated
- grad_w_key: float32 [768, 768], P('dp', 'blk')
- grad_w_value: float32 [768, 768], P('dp', 'blk')
- grad_b_value: float32 [768], replicated
- grad_w_out: float32 [768, 768], P('dp', 'blk')
- grad_b_out: float32 [768], replicated
- grad_gain_one: float32 [768], replicated
- grad_shift_one: float32 [768], replicated
- grad_w_up: float32 [768, 3072], P('dp', 'blk')
- grad_b_up: float32 [3072], replicated
- grad_w_down: float32 [3072, 768], P('dp', 'blk')
- grad_b_down: float32 [768], replicated
- grad_gain_two: float32 [768], replicated
- grad_shift_two: float32 [768], replicated
The draws below stay inside these ranges and needn't reach their ends.
Inputs may be any that keep to these rules, and one draw needn't show every extreme that they name: `pad_mask`: in each document the ones form a prefix of 64 or more slots; among the 4 documents of every index of dp, one has ones in all slots.
All inputs are finite; a program needn't handle non-finite values. No bound on the sum of `masked_flag` or of `replaced_flag` on one device may be relied on, other than what follows from the above.
Results may differ from the reference program's by a relative error of at most 0.02.
Values may be sent and summed in bfloat16 or wider, within the bound.
No kernel may reach another device: no remote copies, remote signals or barrier semaphores. Data moves between devices by JAX's collectives and lax.ppermute only.
A program may use at most 192 MiB of HBM per device.

```python
import math
import jax
import jax.numpy as jnp
from jax import lax

D = 768
HEADS = 12
HEAD_SIZE = 64
FF = 3072
DOC_LEN = 512
DOCS_DEV = 4
DOCUMENTS = 32


def draw_pad_mask(key, part):
    key = jax.random.fold_in(key, 11)
    length_key, chosen_key = jax.random.split(key)
    lengths = jax.random.randint(length_key, (DOCUMENTS,), DOC_LEN // 8, DOC_LEN + 1)
    chosen = jax.random.randint(chosen_key, (DOCUMENTS // DOCS_DEV, 1), 0, DOCS_DEV)
    full_slot = (jnp.arange(DOCS_DEV)[None, :] == chosen).reshape(-1)
    lengths = jnp.where(full_slot, DOC_LEN, lengths)
    positions = jnp.arange(DOC_LEN)[None, :]
    return (positions < lengths[:, None]).astype(jnp.int32)


def place_ends(result, stream_key, least, high):
    place = [jax.random.randint(jax.random.fold_in(stream_key, axis), (), 0, length) for axis, length in enumerate(result.shape)]
    main_axis = result.shape.index(max(result.shape))
    beside = place[:main_axis] + [(place[main_axis] + 1) % result.shape[main_axis]] + place[main_axis + 1:]
    return result.at[tuple(place)].set(least).at[tuple(beside)].set(high)


def block_levels(key, extent, shards, low, top_value):
    def one(dim, shards_of):
        heights = jax.random.uniform(jax.random.fold_in(jax.random.fold_in(key, 6), dim), (shards_of,), jnp.float32, low / len(shards), top_value / len(shards))
        return jnp.repeat(jnp.exp(heights), extent[dim] // shards_of).reshape((-1,) + (1,) * (len(extent) - dim - 1))

    loudness = one(*shards[0])
    for cut in shards[1:]:
        loudness = loudness * one(*cut)
    return loudness


def gaussian(stream_key, dims, scale, most, shards=(), dtype=jnp.bfloat16):
    result = jax.random.normal(stream_key, dims, jnp.float32) * scale
    if len(shards) > 0:
        result = block_levels(stream_key, dims, shards, -0.22, 0.18) * result
    return jnp.clip(result, min=-most, max=most).astype(dtype)


def setup_inputs(seed: int = 0) -> dict:
    streams_of = jax.random.split(jax.random.key(seed), 23)
    return {
        "hidden_in": gaussian(streams_of[0], (DOCUMENTS, DOC_LEN, D), 1.0, 6.0, ((0, 8), (1, 4))),
        "pad_mask": draw_pad_mask(jax.random.fold_in(streams_of[22], 71), 0),
        "masked_flag": place_ends((jax.random.randint(streams_of[2], (DOCUMENTS, DOC_LEN), 0, 20) < 3).astype(jnp.int32), jax.random.fold_in(streams_of[2], 1), 0, 1),
        "replaced_flag": place_ends((jax.random.randint(streams_of[3], (DOCUMENTS, DOC_LEN), 0, 10) < 1).astype(jnp.int32), jax.random.fold_in(streams_of[3], 1), 0, 1),
        "mask_vector": gaussian(streams_of[4], (D,), 1.0, 4.0, (), jnp.float32),
        "replace_vector": gaussian(streams_of[5], (D,), 0.5, 3.0, (), jnp.float32),
        "w_query": gaussian(streams_of[6], (D, D), (D // 2) ** -0.5, 0.3125),
        "b_query": gaussian(streams_of[7], (D,), 0.3, 2.0, (), jnp.float32),
        "w_key": gaussian(streams_of[8], (D, D), (D // 2) ** -0.5, 0.3125),
        "w_value": gaussian(streams_of[9], (D, D), D ** -0.5, 0.21875),
        "b_value": gaussian(streams_of[10], (D,), 0.3, 2.0, (), jnp.float32),
        "w_out": gaussian(streams_of[11], (D, D), (D // 32) ** -0.5, 1.25),
        "b_out": gaussian(streams_of[12], (D,), 0.5, 3.0, (), jnp.float32),
        "gain_one": jnp.clip(1.0 + 0.18 * jax.random.normal(streams_of[13], (D,), jnp.float32), 0.1, 1.9),
        "shift_one": gaussian(streams_of[14], (D,), 0.5, 3.0, (), jnp.float32),
        "w_up": gaussian(streams_of[15], (D, FF), D ** -0.5, 0.21875),
        "b_up": gaussian(streams_of[16], (FF,), 0.5, 3.0, (), jnp.float32),
        "w_down": gaussian(streams_of[17], (FF, D), (FF // 2) ** -0.5, 0.15625),
        "b_down": gaussian(streams_of[18], (D,), 0.5, 3.0, (), jnp.float32),
        "gain_two": jnp.clip(1.0 + 0.18 * jax.random.normal(streams_of[19], (D,), jnp.float32), 0.1, 1.9),
        "shift_two": gaussian(streams_of[20], (D,), 0.5, 3.0, (), jnp.float32),
        "out_grad": gaussian(streams_of[21], (DOCUMENTS, DOC_LEN, D), 1.0, 6.0, ((0, 8), (1, 4))),
    }


minus_huge = -1e+30
epsilon = 1e-05
log_two_e = 1.4426950408889634
highest = lax.Precision.HIGHEST

@jax.custom_vjp
def low(v):
    return lax.optimization_barrier(v.astype(jnp.bfloat16)).astype(jnp.float32)

@jax.custom_vjp
def low_back(v):
    return v

def low_keep(v):
    return (low(v), None)

def low_pass(kept, grad):
    return (grad,)

def back_keep(v):
    return (v, None)

def back_low(kept, grad):
    return (low(grad),)
low.defvjp(low_keep, low_pass)
low_back.defvjp(back_keep, back_low)

def matmul(left_side, right_side):
    return jnp.dot(left_side, right_side, preferred_element_type=jnp.float32, precision=highest)

def norm_rows(values, gain_vector, shift_vector):
    row_mean = lax.optimization_barrier(jnp.mean(values, axis=-1, keepdims=True))
    centred = values - row_mean
    spread = lax.optimization_barrier(jnp.mean(centred * centred, axis=-1, keepdims=True))
    return centred * lax.rsqrt(spread + epsilon) * gain_vector + shift_vector

def attend_group(grouped):
    queries, keyed, valued, key_valid = grouped
    raw_scores = low_back(jnp.einsum('gqhe,gkhe->ghqk', queries, keyed, precision=highest) * HEAD_SIZE ** (-0.5))
    scores = jnp.where(key_valid[:, None, None, :] > 0, raw_scores * log_two_e, minus_huge)
    row_peak = jnp.ceil(lax.optimization_barrier(jnp.max(scores, axis=-1, keepdims=True)))
    weights = jnp.where(key_valid[:, None, None, :] > 0, jnp.exp2(scores - row_peak), 0.0)
    row_total = lax.optimization_barrier(jnp.sum(weights, axis=-1))
    summed = low_back(jnp.einsum('ghqk,gkhe->gqhe', low(weights), valued, precision=highest))
    return summed / jnp.transpose(row_total, (0, 2, 1))[..., None]

def regroup(values, group_docs):
    return values.reshape(DOCUMENTS // group_docs, group_docs, DOC_LEN, HEADS, HEAD_SIZE)

def forward(hidden, parameters, masked_flag, replaced_flag, pad_mask):
    mask_vector, replace_vector, w_query, b_query, w_key, w_value, b_value, w_out, b_out, gain_one, shift_one, w_up, b_up, w_down, b_down, gain_two, shift_two = parameters
    masked = masked_flag.reshape(-1, 1) > 0
    replaced = replaced_flag.reshape(-1, 1).astype(jnp.float32)
    start_rows = jnp.where(masked, mask_vector, hidden.reshape(-1, D)) + replaced * replace_vector
    entries = low(start_rows)
    queries = low(low_back(matmul(entries, w_query) + b_query))
    keyed = low(low_back(matmul(entries, w_key)))
    valued = low(low_back(matmul(entries, w_value) + b_value))
    group_docs = math.gcd(DOCUMENTS, 8)
    key_valid = pad_mask.reshape(DOCUMENTS // group_docs, group_docs, DOC_LEN)
    attended = lax.map(jax.checkpoint(attend_group), (regroup(queries, group_docs), regroup(keyed, group_docs), regroup(valued, group_docs), key_valid))
    context = low(attended.reshape(-1, D))
    branch = low_back(matmul(context, w_out) + b_out)
    normed = norm_rows(start_rows + branch, gain_one, shift_one)
    lifted = low_back(matmul(low(normed), w_up) + b_up)
    active = low(jax.nn.gelu(lifted, approximate=False))
    dropped = low_back(matmul(active, w_down) + b_down)
    return norm_rows(normed + dropped, gain_two, shift_two)

def reference(hidden_in, pad_mask, masked_flag, replaced_flag, mask_vector, replace_vector, w_query, b_query, w_key, w_value, b_value, w_out, b_out, gain_one, shift_one, w_up, b_up, w_down, b_down, gain_two, shift_two, out_grad):
    parameters = (mask_vector, replace_vector, w_query.astype(jnp.float32), b_query, w_key.astype(jnp.float32), w_value.astype(jnp.float32), b_value, w_out.astype(jnp.float32), b_out, gain_one, shift_one, w_up.astype(jnp.float32), b_up, w_down.astype(jnp.float32), b_down, gain_two, shift_two)

    def layer(hidden, weights_all):
        return forward(hidden, weights_all, masked_flag, replaced_flag, pad_mask)
    output, pullback = jax.vjp(layer, hidden_in.astype(jnp.float32), parameters)
    grad_hidden, grads_all = pullback(out_grad.astype(jnp.float32).reshape(-1, D))
    grad_mask_vector, grad_replace_vector, grad_w_query, grad_b_query, grad_w_key, grad_w_value, grad_b_value, grad_w_out, grad_b_out, grad_gain_one, grad_shift_one, grad_w_up, grad_b_up, grad_w_down, grad_b_down, grad_gain_two, grad_shift_two = grads_all
    return (output.reshape(DOCUMENTS, DOC_LEN, D).astype(jnp.bfloat16), grad_hidden.astype(jnp.bfloat16), grad_mask_vector, grad_replace_vector, grad_w_query, grad_b_query, grad_w_key, grad_w_value, grad_b_value, grad_w_out, grad_b_out, grad_gain_one, grad_shift_one, grad_w_up, grad_b_up, grad_w_down, grad_b_down, grad_gain_two, grad_shift_two)
```

```python
import jax
import jax.numpy as jnp
from jax import lax
from jax.experimental import pallas as pl
from jax.experimental.pallas import tpu as pltpu
from jax.sharding import PartitionSpec as P

D = 768
HEADS = 12
HEAD_SIZE = 64
FF = 3072
PIECES = 4
MIB = 1024 * 1024

epsilon = 1e-05
log_two_e = 1.4426950408889634
query_scale = HEAD_SIZE ** (-0.5) * log_two_e
left_out = -1e30

f32 = jnp.float32
bf16 = jnp.bfloat16

VMEM = pl.BlockSpec(memory_space=pltpu.VMEM)
SMEM = pl.BlockSpec(memory_space=pltpu.SMEM)
HBM = pl.BlockSpec(memory_space=pl.ANY)


def shape(dims, dtype):
    return jax.ShapeDtypeStruct(dims, dtype)


def dot(left_side, right_side):
    return jnp.dot(left_side, right_side, preferred_element_type=f32)


def dot_right_t(left_side, right_side):
    return lax.dot_general(
        left_side, right_side, (((1,), (1,)), ((), ())), preferred_element_type=f32
    )


def lane_half(rows, which):
    lane = lax.broadcasted_iota(jnp.int32, (rows, 2 * HEAD_SIZE), 1)
    return (lane < HEAD_SIZE) if which == 0 else (lane >= HEAD_SIZE)


def normal_cdf(values):
    bell = jnp.exp2(values * values * (-0.5 * log_two_e))
    t = 1.0 / (1.0 + jnp.abs(values) * (0.3275911 * 0.7071067811865476))
    poly = 0.5 * 1.061405429 * t + 0.5 * -1.453152027
    poly = poly * t + 0.5 * 1.421413741
    poly = poly * t + 0.5 * -0.284496736
    poly = poly * t + 0.5 * 0.254829592
    tail = poly * t * bell
    return jnp.where(values >= 0, 1.0 - tail, tail), bell


def norm(values):
    centred = values - jnp.mean(values, axis=-1, keepdims=True)
    spread = jnp.mean(centred * centred, axis=-1, keepdims=True)
    scale = lax.rsqrt(spread + epsilon)
    return centred * scale, scale


def norm_back(grad, hat, scale, gain):
    lifted = grad * gain
    mean_one = jnp.mean(lifted, axis=-1, keepdims=True)
    mean_two = jnp.mean(lifted * hat, axis=-1, keepdims=True)
    return scale * (lifted - mean_one - hat * mean_two)


def forward_kernel(
    piece0,
    piece1,
    piece2,
    piece3,
    mask_vector,
    replace_vector,
    w_query,
    b_query,
    w_key,
    w_value,
    b_value,
    w_out_hbm,
    b_out,
    gain_one,
    shift_one,
    w_up_hbm,
    b_up,
    w_down_hbm,
    b_down,
    gain_two,
    shift_two,
    entries,
    queries,
    keyed,
    valued,
    context,
    key_bias,
    stats,
    hat_one,
    scale_one,
    normed_low,
    active,
    slope,
    hat_two,
    scale_two,
    hidden_out,
    flags_out,
    start,
    value_t,
    context_t,
    dropped,
    w_out,
    w_up,
    w_down,
    sems,
):
    copies = [
        pltpu.make_async_copy(w_out_hbm, w_out, sems.at[0]),
        pltpu.make_async_copy(w_up_hbm, w_up, sems.at[1]),
        pltpu.make_async_copy(w_down_hbm, w_down, sems.at[2]),
    ]
    for copy in copies:
        copy.start()
    seq = piece0.shape[0] - 16
    rows = PIECES * seq
    row_id = lax.broadcasted_iota(jnp.int32, (seq, seq), 0)
    col_id = lax.broadcasted_iota(jnp.int32, (seq, seq), 1)
    eye = (row_id == col_id).astype(bf16)
    for index, piece in enumerate((piece0, piece1, piece2, piece3)):
        where = pl.ds(index * seq, seq)
        flags = piece[pl.ds(seq, 16), pl.ds(0, seq)]
        columns = dot_right_t(eye, flags)
        flags_out[where, :] = columns
        key_bias[where, :] = jnp.where(
            lax.broadcasted_iota(jnp.int32, (seq, 128), 1) == 0,
            (1.0 - columns[:, 0:1]) * left_out,
            0.0,
        ).astype(bf16)
        rows_here = jnp.where(
            columns[:, 1:2] > 0, mask_vector[...], piece[pl.ds(0, seq), :].astype(f32)
        )
        rows_here = rows_here + columns[:, 2:3] * replace_vector[...]
        start[where, :] = rows_here
        entries[where, :] = rows_here.astype(bf16)
    queries[...] = ((dot(entries[...], w_query[...]) + b_query[...]) * query_scale).astype(bf16)
    keyed[...] = dot(entries[...], w_key[...]).astype(bf16)
    valued[...] = (dot(entries[...], w_value[...]) + b_value[...]).astype(bf16)
    value_t[...] = valued[...].T

    ones_lane = (lax.broadcasted_iota(jnp.int32, (rows, 128), 1) == 0).astype(bf16)
    ones_rows = jnp.ones((16, rows), bf16)

    def pair_step(pair, carry):
        columns = pl.ds(pl.multiple_of(pair * 128, 128), 128)
        query_pair = jnp.concatenate([queries[:, columns], ones_lane], axis=1)
        key_pair = keyed[:, columns]
        for which in range(2):
            key_head = jnp.where(lane_half(rows, which), key_pair, jnp.zeros_like(key_pair))
            key_head = jnp.concatenate([key_head, key_bias[...]], axis=1)
            scores = dot_right_t(key_head, query_pair)
            peak = jnp.max(scores, axis=0, keepdims=True)
            weights = jnp.exp2(scores - peak).astype(bf16)
            head_rows = pl.ds(pl.multiple_of(pair * 128 + which * HEAD_SIZE, HEAD_SIZE), HEAD_SIZE)
            values = jnp.concatenate([value_t[head_rows, :], ones_rows], axis=0)
            summed = dot(values, weights)
            total = summed[HEAD_SIZE : HEAD_SIZE + 1, :]
            context_t[head_rows, :] = (summed[:HEAD_SIZE, :] * (1.0 / total)).astype(bf16)
            stats[pl.ds(pair * 2 + which, 1), :] = peak + jnp.log2(total)
        return carry

    lax.fori_loop(0, HEADS // 2, pair_step, 0)
    context[...] = context_t[...].T
    copies[0].wait()
    half = rows // 2
    for index in range(2):
        where = pl.ds(index * half, half)
        branch = dot(context[where, :], w_out[...]) + b_out[...]
        hat, scale = norm(start[where, :] + branch)
        hat_one[where, :] = hat
        scale_one[where, :] = scale
        normed_low[where, :] = (hat * gain_one[...] + shift_one[...]).astype(bf16)
    copies[1].wait()
    copies[2].wait()
    chunk = 512
    for index in range(FF // chunk):
        columns = pl.ds(index * chunk, chunk)
        lifted = dot(normed_low[...], w_up[:, columns]) + b_up[:, columns]
        cdf, bell = normal_cdf(lifted)
        act = (lifted * cdf).astype(bf16)
        active[:, columns] = act
        slope[:, columns] = (cdf + lifted * bell * 0.3989422804014327).astype(bf16)
        part = dot(act, w_down[columns, :])
        if index == 0:
            dropped[...] = part
        else:
            dropped[...] += part
    for index in range(2):
        where = pl.ds(index * half, half)
        normed = hat_one[where, :] * gain_one[...] + shift_one[...]
        hat, scale = norm(normed + dropped[where, :] + b_down[...])
        hat_two[where, :] = hat
        scale_two[where, :] = scale
        hidden_out[where, :] = (hat * gain_two[...] + shift_two[...]).astype(bf16)


def forward(pieces, weights):
    seq = pieces[0].shape[0] - 16
    rows = PIECES * seq
    (
        mask_vector,
        replace_vector,
        w_query,
        b_query,
        w_key,
        w_value,
        b_value,
        w_out,
        b_out,
        gain_one,
        shift_one,
        w_up,
        b_up,
        w_down,
        b_down,
        gain_two,
        shift_two,
    ) = weights
    specs = [VMEM] * 21
    specs[11] = specs[15] = specs[17] = HBM
    return pl.pallas_call(
        forward_kernel,
        out_shape=(
            shape((rows, D), bf16),
            shape((rows, D), bf16),
            shape((rows, D), bf16),
            shape((rows, D), bf16),
            shape((rows, D), bf16),
            shape((rows, 128), bf16),
            shape((16, rows), f32),
            shape((rows, D), f32),
            shape((rows, 1), f32),
            shape((rows, D), bf16),
            shape((rows, FF), bf16),
            shape((rows, FF), bf16),
            shape((rows, D), f32),
            shape((rows, 1), f32),
            shape((rows, D), bf16),
            shape((rows, 16), f32),
        ),
        in_specs=specs,
        out_specs=(VMEM,) * 16,
        scratch_shapes=[
            pltpu.VMEM((rows, D), f32),
            pltpu.VMEM((D, rows), bf16),
            pltpu.VMEM((D, rows), bf16),
            pltpu.VMEM((rows, D), f32),
            pltpu.VMEM((D, D), bf16),
            pltpu.VMEM((D, FF), bf16),
            pltpu.VMEM((FF, D), bf16),
            pltpu.SemaphoreType.DMA((3,)),
        ],
        compiler_params=pltpu.CompilerParams(vmem_limit_bytes=60 * MIB),
        name="forward_layer",
    )(
        *pieces,
        mask_vector,
        replace_vector,
        w_query,
        b_query,
        w_key,
        w_value,
        b_value,
        w_out,
        b_out,
        gain_one,
        shift_one,
        w_up,
        b_up,
        w_down,
        b_down,
        gain_two,
        shift_two,
    )


def sums(values):
    return jnp.sum(values, axis=0, keepdims=True)


def down_kernel(
    place,
    piece0,
    piece1,
    piece2,
    piece3,
    hat_two,
    scale_two,
    gain_two,
    active,
    grad_z_two,
    grad_dropped,
    sent,
    kept,
    vectors,
    grad_t,
):
    seq = piece0.shape[0]
    core = place[0]
    totals = [jnp.zeros((1, D), f32)] * 3
    for index, piece in enumerate((piece0, piece1, piece2, piece3)):
        where = pl.ds(index * seq, seq)
        grad = piece[...].astype(f32)
        hat = hat_two[where, :]
        grad_z = norm_back(grad, hat, scale_two[where, :], gain_two[...])
        low = grad_z.astype(bf16)
        grad_z_two[where, :] = grad_z
        grad_dropped[where, :] = low
        terms = (grad * hat, grad, low.astype(f32))
        totals = [total + sums(term) for total, term in zip(totals, terms)]
    for index in range(3):
        vectors[pl.ds(index, 1), :] = totals[index]
    block = D // PIECES
    turned = grad_dropped[...].T
    grad_t[...] = turned
    order = [1 - core, 3 - core, core, 2 + core]
    left_side = jnp.concatenate(
        [grad_t[pl.ds(pl.multiple_of(index * block, block), block), :] for index in order], axis=0
    )
    half = block // 2
    for pair in range(4):
        part = dot(left_side, active[:, pl.ds(pair * D, D)]).astype(bf16)
        for dp in range(2):
            for y in range(2):
                for ab in range(2):
                    low = y * block + ab * half
                    columns = slice(dp * 384, dp * 384 + 384)
                    sent[y, ab, pair * 2 + dp] = part[low : low + half, columns]
                    low += 2 * block
                    kept[y, ab, pair * 2 + dp] = part[low : low + half, columns]


TILES = (2, 2, 8, 96, 384)


def down_back(place, pieces, hat_two, scale_two, gain_two, active):
    rows = PIECES * pieces[0].shape[0]
    return pl.pallas_call(
        down_kernel,
        out_shape=(
            shape((rows, D), f32),
            shape((rows, D), bf16),
            shape(TILES, bf16),
            shape(TILES, bf16),
            shape((8, D), f32),
        ),
        in_specs=[SMEM] + [VMEM] * 8,
        out_specs=(VMEM,) * 5,
        scratch_shapes=[pltpu.VMEM((D, rows), bf16)],
        compiler_params=pltpu.CompilerParams(vmem_limit_bytes=60 * MIB),
        name="down_back",
    )(place, *pieces, hat_two, scale_two, gain_two, active)


def up_kernel(
    place, grad_dropped, w_down, slope, normed_low, grad_lifted, sent, kept, grad_b_up, normed_t
):
    core = place[0]
    normed_t[...] = normed_low[...].T
    block = FF // PIECES
    for index, which in enumerate([1 - core, 3 - core, core, 2 + core]):
        columns = pl.ds(pl.multiple_of(which * block, block), block)
        grad = dot_right_t(grad_dropped[...], w_down[columns, :])
        grad = (grad * slope[:, columns].astype(f32)).astype(bf16)
        grad_lifted[:, columns] = grad
        grad_b_up[:, columns] = sums(grad.astype(f32))
        part = dot(normed_t[...], grad).astype(bf16)
        target = sent if index < 2 else kept
        for dp in range(8):
            for ab in range(2):
                target[index % 2, ab, dp] = part[dp * 96 : dp * 96 + 96, ab * 384 : ab * 384 + 384]


def up_back(place, grad_dropped, w_down, slope, normed_low):
    rows = grad_dropped.shape[0]
    return pl.pallas_call(
        up_kernel,
        out_shape=(
            shape((rows, FF), bf16),
            shape(TILES, bf16),
            shape(TILES, bf16),
            shape((1, FF), f32),
        ),
        in_specs=[SMEM] + [VMEM] * 4,
        out_specs=(VMEM,) * 4,
        scratch_shapes=[pltpu.VMEM((D, rows), bf16)],
        compiler_params=pltpu.CompilerParams(vmem_limit_bytes=60 * MIB),
        name="up_back",
    )(place, grad_dropped, w_down, slope, normed_low)


def middle_kernel(
    grad_z_two,
    grad_lifted,
    w_up,
    hat_one,
    scale_one,
    gain_one,
    w_out,
    context,
    grad_z_one,
    grad_branch,
    grad_attended,
    delta,
    vectors,
):
    rows = grad_z_two.shape[0]
    half = rows // 2
    totals = [jnp.zeros((1, D), f32)] * 3
    head = lax.broadcasted_iota(jnp.int32, (16, D), 0)
    feature = lax.broadcasted_iota(jnp.int32, (16, D), 1)
    heads = (feature // HEAD_SIZE == head).astype(bf16)
    for index in range(2):
        where = pl.ds(index * half, half)
        grad = grad_z_two[where, :] + dot_right_t(grad_lifted[where, :], w_up[...])
        hat = hat_one[where, :]
        grad_z = norm_back(grad, hat, scale_one[where, :], gain_one[...])
        low = grad_z.astype(bf16)
        grad_z_one[where, :] = grad_z
        grad_branch[where, :] = low
        terms = (grad * hat, grad, low.astype(f32))
        totals = [total + sums(term) for total, term in zip(totals, terms)]
        attended = dot_right_t(low, w_out[...])
        grad_attended[where, :] = attended.astype(bf16)
        products = attended * context[where, :].astype(f32)
        high = products.astype(bf16)
        rest = (products - high.astype(f32)).astype(bf16)
        delta[:, where] = dot_right_t(heads, high) + dot_right_t(heads, rest)
    for index in range(3):
        vectors[pl.ds(index, 1), :] = totals[index]


def middle_back(grad_z_two, grad_lifted, w_up, hat_one, scale_one, gain_one, w_out, context):
    rows = grad_z_two.shape[0]
    return pl.pallas_call(
        middle_kernel,
        out_shape=(
            shape((rows, D), f32),
            shape((rows, D), bf16),
            shape((rows, D), bf16),
            shape((16, rows), f32),
            shape((8, D), f32),
        ),
        in_specs=[VMEM] * 8,
        out_specs=(VMEM,) * 5,
        compiler_params=pltpu.CompilerParams(vmem_limit_bytes=60 * MIB),
        name="middle_back",
    )(grad_z_two, grad_lifted, w_up, hat_one, scale_one, gain_one, w_out, context)


def attention_kernel(
    first,
    pairs,
    queries,
    keyed,
    valued,
    key_bias,
    stats,
    grad_attended,
    delta,
    grad_q,
    grad_k,
    grad_v,
):
    rows = queries.shape[0]
    ones_lane = (lax.broadcasted_iota(jnp.int32, (rows, 128), 1) == 0).astype(bf16)

    def pair_step(index, carry):
        pair = first + index
        columns = pl.ds(pl.multiple_of(pair * 128, 128), 128)
        out_columns = pl.ds(pl.multiple_of(index * 128, 128), 128)
        query_pair = queries[:, columns]
        query_wide = jnp.concatenate([query_pair, ones_lane], axis=1)
        key_pair = keyed[:, columns]
        key_pair_t = key_pair.T
        value_pair = valued[:, columns]
        grad_pair = grad_attended[:, columns]
        found = []
        for which in range(2):
            mine = lane_half(rows, which)
            nothing = jnp.zeros_like(key_pair)
            key_head = jnp.concatenate([jnp.where(mine, key_pair, nothing), key_bias[...]], axis=1)
            scores = dot_right_t(key_head, query_wide)
            here = pl.ds(pair * 2 + which, 1)
            weights = jnp.exp2(scores - stats[here, :])
            grad_weights = dot_right_t(jnp.where(mine, value_pair, nothing), grad_pair)
            grad_raw = (weights * (grad_weights - delta[here, :])).astype(bf16)
            grad_v_pair = dot(weights.astype(bf16), grad_pair)
            grad_k_pair = dot(grad_raw, query_pair)
            head_rows = slice(which * HEAD_SIZE, which * HEAD_SIZE + HEAD_SIZE)
            grad_q_t = dot(key_pair_t[head_rows, :], grad_raw)
            found.append((grad_q_t, grad_k_pair, grad_v_pair))
        low = lane_half(rows, 0)
        grad_q_t = jnp.concatenate([found[0][0], found[1][0]], axis=0) * HEAD_SIZE ** (-0.5)
        grad_q[:, out_columns] = grad_q_t.T.astype(bf16)
        grad_k_pair = jnp.where(low, found[0][1], found[1][1]) * (1.0 / log_two_e)
        grad_k[:, out_columns] = grad_k_pair.astype(bf16)
        grad_v[:, out_columns] = jnp.where(low, found[0][2], found[1][2]).astype(bf16)
        return carry

    lax.fori_loop(0, pairs, pair_step, 0)


def attention_back(
    first, pairs, queries, keyed, valued, key_bias, stats, grad_attended, delta
):
    rows = queries.shape[0]
    result = shape((rows, pairs * 2 * HEAD_SIZE), bf16)

    def kernel(*refs):
        attention_kernel(first, pairs, *refs)

    return pl.pallas_call(
        kernel,
        out_shape=(result, result, result),
        in_specs=[VMEM] * 7,
        out_specs=(VMEM,) * 3,
        compiler_params=pltpu.CompilerParams(vmem_limit_bytes=60 * MIB),
        name="attention_back",
    )(queries, keyed, valued, key_bias, stats, grad_attended, delta)


def weights_kernel(parts, place, *refs):
    core = place[0]
    grads = [refs[index * parts : (index + 1) * parts] for index in range(3)]
    grad_branch, entries, context, sent, kept, vectors, wide_a, wide_b, wide_c, left_e, left_c = (
        refs[3 * parts :]
    )
    grad_q, grad_k, grad_v = (
        jnp.concatenate([part[...] for part in group], axis=1) for group in grads
    )
    vectors[0:1, :] = sums(grad_q.astype(f32))
    vectors[1:2, :] = sums(grad_v.astype(f32))
    left_e[...] = entries[...].T
    left_c[...] = context[...].T
    rows = entries.shape[0]
    block = D // PIECES
    branch = grad_branch[...]
    nothing = jnp.zeros((rows, block), bf16)
    for index in range(PIECES):
        low = index * block
        wide = slice(index * 2 * block, (index + 1) * 2 * block)
        wide_a[:, wide] = jnp.concatenate(
            [grad_q[:, low : low + block], grad_k[:, low : low + block]], axis=1
        )
        wide_b[:, wide] = jnp.concatenate([grad_v[:, low : low + block], nothing], axis=1)
        wide_c[:, wide] = jnp.concatenate([nothing, branch[:, low : low + block]], axis=1)
    for index, which in enumerate([1 - core, 3 - core, core, 2 + core]):
        columns = pl.ds(pl.multiple_of(which * 2 * block, 2 * block), 2 * block)
        target = sent if index < 2 else kept
        part_a = dot(left_e[...], wide_a[:, columns]).astype(bf16)
        part_b = dot(left_e[...], wide_b[:, columns]) + dot(left_c[...], wide_c[:, columns])
        part_b = part_b.astype(bf16)
        for dp in range(8):
            target[index % 2, 0, dp] = part_a[dp * 96 : dp * 96 + 96, :]
            target[index % 2, 1, dp] = part_b[dp * 96 : dp * 96 + 96, :]


def weights_back(place, grad_q, grad_k, grad_v, grad_branch, entries, context):
    rows = entries.shape[0]
    parts = len(grad_q)

    def kernel(*refs):
        weights_kernel(parts, *refs)

    return pl.pallas_call(
        kernel,
        out_shape=(shape(TILES, bf16), shape(TILES, bf16), shape((8, D), f32)),
        in_specs=[SMEM] + [VMEM] * (3 * parts + 3),
        out_specs=(VMEM,) * 3,
        scratch_shapes=[pltpu.VMEM((rows, 2 * D), bf16)] * 3 + [pltpu.VMEM((D, rows), bf16)] * 2,
        compiler_params=pltpu.CompilerParams(vmem_limit_bytes=60 * MIB),
        name="weights_back",
    )(place, *grad_q, *grad_k, *grad_v, grad_branch, entries, context)


def start_kernel(parts, *refs):
    grads = [refs[index * parts : (index + 1) * parts] for index in range(3)]
    w_query, w_key, w_value, grad_z_one, flags, piece0, piece1, piece2, piece3, vectors = refs[
        3 * parts :
    ]
    pieces = (piece0, piece1, piece2, piece3)
    seq = piece0.shape[0]
    totals = [jnp.zeros((1, D), f32)] * 2
    for step in range(2):
        where = pl.ds(step * 2 * seq, 2 * seq)
        grad = grad_z_one[where, :]
        for group, weight in zip(grads, (w_query, w_key, w_value)):
            value = jnp.concatenate([part[where, :] for part in group], axis=1)
            grad = grad + dot_right_t(value, weight[...])
        masked = flags[where, 1:2]
        replaced = flags[where, 2:3]
        terms = (grad * masked, grad * replaced)
        totals = [total + sums(term) for total, term in zip(totals, terms)]
        low = jnp.where(masked > 0, 0.0, grad).astype(bf16)
        pieces[2 * step][...] = low[:seq, :]
        pieces[2 * step + 1][...] = low[seq:, :]
    for index in range(2):
        vectors[pl.ds(index, 1), :] = totals[index]


def start_back(grad_q, grad_k, grad_v, w_query, w_key, w_value, grad_z_one, flags):
    rows = grad_z_one.shape[0]
    parts = len(grad_q)

    def kernel(*refs):
        start_kernel(parts, *refs)

    return pl.pallas_call(
        kernel,
        out_shape=(shape((rows // PIECES, D), bf16),) * PIECES + (shape((8, D), f32),),
        in_specs=[VMEM] * (3 * parts + 5),
        out_specs=(VMEM,) * 5,
        compiler_params=pltpu.CompilerParams(vmem_limit_bytes=60 * MIB),
        name="start_back",
    )(*grad_q, *grad_k, *grad_v, w_query, w_key, w_value, grad_z_one, flags)


def swap(value, axis, bit):
    size = lax.axis_size(axis)
    return lax.ppermute(value, axis, [(i, i ^ bit) for i in range(size)])


def pick(value, axis, index):
    return lax.dynamic_index_in_dim(value, index, axis, keepdims=False)


def total(terms):
    result = terms[0].astype(f32)
    for term in terms[1:]:
        result = result + term.astype(f32)
    return result


def reduce_tiles(sent, kept):
    blk = lax.axis_index("blk")
    fine = lax.axis_size("dp") // 8
    coarse = lax.axis_index("dp") // fine
    y = blk // 2
    bit0 = coarse % 2
    bit1 = (coarse // 2) % 2
    bit2 = coarse // 4
    split = (2, 2, 2, 2, 2) + TILES[3:]
    terms = [kept.reshape(split), swap(sent, "blk", 1).reshape(split)]
    terms_a = [t[:, 0] for t in terms]
    terms_b = [t[:, 1] for t in terms]
    send_a = total([pick(t, 3, 1 - bit0) for t in terms_a]).astype(bf16)
    send_b = total([pick(t, 0, 1 - y) for t in terms_b]).astype(bf16)
    got_a = swap(send_a, "dp", fine)
    got_b = swap(send_b, "blk", 2)
    terms_a = [pick(t, 3, bit0) for t in terms_a] + [got_a]
    terms_b = [pick(t, 0, y) for t in terms_b] + [got_b]
    send_a = total([pick(t, 0, 1 - y) for t in terms_a]).astype(bf16)
    send_b = total([pick(t, 2, 1 - bit0) for t in terms_b]).astype(bf16)
    got_a = swap(send_a, "blk", 2)
    got_b = swap(send_b, "dp", fine)
    terms_a = [pick(t, 0, y) for t in terms_a] + [got_a]
    terms_b = [pick(t, 2, bit0) for t in terms_b] + [got_b]
    send = jnp.stack(
        [total([pick(t, 1, 1 - bit1) for t in group]) for group in (terms_a, terms_b)]
    ).astype(bf16)
    got = swap(send, "dp", 2 * fine)
    terms_a = [pick(t, 1, bit1) for t in terms_a] + [got[0]]
    terms_b = [pick(t, 1, bit1) for t in terms_b] + [got[1]]
    send = jnp.stack(
        [total([pick(t, 0, 1 - bit2) for t in group]) for group in (terms_a, terms_b)]
    ).astype(bf16)
    got = swap(send, "dp", 4 * fine)
    part_a = total([pick(t, 0, bit2) for t in terms_a] + [got[0]])
    part_b = total([pick(t, 0, bit2) for t in terms_b] + [got[1]])
    return part_a, part_b


def finish(tile, axis):
    size = lax.axis_size("dp")
    fine = size // 8
    if fine == 1:
        return tile
    groups = [[index * fine + item for item in range(fine)] for index in range(8)]
    return lax.psum_scatter(
        tile, "dp", scatter_dimension=axis, axis_index_groups=groups, tiled=True
    )


def sum_vectors(value):
    for bit in (1, 2):
        value = value + swap(value, "blk", bit)
    bit = 1
    while bit < lax.axis_size("dp"):
        value = value + swap(value, "dp", bit)
        bit *= 2
    return value


def spread_documents(value):
    blk = lax.axis_index("blk")
    own = pick(value, 0, blk)
    return [own] + [swap(pick(value, 0, blk ^ step), "blk", step) for step in range(1, PIECES)]


def gather_documents(pieces):
    blk = lax.axis_index("blk")
    back = [pieces[0]] + [swap(pieces[step], "blk", step) for step in range(1, PIECES)]
    low = blk % 2 == 1
    high = blk // 2 == 1
    back = [jnp.where(low, back[index ^ 1], back[index]) for index in range(PIECES)]
    back = [jnp.where(high, back[index ^ 2], back[index]) for index in range(PIECES)]
    return jnp.stack(back)


def local(
    hidden_in,
    pad_mask,
    masked_flag,
    replaced_flag,
    mask_vector,
    replace_vector,
    w_query,
    b_query,
    w_key,
    w_value,
    b_value,
    w_out,
    b_out,
    gain_one,
    shift_one,
    w_up,
    b_up,
    w_down,
    b_down,
    gain_two,
    shift_two,
    out_grad,
):
    doc_count, seq_rows = pad_mask.shape
    row = lambda vector: vector.reshape(1, -1)
    place = (lax.axis_index("blk") % 2).astype(jnp.int32).reshape(1)
    flags = jnp.stack([pad_mask, masked_flag, replaced_flag], axis=1).astype(bf16)
    flags = jnp.pad(flags, ((0, 0), (0, 13), (0, D - seq_rows)))
    pieces = spread_documents(jnp.concatenate([hidden_in, flags], axis=1))
    grad_pieces = spread_documents(out_grad)
    (
        entries,
        queries,
        keyed,
        valued,
        context,
        key_bias,
        stats,
        hat_one,
        scale_one,
        normed_low,
        active,
        slope,
        hat_two,
        scale_two,
        hidden_out,
        columns,
    ) = forward(
        pieces,
        (
            row(mask_vector),
            row(replace_vector),
            w_query,
            row(b_query),
            w_key,
            w_value,
            row(b_value),
            w_out,
            row(b_out),
            row(gain_one),
            row(shift_one),
            w_up,
            row(b_up),
            w_down,
            row(b_down),
            row(gain_two),
            row(shift_two),
        ),
    )
    grad_z_two, grad_dropped, sent, kept, vectors_two = down_back(
        place, grad_pieces, hat_two, scale_two, row(gain_two), active
    )
    down_a, down_b = reduce_tiles(sent, kept)
    hidden_out = gather_documents(
        [hidden_out[index * seq_rows : (index + 1) * seq_rows] for index in range(PIECES)]
    )
    grad_lifted, sent, kept, grad_b_up = up_back(place, grad_dropped, w_down, slope, normed_low)
    up_a, up_b = reduce_tiles(sent, kept)
    grad_z_one, grad_branch, grad_attended, delta, vectors_one = middle_back(
        grad_z_two, grad_lifted, w_up, hat_one, scale_one, row(gain_one), w_out, context
    )
    early = sum_vectors(
        jnp.concatenate([vectors_two[:3], vectors_one[:3], grad_b_up.reshape(-1, D)], axis=0)
    )
    grads = [
        attention_back(
            first, 2, queries, keyed, valued, key_bias, stats, grad_attended, delta
        )
        for first in (0, 2, 4)
    ]
    grad_q, grad_k, grad_v = zip(*grads)
    sent, kept, vectors_qv = weights_back(
        place, grad_q, grad_k, grad_v, grad_branch, entries, context
    )
    pair_a, pair_b = reduce_tiles(sent, kept)
    *grad_in, vectors_start = start_back(
        grad_q, grad_k, grad_v, w_query, w_key, w_value, grad_z_one, columns
    )
    grad_in = gather_documents(grad_in)
    late = sum_vectors(jnp.concatenate([vectors_start[:2], vectors_qv[:2]], axis=0))
    block = D // PIECES
    grad_w_down = finish(jnp.concatenate([down_a, down_b], axis=0).T, 0)
    grad_w_up = finish(jnp.concatenate([up_a, up_b], axis=1), 0)
    pair_a = finish(pair_a, 0)
    pair_b = finish(pair_b, 0)
    return (
        hidden_out,
        grad_in,
        late[0],
        late[1],
        pair_a[:, :block],
        late[2],
        pair_a[:, block:],
        pair_b[:, :block],
        late[3],
        pair_b[:, block:],
        early[5],
        early[3],
        early[4],
        grad_w_up,
        early[6:].reshape(-1),
        grad_w_down,
        early[2],
        early[0],
        early[1],
    )


def solution(mesh):
    replicated = (P(),) * 17
    placed = (P("dp", "blk", None),) + (P("dp", "blk"),) * 3 + replicated
    placed = placed + (P("dp", "blk", None),)
    tiles = P("dp", "blk")
    rows = P("dp", "blk", None)
    return jax.shard_map(
        local,
        mesh=mesh,
        in_specs=placed,
        out_specs=(
            rows,
            rows,
            P(),
            P(),
            tiles,
            P(),
            tiles,
            tiles,
            P(),
            tiles,
            P(),
            P(),
            P(),
            tiles,
            P(),
            tiles,
            P(),
            P(),
            P(),
        ),
        check_vma=False,
    )
```

```python
import functools

import jax
import jax.numpy as jnp
import numpy as np
from jax import lax
from jax.experimental import pallas as pl
from jax.experimental.pallas import tpu as pltpu
from jax.sharding import PartitionSpec as P

D = 768
HEADS = 12
HEAD_SIZE = 64
FF = 3072
PIECES = 4
MIB = 1024 * 1024

epsilon = 1e-05
log_two_e = 1.4426950408889634
query_scale = HEAD_SIZE ** (-0.5) * log_two_e
left_out = -1e30

f32 = jnp.float32
bf16 = jnp.bfloat16

VMEM = pl.BlockSpec(memory_space=pltpu.VMEM)


def cost(micros):
    return pl.CostEstimate(flops=int(micros * 4e9), bytes_accessed=1024, transcendentals=0)


def shape(dims, dtype):
    return jax.ShapeDtypeStruct(dims, dtype)


def dot(left_side, right_side):
    return jnp.dot(left_side, right_side, preferred_element_type=f32)


def dot_right_t(left_side, right_side):
    return lax.dot_general(
        left_side, right_side, (((1,), (1,)), ((), ())), preferred_element_type=f32
    )


def lane_half(rows, which):
    lane = lax.broadcasted_iota(jnp.int32, (rows, 2 * HEAD_SIZE), 1)
    return (lane < HEAD_SIZE) if which == 0 else (lane >= HEAD_SIZE)


def normal_cdf(values):
    bell = jnp.exp2(values * values * (-0.5 * log_two_e))
    t = 1.0 / (1.0 + jnp.abs(values) * (0.3275911 * 0.7071067811865476))
    poly = 0.5 * 1.061405429 * t + 0.5 * -1.453152027
    poly = poly * t + 0.5 * 1.421413741
    poly = poly * t + 0.5 * -0.284496736
    poly = poly * t + 0.5 * 0.254829592
    tail = poly * t * bell
    return jnp.where(values >= 0, 1.0 - tail, tail), bell


def norm(values):
    centred = values - jnp.mean(values, axis=-1, keepdims=True)
    spread = jnp.mean(centred * centred, axis=-1, keepdims=True)
    scale = lax.rsqrt(spread + epsilon)
    return centred * scale, scale


def norm_back(grad, hat, scale, gain):
    lifted = grad * gain
    mean_one = jnp.mean(lifted, axis=-1, keepdims=True)
    mean_two = jnp.mean(lifted * hat, axis=-1, keepdims=True)
    return scale * (lifted - mean_one - hat * mean_two)


def room(items, more):
    total = more * MIB
    for item in items:
        *lead, rows, lanes = (1,) + tuple(item.shape)
        size = (rows + 15) // 16 * 16 * ((lanes + 127) // 128 * 128)
        total += int(np.prod(lead)) * size * jnp.dtype(item.dtype).itemsize
    return min(total, 62 * MIB)


def run(kernel, name, micros, ins, outs, scratch=(), more=10):
    return pl.pallas_call(
        kernel,
        out_shape=outs,
        in_specs=[VMEM] * len(ins),
        out_specs=(VMEM,) * len(outs),
        scratch_shapes=[pltpu.VMEM(item.shape, item.dtype) for item in scratch],
        compiler_params=pltpu.CompilerParams(vmem_limit_bytes=room(scratch, more)),
        cost_estimate=cost(micros),
        name=name,
    )(*ins)


def sums(values):
    return jnp.sum(values, axis=0, keepdims=True)


def place_bits():
    blk = lax.axis_index("blk")
    coarse = lax.axis_index("dp") // (lax.axis_size("dp") // 8)
    return blk % 2, blk // 2, coarse % 2, (coarse // 2) % 2, coarse // 4


def forward_kernel(*refs):
    vectors, refs = refs[:11], refs[11:]
    inside, refs = refs[:10], refs[10:]
    made, refs = refs[:19], refs[19:]
    start, value_t, context_t, dropped = refs
    *pieces, w_query, w_key, w_value, w_out, w_up, w_down = inside
    (
        entries,
        queries,
        keyed,
        valued,
        context,
        key_bias,
        stats,
        hat_one,
        scale_one,
        normed_low,
        active,
        slope,
        hat_two,
        scale_two,
        flags_out,
        *hidden_out,
    ) = made
    (
        mask_vector,
        replace_vector,
        b_query,
        b_value,
        b_out,
        gain_one,
        shift_one,
        b_down,
        gain_two,
        shift_two,
        b_up,
    ) = (vector[...].reshape(1, -1) for vector in vectors)
    seq = pieces[0].shape[0] - 16
    rows = PIECES * seq
    row_id = lax.broadcasted_iota(jnp.int32, (seq, seq), 0)
    col_id = lax.broadcasted_iota(jnp.int32, (seq, seq), 1)
    eye = (row_id == col_id).astype(bf16)
    for index, piece in enumerate(pieces):
        where = pl.ds(index * seq, seq)
        flags = piece[pl.ds(seq, 16), pl.ds(0, seq)]
        columns = dot_right_t(eye, flags)
        flags_out[where, :] = columns
        key_bias[where, :] = jnp.where(
            lax.broadcasted_iota(jnp.int32, (seq, 128), 1) == 0,
            (1.0 - columns[:, 0:1]) * left_out,
            0.0,
        ).astype(bf16)
        rows_here = jnp.where(
            columns[:, 1:2] > 0, mask_vector, piece[pl.ds(0, seq), :].astype(f32)
        )
        rows_here = rows_here + columns[:, 2:3] * replace_vector
        start[where, :] = rows_here
        entries[where, :] = rows_here.astype(bf16)
    queries[...] = ((dot(entries[...], w_query[...]) + b_query) * query_scale).astype(bf16)
    keyed[...] = dot(entries[...], w_key[...]).astype(bf16)
    valued[...] = (dot(entries[...], w_value[...]) + b_value).astype(bf16)
    value_t[...] = valued[...].T

    ones_lane = (lax.broadcasted_iota(jnp.int32, (rows, 128), 1) == 0).astype(bf16)
    ones_rows = jnp.ones((16, rows), bf16)

    def pair_step(pair, carry):
        columns = pl.ds(pl.multiple_of(pair * 128, 128), 128)
        query_pair = jnp.concatenate([queries[:, columns], ones_lane], axis=1)
        key_pair = keyed[:, columns]
        for which in range(2):
            key_head = jnp.where(lane_half(rows, which), key_pair, jnp.zeros_like(key_pair))
            key_head = jnp.concatenate([key_head, key_bias[...]], axis=1)
            scores = dot_right_t(key_head, query_pair)
            peak = jnp.max(scores, axis=0, keepdims=True)
            weights = jnp.exp2(scores - peak).astype(bf16)
            head_rows = pl.ds(pl.multiple_of(pair * 128 + which * HEAD_SIZE, HEAD_SIZE), HEAD_SIZE)
            values = jnp.concatenate([value_t[head_rows, :], ones_rows], axis=0)
            summed = dot(values, weights)
            total = summed[HEAD_SIZE : HEAD_SIZE + 1, :]
            context_t[head_rows, :] = (summed[:HEAD_SIZE, :] * (1.0 / total)).astype(bf16)
            stats[pl.ds(pair * 2 + which, 1), :] = peak + jnp.log2(total)
        return carry

    stats[pl.ds(8, 8), :] = jnp.zeros((8, rows), f32)
    lax.fori_loop(0, HEADS // 2, pair_step, 0)
    context[...] = context_t[...].T
    half = rows // 2
    for index in range(2):
        where = pl.ds(index * half, half)
        branch = dot(context[where, :], w_out[...]) + b_out
        hat, scale = norm(start[where, :] + branch)
        hat_one[where, :] = hat
        scale_one[where, :] = scale
        normed_low[where, :] = (hat * gain_one + shift_one).astype(bf16)
    chunk = 512
    for index in range(FF // chunk):
        columns = pl.ds(index * chunk, chunk)
        lifted = dot(normed_low[...], w_up[:, columns]) + b_up[:, index * chunk : (index + 1) * chunk]
        cdf, bell = normal_cdf(lifted)
        act = (lifted * cdf).astype(bf16)
        active[:, columns] = act
        slope[:, columns] = (cdf + lifted * bell * 0.3989422804014327).astype(bf16)
        part = dot(act, w_down[columns, :])
        if index == 0:
            dropped[...] = part
        else:
            dropped[...] += part
    for index in range(2):
        where = pl.ds(index * half, half)
        normed = hat_one[where, :] * gain_one + shift_one
        hat, scale = norm(normed + dropped[where, :] + b_down)
        hat_two[where, :] = hat
        scale_two[where, :] = scale
        low = (hat * gain_two + shift_two).astype(bf16)
        for item in (0, 1):
            hidden_out[2 * index + item][...] = low[item * seq : (item + 1) * seq, :]


def forward(pieces, vectors, *weights):
    rows = PIECES * (pieces[0].shape[0] - 16)
    ins = tuple(vectors) + tuple(pieces) + weights
    outs = (
        shape((rows, D), bf16),
        shape((rows, D), bf16),
        shape((rows, D), bf16),
        shape((rows, D), bf16),
        shape((rows, D), bf16),
        shape((rows, 128), bf16),
        shape((16, rows), f32),
        shape((rows, D), f32),
        shape((rows, 1), f32),
        shape((rows, D), bf16),
        shape((rows, FF), bf16),
        shape((rows, FF), bf16),
        shape((rows, D), f32),
        shape((rows, 1), f32),
        shape((rows, 16), f32),
    ) + (shape((rows // PIECES, D), bf16),) * PIECES
    more = (
        shape((rows, D), f32),
        shape((D, rows), bf16),
        shape((D, rows), bf16),
        shape((rows, D), f32),
    )
    return run(forward_kernel, "forward_layer", 22, ins, outs, more)


LANES = 384
ROWS_DOWN = 192
ROWS_UP = 240
ROWS_PAIR = 144


def tiles(rows):
    return shape((2, 8, rows, LANES), bf16)


def halves_t(values, target):
    rows = values.shape[0]
    turned = values.T
    for dp in range(8):
        for half in range(2):
            low = dp * 96 + half * 48
            target[dp * 48 : dp * 48 + 48, half * rows : (half + 1) * rows] = turned[
                low : low + 48, :
            ]


def halves_wide(values, target):
    rows = values.shape[0]
    block = D // PIECES
    nothing = jnp.zeros((rows, block), bf16)
    for index in range(PIECES):
        piece = values[:, index * block : (index + 1) * block]
        wide = slice(index * LANES, (index + 1) * LANES)
        target[0:rows, wide] = jnp.concatenate([piece, nothing], axis=1)
        target[rows : 2 * rows, wide] = jnp.concatenate([nothing, piece], axis=1)


def down_kernel(*refs):
    gain, refs = refs[0], refs[1:]
    inside, refs = refs[:7], refs[7:]
    made, (grad_t,) = refs[:5], refs[5:]
    *pieces, hat_two, scale_two, active = inside
    grad_z_two, grad_dropped, sent, kept, vectors = made
    gain_two = gain[...].reshape(1, D)
    seq = pieces[0].shape[0]
    core = place_bits()[0]
    totals = [jnp.zeros((1, D), f32)] * 3
    for index, piece in enumerate(pieces):
        where = pl.ds(index * seq, seq)
        grad = piece[...].astype(f32)
        hat = hat_two[where, :]
        grad_z = norm_back(grad, hat, scale_two[where, :], gain_two)
        low = grad_z.astype(bf16)
        grad_z_two[where, :] = grad_z
        grad_dropped[where, :] = low
        terms = (grad * hat, grad, low.astype(f32))
        totals = [total + sums(term) for total, term in zip(totals, terms)]
    vectors[...] = jnp.concatenate(totals + [jnp.zeros((5, D), f32)], axis=0)
    block = D // PIECES
    grad_t[...] = grad_dropped[...].T
    order = [1 - core, 3 - core, core, 2 + core]
    left_side = jnp.concatenate(
        [grad_t[pl.ds(pl.multiple_of(index * block, block), block), :] for index in order], axis=0
    )
    for pair in range(4):
        part = dot(left_side, active[:, pl.ds(pair * D, D)]).astype(bf16)
        for dp in range(2):
            columns = slice(dp * LANES, dp * LANES + LANES)
            for y in range(2):
                sent[y, pair * 2 + dp] = part[y * block : (y + 1) * block, columns]
                kept[y, pair * 2 + dp] = part[(y + 2) * block : (y + 3) * block, columns]


def down_back(pieces, hat_two, scale_two, active, gain_two):
    rows = PIECES * pieces[0].shape[0]
    ins = (gain_two,) + tuple(pieces) + (hat_two, scale_two, active)
    outs = (
        shape((rows, D), f32),
        shape((rows, D), bf16),
        tiles(ROWS_DOWN),
        tiles(ROWS_DOWN),
        shape((8, D), f32),
    )
    more = (shape((D, rows), bf16),)
    return run(down_kernel, "down_back", 7, ins, outs, more)


def lifted_kernel(grad_dropped, w_down, slope, grad_lifted, grad_b_up):
    block = FF // PIECES
    for index in range(PIECES):
        columns = pl.ds(index * block, block)
        grad = dot_right_t(grad_dropped[...], w_down[columns, :])
        grad = (grad * slope[:, columns].astype(f32)).astype(bf16)
        grad_lifted[:, columns] = grad
        grad_b_up[:, columns] = sums(grad.astype(f32))


def lifted_back(grad_dropped, w_down, slope):
    rows = grad_dropped.shape[0]
    ins = (grad_dropped, w_down, slope)
    outs = (shape((rows, FF), bf16), shape((1, FF), f32))
    return run(lifted_kernel, "lifted_back", 5, ins, outs)


def middle_kernel(gain, *refs):
    inside, refs = refs[:8], refs[8:]
    made, refs = refs[:7], refs[7:]
    normed_t, context_t, wide = refs
    grad_lifted, w_up, grad_z_two, hat_one, scale_one, w_out, context, normed_low = inside
    grad_z_one, grad_attended, delta, vectors, grad_branch, sent, kept = made
    core = place_bits()[0]
    rows = grad_z_two.shape[0]
    half = rows // 2
    gain_one = gain[...].reshape(1, D)
    totals = [jnp.zeros((1, D), f32)] * 3
    head = lax.broadcasted_iota(jnp.int32, (16, D), 0)
    feature = lax.broadcasted_iota(jnp.int32, (16, D), 1)
    heads = (feature // HEAD_SIZE == head).astype(bf16)
    for index in range(2):
        where = pl.ds(index * half, half)
        grad = dot_right_t(grad_lifted[where, :], w_up[...])
        grad = grad_z_two[where, :] + grad
        hat = hat_one[where, :]
        grad_z = norm_back(grad, hat, scale_one[where, :], gain_one)
        low = grad_z.astype(bf16)
        grad_z_one[where, :] = grad_z
        grad_branch[where, :] = low
        terms = (grad * hat, grad, low.astype(f32))
        totals = [total + sums(term) for total, term in zip(totals, terms)]
        attended = dot_right_t(low, w_out[...])
        grad_attended[where, :] = attended.astype(bf16)
        products = attended * context[where, :].astype(f32)
        high = products.astype(bf16)
        rest = (products - high.astype(f32)).astype(bf16)
        delta[:, where] = dot_right_t(heads, high) + dot_right_t(heads, rest)
    vectors[...] = jnp.concatenate(totals + [jnp.zeros((5, D), f32)], axis=0)
    normed_t[...] = normed_low[...].T
    halves_wide(grad_branch[...], wide)
    halves_t(context[...], context_t)
    block = FF // PIECES
    for index, which in enumerate([1 - core, 3 - core, core, 2 + core]):
        columns = pl.ds(pl.multiple_of(which * block, block), block)
        part = dot(normed_t[...], grad_lifted[:, columns]).astype(bf16)
        columns = pl.ds(pl.multiple_of(which * LANES, LANES), LANES)
        extra = dot(context_t[...], wide[:, columns]).astype(bf16)
        target = (sent, kept)[index // 2]
        y = index % 2
        for dp in range(8):
            target[y, dp, 0:96] = part[dp * 96 : dp * 96 + 96, 0:LANES]
            target[y, dp, 96:144] = extra[dp * 48 : dp * 48 + 48, :]
            target[y, dp, 144:240] = part[dp * 96 : dp * 96 + 96, LANES:]


def middle_back(
    grad_lifted, w_up, grad_z_two, hat_one, scale_one, w_out, context, normed_low, gain_one
):
    rows = grad_z_two.shape[0]
    ins = (gain_one, grad_lifted, w_up, grad_z_two, hat_one, scale_one, w_out, context, normed_low)
    whole = shape((rows, D), bf16)
    outs = (
        shape((rows, D), f32),
        whole,
        shape((16, rows), f32),
        shape((8, D), f32),
        whole,
        tiles(ROWS_UP),
        tiles(ROWS_UP),
    )
    more = (
        shape((D, rows), bf16),
        shape((D // 2, 2 * rows), bf16),
        shape((2 * rows, 2 * D), bf16),
    )
    return run(middle_kernel, "middle_up_back", 16, ins, outs, more)


def attention_steps(first, pairs, inside, grads):
    queries, keyed, valued, grad_attended, key_bias, stats, delta = inside
    grad_q, grad_k, grad_v = grads
    rows = queries.shape[0]
    ones_lane = (lax.broadcasted_iota(jnp.int32, (rows, 128), 1) == 0).astype(bf16)
    low = lane_half(rows, 0)
    for index in range(pairs):
        pair = first + index
        columns = pl.ds(pair * 128, 128)
        target = pl.ds(index * 128, 128)
        query_pair = queries[:, columns]
        query_wide = jnp.concatenate([query_pair, ones_lane], axis=1)
        key_pair = keyed[:, columns]
        key_pair_t = key_pair.T
        value_pair = valued[:, columns]
        grad_pair = grad_attended[:, columns]
        nothing = jnp.zeros_like(key_pair)
        found = []
        for which in range(2):
            own = lane_half(rows, which)
            key_head = jnp.concatenate([jnp.where(own, key_pair, nothing), key_bias[...]], axis=1)
            scores = dot_right_t(key_head, query_wide)
            here = pl.ds(pair * 2 + which, 1)
            weights = jnp.exp2(scores - stats[here, :])
            grad_weights = dot_right_t(jnp.where(own, value_pair, nothing), grad_pair)
            grad_raw = (weights * (grad_weights - delta[here, :])).astype(bf16)
            grad_v_pair = dot(weights.astype(bf16), grad_pair)
            grad_k_pair = dot(grad_raw, query_pair)
            head_rows = slice(which * HEAD_SIZE, which * HEAD_SIZE + HEAD_SIZE)
            grad_q_t = dot(key_pair_t[head_rows, :], grad_raw)
            found.append((grad_q_t, grad_k_pair, grad_v_pair))
        grad_q_t = jnp.concatenate([found[0][0], found[1][0]], axis=0) * HEAD_SIZE ** (-0.5)
        grad_q[:, target] = grad_q_t.T.astype(bf16)
        grad_k_pair = jnp.where(low, found[0][1], found[1][1]) * (1.0 / log_two_e)
        grad_k[:, target] = grad_k_pair.astype(bf16)
        grad_v[:, target] = jnp.where(low, found[0][2], found[1][2]).astype(bf16)


def attention_kernel(first, pairs, *refs):
    attention_steps(first, pairs, refs[:7], refs[7:])


def attention_back(first, pairs, *ins):
    rows = ins[0].shape[0]
    outs = (shape((rows, pairs * 128), bf16),) * 3
    kernel = functools.partial(attention_kernel, first, pairs)
    return run(kernel, "attention_back", 2.2 * pairs, ins, outs)


def weights_kernel(first, pairs, *refs):
    inside, (entries, *before), refs = refs[:7], refs[7:11], refs[11:]
    after, refs = refs[:3], refs[3:]
    sent, kept, vectors, entries_t, entries_half, wide_qk, wide_v = refs
    core = place_bits()[0]
    attention_steps(first, pairs, inside, after)
    turned = entries[...]
    entries_t[...] = turned.T
    halves_t(turned, entries_half)
    block = D // PIECES
    rows = entries.shape[0]
    nothing = jnp.zeros((rows, block), bf16)
    for index in range(PIECES):
        grad_q, grad_k, grad_v = (before, after)[index // 2]
        piece = slice(index % 2 * block, (index % 2 + 1) * block)
        wide = slice(index * LANES, (index + 1) * LANES)
        wide_qk[:, wide] = jnp.concatenate([grad_q[:, piece], grad_k[:, piece]], axis=1)
        wide_v[0:rows, wide] = jnp.concatenate([grad_v[:, piece], nothing], axis=1)
        wide_v[rows : 2 * rows, wide] = jnp.concatenate([nothing, grad_v[:, piece]], axis=1)
    for index, which in enumerate([1 - core, 3 - core, core, 2 + core]):
        columns = pl.ds(pl.multiple_of(which * LANES, LANES), LANES)
        part = dot(entries_t[...], wide_qk[:, columns]).astype(bf16)
        extra = dot(entries_half[...], wide_v[:, columns]).astype(bf16)
        target = (sent, kept)[index // 2]
        y = index % 2
        for dp in range(8):
            target[y, dp, 0:96] = part[dp * 96 : dp * 96 + 96, :]
            target[y, dp, 96:144] = extra[dp * 48 : dp * 48 + 48, :]
    half = D // 2
    for index, grads in enumerate((before, after)):
        columns = pl.ds(index * half, half)
        vectors[0:1, columns] = sums(grads[0][...].astype(f32))
        vectors[1:2, columns] = sums(grads[2][...].astype(f32))


def weights_back(first, pairs, *ins):
    rows = ins[0].shape[0]
    part = shape((rows, pairs * 128), bf16)
    outs = (part,) * 3 + (tiles(ROWS_PAIR),) * 2 + (shape((2, D), f32),)
    more = (
        shape((D, rows), bf16),
        shape((D // 2, 2 * rows), bf16),
        shape((rows, 2 * D), bf16),
        shape((2 * rows, 2 * D), bf16),
    )
    kernel = functools.partial(weights_kernel, first, pairs)
    return run(kernel, "attention_weights_back", 2.2 * pairs + 6, ins, outs, more)


def start_kernel(*refs):
    w_query, w_key, w_value, grad_z_one, flags, two, one, b_up, late = refs[:9]
    before, after, made = refs[9:12], refs[12:15], refs[15:]
    *grad_in, vectors = made
    seq = grad_z_one.shape[0] // PIECES
    half = D // 2
    totals = [jnp.zeros((1, D), f32)] * 2
    for step in range(2):
        where = pl.ds(step * 2 * seq, 2 * seq)
        grad = grad_z_one[where, :]
        for first, second, weight in zip(before, after, (w_query, w_key, w_value)):
            value = jnp.concatenate([first[where, :], second[where, :]], axis=1)
            grad = grad + dot_right_t(value, weight[...])
        masked = flags[where, 1:2]
        replaced = flags[where, 2:3]
        terms = (grad * masked, grad * replaced)
        totals = [total + sums(term) for total, term in zip(totals, terms)]
        low = jnp.where(masked > 0, 0.0, grad).astype(bf16)
        for item in (0, 1):
            grad_in[2 * step + item][...] = low[item * seq : (item + 1) * seq, :]
    rows = totals + [late[...], two[0:3, :], one[0:3, :]]
    rows += [b_up[:, index * D : (index + 1) * D] for index in range(FF // D)]
    rows = jnp.concatenate(rows + [jnp.zeros((2, D), f32)], axis=0)
    vectors[0:16, :] = rows[:, :half]
    vectors[16:32, :] = rows[:, half:]


def start_back(weights, grad_z_one, flags, vectors, grads):
    rows = grad_z_one.shape[0]
    ins = tuple(weights) + (grad_z_one, flags) + tuple(vectors) + tuple(grads)
    outs = (shape((rows // PIECES, D), bf16),) * PIECES + (shape((32, LANES), f32),)
    return run(start_kernel, "start_back", 5, ins, outs)


def swap(value, axis, bit):
    size = lax.axis_size(axis)
    return lax.ppermute(value, axis, [(i, i ^ bit) for i in range(size)])


def swap_turned(value, first):
    blks = lax.axis_size("blk")
    fine = lax.axis_size("dp") // 8
    pairs = []
    for dp in range(lax.axis_size("dp")):
        for blk in range(blks):
            along_dp = (blk % 2 == 0) == first
            other = (dp ^ fine) * blks + blk if along_dp else dp * blks + (blk ^ 2)
            pairs.append((dp * blks + blk, other))
    return lax.ppermute(value, ("dp", "blk"), pairs)


def tie(value, *others):
    return lax.optimization_barrier((value,) + tuple(others))[0]


def spread_kernel(hidden, *refs):
    flags, out = refs[:-PIECES], refs[-PIECES:]
    blk = lax.axis_index("blk")
    seq = hidden.shape[1]
    for step in range(PIECES):
        document = blk ^ step
        out[step][0:seq, :] = hidden[document]
        if flags:
            out[step][seq : seq + 16, :] = jnp.zeros((16, hidden.shape[2]), bf16)
        for index, flag in enumerate(flags):
            row = flag[pl.ds(document, 1), :].astype(bf16)
            out[step][seq + index : seq + index + 1, 0:seq] = row


def spread(hidden, flags=()):
    documents, seq, width = hidden.shape
    outs = (shape((seq + (16 if flags else 0), width), bf16),) * PIECES
    return run(spread_kernel, "spread_documents", 1, (hidden,) + tuple(flags), outs, (), 4)


def collect_kernel(*refs):
    blk = lax.axis_index("blk")
    for step in range(PIECES):
        refs[PIECES][blk ^ step] = refs[step][...]


def gather_documents(pieces, late):
    back = [swap(pieces[step], "blk", step) for step in range(1, PIECES)]
    ins = (pieces[0], *(tie(piece, *late) for piece in back))
    outs = (shape((PIECES,) + pieces[0].shape, bf16),)
    return run(collect_kernel, "collect_documents", 1, ins, outs, (), 4)[0]


def split_vectors(values):
    high = values.astype(bf16)
    return high, (values - high.astype(f32)).astype(bf16)


def sum_kernel(plan, emit, rows, counts, *refs):
    n_in, n_out, n_vectors = counts
    operands, made = refs[:n_in], refs[n_in:]
    tiles_out = plan(*place_bits())
    for place, terms in enumerate(tiles_out):
        value = None
        for operand, index, low in terms:
            source = operands[operand]
            if index is None:
                term = source[pl.ds(pl.multiple_of(low, 16), rows), :]
            else:
                term = source[index]
            value = term.astype(f32) if value is None else value + term.astype(f32)
        if emit is None:
            made[0][place * rows : (place + 1) * rows, :] = value.astype(bf16)
    if n_vectors:
        own, other = operands[n_in - 2], operands[n_in - 1]
        if other.dtype == f32:
            total = own[...] + other[...]
        else:
            start = other.shape[0] - 64
            high, low = other[start : start + 32, :], other[start + 32 : start + 64, :]
            total = own[...] + (high.astype(f32) + low.astype(f32))
        if emit is None:
            high, low = split_vectors(total)
            start = len(tiles_out) * rows
            made[0][start : start + 32, :] = high
            made[0][start + 32 : start + 64, :] = low
            made[1][...] = high.astype(f32) + low.astype(f32)
        else:
            made[n_out - 1][...] = total
    if emit is not None:
        emit(value, made)


def sum_stage(name, arrays, rows, plan, count, vectors=(), emit=None, outs=None):
    if outs is None:
        outs = (shape((count * rows + (64 if vectors else 0), LANES), bf16),)
    if vectors:
        outs = outs + (shape((32, LANES), f32),)
    ins = tuple(arrays) + tuple(vectors)
    kernel = functools.partial(sum_kernel, plan, emit, rows, (len(ins), len(outs), len(vectors)))
    return run(kernel, name, 1, ins, outs, (), 4)


def reduce_tiles(sent, kept, emit, outs, vectors=None):
    rows = kept.shape[2]
    fine = lax.axis_size("dp") // 8

    def base(y, b2, b1, b0):
        index = (y, b2 * 4 + b1 * 2 + b0)
        return [(0, index, 0), (1, index, 0)]

    late = yield (sent,)
    both = ()
    if vectors:
        own = late[0]
        both = (own, tie(swap(own, "blk", 1), *late))
    arrays = [kept, tie(swap(sent, "blk", 1), *late)]

    def core_plan(core, y, b0, b1, b2):
        return [
            base(
                core * (1 - y) + (1 - core) * u, i, j, core * u + (1 - core) * (1 - b0)
            )
            for u in (0, 1)
            for i in (0, 1)
            for j in (0, 1)
        ]

    send, *own = sum_stage("sum_core", arrays, rows, core_plan, 8, both)
    late = yield (send,)
    arrays.append(tie(swap_turned(send, True), *late))
    both = (own[0], arrays[-1]) if own else ()

    def first_plan(core, y, b0, b1, b2):
        u = core * (1 - b0) + (1 - core) * (1 - y)
        to_y = core * y + (1 - core) * (1 - y)
        to_x = core * (1 - b0) + (1 - core) * b0
        return [
            base(to_y, i, j, to_x) + [(2, None, (u * 4 + i * 2 + j) * rows)]
            for i in (0, 1)
            for j in (0, 1)
        ]

    send, *own = sum_stage("sum_first", arrays, rows, first_plan, 4, both)
    late = yield (send,)
    arrays.append(tie(swap_turned(send, False), *late))
    both = (own[0], arrays[-1]) if own else ()

    def line(core, y, b0, i, j):
        u = core * b0 + (1 - core) * y
        return base(y, i, j, b0) + [
            (2, None, (u * 4 + i * 2 + j) * rows),
            (3, None, (i * 2 + j) * rows),
        ]

    def second_plan(core, y, b0, b1, b2):
        return [line(core, y, b0, i, 1 - b1) for i in (0, 1)]

    send, *own = sum_stage("sum_second", arrays, rows, second_plan, 2, both)
    late = yield (send,)
    arrays.append(tie(swap(send, "dp", 2 * fine), *late))
    both = (own[0], arrays[-1]) if own else ()

    def third_plan(core, y, b0, b1, b2):
        return [line(core, y, b0, 1 - b2, b1) + [(4, None, (1 - b2) * rows)]]

    send, *own = sum_stage("sum_third", arrays, rows, third_plan, 1, both)
    late = yield (send,)
    arrays.append(tie(swap(send, "dp", 4 * fine), *late))
    both = (own[0], arrays[-1]) if own else ()

    def last_plan(core, y, b0, b1, b2):
        return [line(core, y, b0, b2, b1) + [(4, None, b2 * rows), (5, None, 0)]]

    yield sum_stage("sum_last", arrays, rows, last_plan, 1, both, emit, outs)


def emit_down(tile, made):
    made[0][...] = tile.T


def emit_up(tile, made):
    block = D // PIECES
    made[0][:, 0:LANES] = tile[0:96]
    made[0][:, LANES:] = tile[144:240]
    made[1][0:48, :] = tile[96:144, :block]
    made[1][48:96, :] = tile[96:144, block:]


def emit_pair(tile, made):
    block = D // PIECES
    made[0][...] = tile[0:96, :block]
    made[1][...] = tile[0:96, block:]
    made[2][0:48, :] = tile[96:144, :block]
    made[2][48:96, :] = tile[96:144, block:]


def finish(tile, axis):
    size = lax.axis_size("dp")
    fine = size // 8
    if fine == 1:
        return tile
    groups = [[index * fine + item for item in range(fine)] for index in range(8)]
    return lax.psum_scatter(
        tile, "dp", scatter_dimension=axis, axis_index_groups=groups, tiled=True
    )


def local(
    hidden_in,
    pad_mask,
    masked_flag,
    replaced_flag,
    mask_vector,
    replace_vector,
    w_query,
    b_query,
    w_key,
    w_value,
    b_value,
    w_out,
    b_out,
    gain_one,
    shift_one,
    w_up,
    b_up,
    w_down,
    b_down,
    gain_two,
    shift_two,
    out_grad,
):
    own, *others = spread(hidden_in, (pad_mask, masked_flag, replaced_flag))
    pieces = [own] + [swap(piece, "blk", step + 1) for step, piece in enumerate(others)]
    own, *others = spread(tie(out_grad, *others))
    grad_pieces = [own] + [swap(piece, "blk", step + 1) for step, piece in enumerate(others)]
    vectors = (
        mask_vector,
        replace_vector,
        b_query,
        b_value,
        b_out,
        gain_one,
        shift_one,
        b_down,
        gain_two,
        shift_two,
        b_up,
    )
    (
        entries,
        queries,
        keyed,
        valued,
        context,
        key_bias,
        stats,
        hat_one,
        scale_one,
        normed_low,
        active,
        slope,
        hat_two,
        scale_two,
        flags,
        *hidden_out,
    ) = forward(pieces, vectors, w_query, w_key, w_value, w_out, w_up, w_down)
    grad_z_two, grad_dropped, sent, kept, vectors_two = down_back(
        grad_pieces, hat_two, scale_two, active, gain_two
    )
    block = D // PIECES
    square = shape((D // 8, block), f32)
    down = reduce_tiles(sent, kept, emit_down, (shape((FF // 8, block), f32),))
    ties = next(down)
    grad_lifted, grad_b_up = lifted_back(tie(grad_dropped, *ties), w_down, slope)
    hidden_out = gather_documents(hidden_out, (grad_b_up,))
    ties = down.send((grad_b_up,))
    grad_z_one, grad_attended, delta, vectors_one, _, sent, kept = middle_back(
        grad_lifted,
        w_up,
        tie(grad_z_two, hidden_out, *ties),
        hat_one,
        scale_one,
        w_out,
        context,
        normed_low,
        gain_one,
    )
    up = reduce_tiles(sent, kept, emit_up, (shape((D // 8, D), f32), square))
    ties = next(up) + down.send((delta,))
    attention = (queries, keyed, valued, grad_attended, key_bias, stats)
    half = HEADS // 4
    grads = attention_back(0, half, *attention, tie(delta, *ties))
    done = (grads[0],)
    ties = up.send(done) + down.send(done)
    *more, sent, kept, vectors_qv = weights_back(
        half, half, *attention, tie(delta, *ties), entries, *grads
    )
    pair = reduce_tiles(sent, kept, emit_pair, (square,) * 3, True)
    done = (vectors_qv,)
    ties = next(pair) + up.send(done) + down.send(done)
    *grad_in, vectors = start_back(
        (w_query, w_key, w_value),
        tie(grad_z_one, *ties),
        flags,
        (vectors_two, vectors_one, grad_b_up, vectors_qv),
        tuple(grads) + tuple(more),
    )
    ties = pair.send((vectors,))
    ties = up.send(ties)
    (grad_w_down,) = down.send(ties)
    ties = pair.send((grad_w_down,))
    ties = up.send(ties)
    grad_in = gather_documents(grad_in, ties)
    ties = pair.send((grad_in,))
    grad_w_up, grad_w_out = up.send(ties)
    ties = pair.send((grad_w_up,))
    grad_w_query, grad_w_key, grad_w_value, vectors = pair.send(())
    vectors = jnp.concatenate([vectors[:16], vectors[16:]], axis=1)
    return (
        hidden_out,
        grad_in,
        vectors[0],
        vectors[1],
        finish(grad_w_query, 0),
        vectors[2],
        finish(grad_w_key, 0),
        finish(grad_w_value, 0),
        vectors[3],
        finish(grad_w_out, 0),
        vectors[9],
        vectors[7],
        vectors[8],
        finish(grad_w_up, 0),
        vectors[10:14].reshape(-1),
        finish(grad_w_down, 0),
        vectors[6],
        vectors[4],
        vectors[5],
    )


def solution(mesh):
    replicated = (P(),) * 17
    placed = (P("dp", "blk", None),) + (P("dp", "blk"),) * 3 + replicated
    placed = placed + (P("dp", "blk", None),)
    tiles = P("dp", "blk")
    rows = P("dp", "blk", None)
    return jax.shard_map(
        local,
        mesh=mesh,
        in_specs=placed,
        out_specs=(
            rows,
            rows,
            P(),
            P(),
            tiles,
            P(),
            tiles,
            tiles,
            P(),
            tiles,
            P(),
            P(),
            P(),
            tiles,
            P(),
            tiles,
            P(),
            P(),
            P(),
        ),
        check_vma=False,
    )
```

```python
import functools

import jax
import jax.numpy as jnp
import numpy as np
from jax import lax
from jax.experimental import pallas as pl
from jax.experimental.pallas import tpu as pltpu
from jax.sharding import PartitionSpec as P

D = 768
HEADS = 12
HEAD_SIZE = 64
FF = 3072
PIECES = 4
MIB = 1024 * 1024

epsilon = 1e-05
log_two_e = 1.4426950408889634
query_scale = HEAD_SIZE ** (-0.5) * log_two_e
left_out = -1e30

f32 = jnp.float32
bf16 = jnp.bfloat16

VMEM = pl.BlockSpec(memory_space=pltpu.VMEM)


def cost(micros):
    return pl.CostEstimate(flops=int(micros * 4e9), bytes_accessed=1024, transcendentals=0)


def shape(dims, dtype):
    return jax.ShapeDtypeStruct(dims, dtype)


def dot(left_side, right_side):
    return jnp.dot(left_side, right_side, preferred_element_type=f32)


def dot_right_t(left_side, right_side):
    return lax.dot_general(
        left_side, right_side, (((1,), (1,)), ((), ())), preferred_element_type=f32
    )


def lane_half(rows, which):
    lane = lax.broadcasted_iota(jnp.int32, (rows, 2 * HEAD_SIZE), 1)
    return (lane < HEAD_SIZE) if which == 0 else (lane >= HEAD_SIZE)


def normal_cdf(values):
    bell = jnp.exp2(values * values * (-0.5 * log_two_e))
    t = 1.0 / (1.0 + jnp.abs(values) * (0.3275911 * 0.7071067811865476))
    poly = 0.5 * 1.061405429 * t + 0.5 * -1.453152027
    poly = poly * t + 0.5 * 1.421413741
    poly = poly * t + 0.5 * -0.284496736
    poly = poly * t + 0.5 * 0.254829592
    tail = poly * t * bell
    return jnp.where(values >= 0, 1.0 - tail, tail), bell


def norm(values):
    centred = values - jnp.mean(values, axis=-1, keepdims=True)
    spread = jnp.mean(centred * centred, axis=-1, keepdims=True)
    scale = lax.rsqrt(spread + epsilon)
    return centred * scale, scale


def norm_back(grad, hat, scale, gain):
    lifted = grad * gain
    mean_one = jnp.mean(lifted, axis=-1, keepdims=True)
    mean_two = jnp.mean(lifted * hat, axis=-1, keepdims=True)
    return scale * (lifted - mean_one - hat * mean_two)


def room(items, more):
    total = more * MIB
    for item in items:
        *lead, rows, lanes = (1,) + tuple(item.shape)
        size = (rows + 15) // 16 * 16 * ((lanes + 127) // 128 * 128)
        total += int(np.prod(lead)) * size * jnp.dtype(item.dtype).itemsize
    return min(total, 62 * MIB)


def run(kernel, name, micros, ins, outs, scratch=(), more=10):
    return pl.pallas_call(
        kernel,
        out_shape=outs,
        in_specs=[VMEM] * len(ins),
        out_specs=(VMEM,) * len(outs),
        scratch_shapes=[pltpu.VMEM(item.shape, item.dtype) for item in scratch],
        compiler_params=pltpu.CompilerParams(vmem_limit_bytes=room(scratch, more)),
        cost_estimate=cost(micros),
        name=name,
    )(*ins)


def back_shapes(rows):
    seq = rows // PIECES
    return (shape((seq, D), bf16),) * 2 + (shape((2, seq, D), bf16),)


def put_pieces(values, targets):
    seq = values.shape[0] // 2
    for item in (0, 1):
        target = targets[item] if len(targets) == 2 else targets[0].at[item]
        target[...] = values[item * seq : (item + 1) * seq, :]


def sums(values):
    return jnp.sum(values, axis=0, keepdims=True)


def place_bits():
    blk = lax.axis_index("blk")
    coarse = lax.axis_index("dp") // (lax.axis_size("dp") // 8)
    return blk % 2, blk // 2, coarse % 2, (coarse // 2) % 2, coarse // 4


def unpack_flags(codes):
    replaced = (codes >= 4).astype(f32)
    codes = codes - 4 * replaced
    masked = (codes >= 2).astype(f32)
    pad = codes - 2 * masked
    lane = lax.broadcasted_iota(jnp.int32, (codes.shape[0], 16), 1)
    return jnp.where(lane == 0, pad, jnp.where(lane == 1, masked, replaced))


def forward_kernel(*refs):
    vectors, refs = refs[:11], refs[11:]
    pieces, refs = refs[:PIECES], refs[PIECES:]
    w_query, w_key, w_value, w_out, w_up, w_down, *refs = refs
    made, refs = refs[:18], refs[18:]
    start, value_t, context_t, dropped = refs
    (
        entries,
        queries,
        keyed,
        valued,
        context,
        key_bias,
        stats,
        hat_one,
        scale_one,
        normed_low,
        active,
        slope,
        hat_two,
        scale_two,
        flags_out,
        *hidden_out,
    ) = made
    (
        mask_vector,
        replace_vector,
        b_query,
        b_value,
        b_out,
        gain_one,
        shift_one,
        b_down,
        gain_two,
        shift_two,
        b_up,
    ) = (vector[...].reshape(1, -1) for vector in vectors)
    seq = pieces[0].shape[0] - 16
    rows = PIECES * seq
    row_id = lax.broadcasted_iota(jnp.int32, (seq, seq), 0)
    col_id = lax.broadcasted_iota(jnp.int32, (seq, seq), 1)
    eye = (row_id == col_id).astype(bf16)
    for index, piece in enumerate(pieces):
        where = pl.ds(index * seq, seq)
        columns = dot_right_t(eye, piece[seq : seq + 16, 0:seq])
        columns = unpack_flags(columns[:, 0:1])
        flags_out[where, :] = columns
        key_bias[where, :] = jnp.where(
            lax.broadcasted_iota(jnp.int32, (seq, 128), 1) == 0,
            (1.0 - columns[:, 0:1]) * left_out,
            0.0,
        ).astype(bf16)
        rows_here = jnp.where(
            columns[:, 1:2] > 0, mask_vector, piece[0:seq, :].astype(f32)
        )
        rows_here = rows_here + columns[:, 2:3] * replace_vector
        start[where, :] = rows_here
        entries[where, :] = rows_here.astype(bf16)
    queries[...] = ((dot(entries[...], w_query[...]) + b_query) * query_scale).astype(bf16)
    keyed[...] = dot(entries[...], w_key[...]).astype(bf16)
    valued[...] = (dot(entries[...], w_value[...]) + b_value).astype(bf16)
    value_t[...] = valued[...].T

    ones_lane = (lax.broadcasted_iota(jnp.int32, (rows, 128), 1) == 0).astype(bf16)
    ones_rows = jnp.ones((16, rows), bf16)

    def head_scores(head):
        columns = pl.ds(head // 2 * 128, 128)
        query_pair = jnp.concatenate([queries[:, columns], ones_lane], axis=1)
        key_pair = keyed[:, columns]
        key_head = jnp.where(lane_half(rows, head % 2), key_pair, jnp.zeros_like(key_pair))
        key_head = jnp.concatenate([key_head, key_bias[...]], axis=1)
        return dot_right_t(key_head, query_pair)

    stats[pl.ds(8, 8), :] = jnp.zeros((8, rows), f32)
    following = head_scores(0)
    for head in range(HEADS):
        scores = following
        if head + 1 < HEADS:
            following = head_scores(head + 1)
        peak = jnp.max(scores, axis=0, keepdims=True)
        weights = jnp.exp2(scores - peak).astype(bf16)
        head_rows = pl.ds(head * HEAD_SIZE, HEAD_SIZE)
        values = jnp.concatenate([value_t[head_rows, :], ones_rows], axis=0)
        summed = dot(values, weights)
        total = summed[HEAD_SIZE : HEAD_SIZE + 1, :]
        context_t[head_rows, :] = (summed[:HEAD_SIZE, :] * (1.0 / total)).astype(bf16)
        stats[pl.ds(head, 1), :] = peak + jnp.log2(total)
    context[...] = context_t[...].T
    half = rows // 2
    for index in range(2):
        where = pl.ds(index * half, half)
        branch = dot(context[where, :], w_out[...]) + b_out
        hat, scale = norm(start[where, :] + branch)
        hat_one[where, :] = hat
        scale_one[where, :] = scale
        normed_low[where, :] = (hat * gain_one + shift_one).astype(bf16)
    chunk = 256
    count = FF // chunk

    def lift(index):
        columns = slice(index * chunk, (index + 1) * chunk)
        return dot(normed_low[...], w_up[:, columns]) + b_up[:, columns]

    following = lift(0)
    for index in range(count):
        lifted = following
        if index + 1 < count:
            following = lift(index + 1)
        columns = pl.ds(index * chunk, chunk)
        cdf, bell = normal_cdf(lifted)
        act = (lifted * cdf).astype(bf16)
        active[:, columns] = act
        slope[:, columns] = (cdf + lifted * bell * 0.3989422804014327).astype(bf16)
        part = dot(act, w_down[columns, :])
        if index == 0:
            dropped[...] = part
        else:
            dropped[...] += part
    for index in range(2):
        where = pl.ds(index * half, half)
        normed = hat_one[where, :] * gain_one + shift_one
        hat, scale = norm(normed + dropped[where, :] + b_down)
        hat_two[where, :] = hat
        scale_two[where, :] = scale
        low = (hat * gain_two + shift_two).astype(bf16)
        put_pieces(low, hidden_out[index * 2 : index * 2 + 2])


def forward(pieces, vectors, *weights):
    rows = PIECES * (pieces[0].shape[0] - 16)
    ins = tuple(vectors) + tuple(pieces) + weights
    outs = (
        shape((rows, D), bf16),
        shape((rows, D), bf16),
        shape((rows, D), bf16),
        shape((rows, D), bf16),
        shape((rows, D), bf16),
        shape((rows, 128), bf16),
        shape((16, rows), f32),
        shape((rows, D), f32),
        shape((rows, 1), f32),
        shape((rows, D), bf16),
        shape((rows, FF), bf16),
        shape((rows, FF), bf16),
        shape((rows, D), f32),
        shape((rows, 1), f32),
        shape((rows, 16), f32),
    ) + back_shapes(rows)
    more = (
        shape((rows, D), f32),
        shape((D, rows), bf16),
        shape((D, rows), bf16),
        shape((rows, D), f32),
    )
    return run(forward_kernel, "forward_layer", 22, ins, outs, more)


LANES = 384
ROWS_DOWN = 192
ROWS_UP = 240
ROWS_PAIR = 144


PARTS_DOWN = (192,)
PARTS_UP = (240,)
PARTS_PAIR = (80, 64)


def tiles(parts):
    return tuple(shape((2, 8, rows, LANES), bf16) for rows in parts)


def put(parts, y, dp, first, value):
    low = 0
    for part in parts:
        high = low + part.shape[2]
        start, stop = max(first, low), min(first + value.shape[0], high)
        if start < stop:
            part[y, dp, start - low : stop - low] = value[start - first : stop - first]
        low = high


def halves_t(values, target):
    rows = values.shape[0]
    turned = values.T
    for dp in range(8):
        for half in range(2):
            low = dp * 96 + half * 48
            target[dp * 48 : dp * 48 + 48, half * rows : (half + 1) * rows] = turned[
                low : low + 48, :
            ]


def halves_wide(values, target):
    rows = values.shape[0]
    block = D // PIECES
    nothing = jnp.zeros((rows, block), bf16)
    for index in range(PIECES):
        piece = values[:, index * block : (index + 1) * block]
        wide = slice(index * LANES, (index + 1) * LANES)
        target[0:rows, wide] = jnp.concatenate([piece, nothing], axis=1)
        target[rows : 2 * rows, wide] = jnp.concatenate([nothing, piece], axis=1)


def down_kernel(*refs):
    gain, refs = refs[0], refs[1:]
    pieces, (hat_two, scale_two, active, *refs) = refs[:PIECES], refs[PIECES:]
    count = len(PARTS_DOWN)
    grad_z_two, grad_dropped, vectors, kept, *refs = refs
    sent, (grad_t,) = refs[:count], refs[count:]
    gain_two = gain[...].reshape(1, D)
    seq = pieces[0].shape[0]
    core = place_bits()[0]
    totals = [jnp.zeros((1, D), f32)] * 3
    for index, piece in enumerate(pieces):
        where = pl.ds(index * seq, seq)
        grad = piece[...].astype(f32)
        hat = hat_two[where, :]
        grad_z = norm_back(grad, hat, scale_two[where, :], gain_two)
        low = grad_z.astype(bf16)
        grad_z_two[where, :] = grad_z
        grad_dropped[where, :] = low
        terms = (grad * hat, grad, low.astype(f32))
        totals = [total + sums(term) for total, term in zip(totals, terms)]
    vectors[...] = jnp.concatenate(totals + [jnp.zeros((5, D), f32)], axis=0)
    block = D // PIECES
    grad_t[...] = grad_dropped[...].T
    order = [1 - core, 3 - core, core, 2 + core]
    left_side = jnp.concatenate(
        [grad_t[pl.ds(pl.multiple_of(index * block, block), block), :] for index in order], axis=0
    )
    for pair in range(4):
        part = dot(left_side, active[:, pl.ds(pair * D, D)]).astype(bf16)
        for dp in range(2):
            columns = slice(dp * LANES, dp * LANES + LANES)
            for y in range(2):
                put(sent, y, pair * 2 + dp, 0, part[y * block : (y + 1) * block, columns])
                kept[y, pair * 2 + dp] = part[(y + 2) * block : (y + 3) * block, columns]


def down_back(pieces, hat_two, scale_two, active, gain_two):
    rows = PIECES * pieces[0].shape[0]
    ins = (gain_two,) + tuple(pieces) + (hat_two, scale_two, active)
    outs = (
        shape((rows, D), f32),
        shape((rows, D), bf16),
        shape((8, D), f32),
        *tiles((ROWS_DOWN,)),
        *tiles(PARTS_DOWN),
    )
    more = (shape((D, rows), bf16),)
    return run(down_kernel, "down_back", 7, ins, outs, more)


def lifted_kernel(grad_dropped, w_down, slope, grad_lifted, grad_b_up):
    block = FF // PIECES
    for index in range(PIECES):
        columns = pl.ds(index * block, block)
        grad = dot_right_t(grad_dropped[...], w_down[columns, :])
        grad = (grad * slope[:, columns].astype(f32)).astype(bf16)
        grad_lifted[:, columns] = grad
        grad_b_up[:, columns] = sums(grad.astype(f32))


def lifted_back(grad_dropped, w_down, slope):
    rows = grad_dropped.shape[0]
    ins = (grad_dropped, w_down, slope)
    outs = (shape((rows, FF), bf16), shape((1, FF), f32))
    return run(lifted_kernel, "lifted_back", 5, ins, outs)


def middle_kernel(pairs, gain, *refs):
    inside, attention, refs = refs[:8], refs[8:13], refs[13:]
    grad_z_one, grad_attended, delta, vectors, grad_branch, kept, *refs = refs
    sent, refs = refs[: len(PARTS_UP)], refs[len(PARTS_UP) :]
    grads, (normed_t, context_t, wide) = refs[:3], refs[3:]
    grad_lifted, w_up, grad_z_two, hat_one, scale_one, w_out, context, normed_low = inside
    core = place_bits()[0]
    rows = grad_z_two.shape[0]
    half = rows // 2
    gain_one = gain[...].reshape(1, D)
    totals = [jnp.zeros((1, D), f32)] * 3
    head = lax.broadcasted_iota(jnp.int32, (16, D), 0)
    feature = lax.broadcasted_iota(jnp.int32, (16, D), 1)
    heads = (feature // HEAD_SIZE == head).astype(bf16)
    for index in range(2):
        where = pl.ds(index * half, half)
        grad = dot_right_t(grad_lifted[where, :], w_up[...])
        grad = grad_z_two[where, :] + grad
        hat = hat_one[where, :]
        grad_z = norm_back(grad, hat, scale_one[where, :], gain_one)
        low = grad_z.astype(bf16)
        grad_z_one[where, :] = grad_z
        grad_branch[where, :] = low
        terms = (grad * hat, grad, low.astype(f32))
        totals = [total + sums(term) for total, term in zip(totals, terms)]
        attended = dot_right_t(low, w_out[...])
        grad_attended[where, :] = attended.astype(bf16)
        products = attended * context[where, :].astype(f32)
        high = products.astype(bf16)
        rest = (products - high.astype(f32)).astype(bf16)
        delta[:, where] = dot_right_t(heads, high) + dot_right_t(heads, rest)
    vectors[...] = jnp.concatenate(totals + [jnp.zeros((5, D), f32)], axis=0)
    normed_t[...] = normed_low[...].T
    halves_wide(grad_branch[...], wide)
    halves_t(context[...], context_t)
    block = FF // PIECES
    for index, which in enumerate([1 - core, 3 - core, core, 2 + core]):
        columns = pl.ds(pl.multiple_of(which * block, block), block)
        part = dot(normed_t[...], grad_lifted[:, columns]).astype(bf16)
        columns = pl.ds(pl.multiple_of(which * LANES, LANES), LANES)
        extra = dot(context_t[...], wide[:, columns]).astype(bf16)
        target = (sent, (kept,))[index // 2]
        y = index % 2
        for dp in range(8):
            put(target, y, dp, 0, part[dp * 96 : dp * 96 + 96, 0:LANES])
            put(target, y, dp, 96, extra[dp * 48 : dp * 48 + 48, :])
            put(target, y, dp, 144, part[dp * 96 : dp * 96 + 96, LANES:])
    attention_steps(0, pairs, (*attention, grad_attended, delta), grads)


def middle_back(pairs, *ins):
    rows = ins[1].shape[0]
    whole = shape((rows, D), bf16)
    outs = (
        shape((rows, D), f32),
        whole,
        shape((16, rows), f32),
        shape((8, D), f32),
        whole,
        *tiles((ROWS_UP,)),
        *tiles(PARTS_UP),
        *(shape((rows, pairs * 128), bf16),) * 3,
    )
    more = (
        shape((D, rows), bf16),
        shape((D // 2, 2 * rows), bf16),
        shape((2 * rows, 2 * D), bf16),
    )
    kernel = functools.partial(middle_kernel, pairs)
    return run(kernel, "middle_up_back", 12, ins, outs, more)


def attention_steps(first, pairs, inside, grads, base=0):
    queries, keyed, valued, key_bias, stats, grad_attended, delta = inside
    grad_q, grad_k, grad_v = grads
    rows = queries.shape[0]
    ones_lane = (lax.broadcasted_iota(jnp.int32, (rows, 128), 1) == 0).astype(bf16)
    low = lane_half(rows, 0)
    nothing = jnp.zeros((rows, 128), bf16)

    def products(head):
        pair, which = head // 2, head % 2
        columns = pl.ds(pair * 128, 128)
        own = lane_half(rows, which)
        query_wide = jnp.concatenate([queries[:, columns], ones_lane], axis=1)
        key_head = jnp.where(own, keyed[:, columns], nothing)
        key_head = jnp.concatenate([key_head, key_bias[...]], axis=1)
        value_head = jnp.where(own, valued[:, columns], nothing)
        return (
            dot_right_t(key_head, query_wide),
            dot_right_t(value_head, grad_attended[:, columns]),
        )

    following = products(2 * first)
    for index in range(pairs):
        pair = first + index
        columns = pl.ds(pair * 128, 128)
        target = pl.ds(base + index * 128, 128)
        query_pair = queries[:, columns]
        key_pair_t = keyed[:, columns].T
        grad_pair = grad_attended[:, columns]
        found = []
        for which in range(2):
            head = 2 * pair + which
            scores, grad_weights = following
            if head + 1 < 2 * (first + pairs):
                following = products(head + 1)
            here = pl.ds(head, 1)
            weights = jnp.exp2(scores - stats[here, :])
            grad_raw = (weights * (grad_weights - delta[here, :])).astype(bf16)
            grad_v_pair = dot(weights.astype(bf16), grad_pair)
            grad_k_pair = dot(grad_raw, query_pair)
            head_rows = slice(which * HEAD_SIZE, which * HEAD_SIZE + HEAD_SIZE)
            grad_q_t = dot(key_pair_t[head_rows, :], grad_raw)
            found.append((grad_q_t, grad_k_pair, grad_v_pair))
        grad_q_t = jnp.concatenate([found[0][0], found[1][0]], axis=0) * HEAD_SIZE ** (-0.5)
        grad_q[:, target] = grad_q_t.T.astype(bf16)
        grad_k_pair = jnp.where(low, found[0][1], found[1][1]) * (1.0 / log_two_e)
        grad_k[:, target] = grad_k_pair.astype(bf16)
        grad_v[:, target] = jnp.where(low, found[0][2], found[1][2]).astype(bf16)


def attention_kernel(first, pairs, *refs):
    attention_steps(first, pairs, refs[:7], refs[7:])


def attention_back(first, pairs, *ins):
    rows = ins[0].shape[0]
    outs = (shape((rows, pairs * 128), bf16),) * 3
    kernel = functools.partial(attention_kernel, first, pairs)
    return run(kernel, "attention_back", 2.2 * pairs, ins, outs)


def weights_kernel(first, pairs, *refs):
    inside, (entries, *before), refs = refs[:7], refs[7:14], refs[14:]
    merged, (vectors, kept, *refs) = refs[:3], refs[3:]
    sent, refs = refs[: len(PARTS_PAIR)], refs[len(PARTS_PAIR) :]
    entries_t, entries_half, wide_qk, wide_v = refs
    core = place_bits()[0]
    low = 0
    for group in (before[:3], before[3:]):
        width = group[0].shape[1]
        for part, target in zip(group, merged):
            target[:, low : low + width] = part[...]
        low += width
    attention_steps(first, pairs, inside, merged, low)
    turned = entries[...]
    entries_t[...] = turned.T
    halves_t(turned, entries_half)
    block = D // PIECES
    grad_q, grad_k, grad_v = merged
    for index in range(PIECES):
        piece = slice(index * block, (index + 1) * block)
        wide = slice(index * LANES, (index + 1) * LANES)
        wide_qk[:, wide] = jnp.concatenate([grad_q[:, piece], grad_k[:, piece]], axis=1)
    halves_wide(grad_v[...], wide_v)
    for index, which in enumerate([1 - core, 3 - core, core, 2 + core]):
        columns = pl.ds(pl.multiple_of(which * LANES, LANES), LANES)
        part = dot(entries_t[...], wide_qk[:, columns]).astype(bf16)
        extra = dot(entries_half[...], wide_v[:, columns]).astype(bf16)
        target = (sent, (kept,))[index // 2]
        y = index % 2
        for dp in range(8):
            put(target, y, dp, 0, part[dp * 96 : dp * 96 + 96, :])
            put(target, y, dp, 96, extra[dp * 48 : dp * 48 + 48, :])
    vectors[0:1, :] = sums(grad_q[...].astype(f32))
    vectors[1:2, :] = sums(grad_v[...].astype(f32))


def weights_back(first, pairs, *ins):
    rows = ins[0].shape[0]
    whole = shape((rows, D), bf16)
    outs = (whole,) * 3 + (shape((2, D), f32), *tiles((ROWS_PAIR,)), *tiles(PARTS_PAIR))
    more = (
        shape((D, rows), bf16),
        shape((D // 2, 2 * rows), bf16),
        shape((rows, 2 * D), bf16),
        shape((2 * rows, 2 * D), bf16),
    )
    kernel = functools.partial(weights_kernel, first, pairs)
    return run(kernel, "attention_weights_back", 2.2 * pairs + 4, ins, outs, more)


def start_kernel(*refs):
    w_query, w_key, w_value, grad_z_one, flags, two, one, b_up, late = refs[:9]
    grads, made = refs[9:12], refs[12:]
    *grad_in, vectors = made
    seq = grad_z_one.shape[0] // PIECES
    half = D // 2
    totals = [jnp.zeros((1, D), f32)] * 2
    for step in range(2):
        where = pl.ds(step * 2 * seq, 2 * seq)
        grad = grad_z_one[where, :]
        for value, weight in zip(grads, (w_query, w_key, w_value)):
            grad = grad + dot_right_t(value[where, :], weight[...])
        masked = flags[where, 1:2]
        replaced = flags[where, 2:3]
        terms = (grad * masked, grad * replaced)
        totals = [total + sums(term) for total, term in zip(totals, terms)]
        low = jnp.where(masked > 0, 0.0, grad).astype(bf16)
        put_pieces(low, grad_in[step * 2 : step * 2 + 2])
    rows = totals + [late[...], two[0:3, :], one[0:3, :]]
    rows += [b_up[:, index * D : (index + 1) * D] for index in range(FF // D)]
    rows = jnp.concatenate(rows + [jnp.zeros((2, D), f32)], axis=0)
    vectors[0:16, :] = rows[:, :half]
    vectors[16:32, :] = rows[:, half:]


def start_back(weights, grad_z_one, flags, vectors, grads):
    rows = grad_z_one.shape[0]
    ins = tuple(weights) + (grad_z_one, flags) + tuple(vectors) + tuple(grads)
    outs = back_shapes(rows) + (shape((32, LANES), f32),)
    return run(start_kernel, "start_back", 0, ins, outs)


def swap(value, axis, bit):
    size = lax.axis_size(axis)
    return lax.ppermute(value, axis, [(i, i ^ bit) for i in range(size)])


def swap_turned(value, first):
    blks = lax.axis_size("blk")
    fine = lax.axis_size("dp") // 8
    pairs = []
    for dp in range(lax.axis_size("dp")):
        for blk in range(blks):
            along_dp = (blk % 2 == 0) == first
            other = (dp ^ fine) * blks + blk if along_dp else dp * blks + (blk ^ 2)
            pairs.append((dp * blks + blk, other))
    return lax.ppermute(value, ("dp", "blk"), pairs)


def tie(value, *others):
    return lax.optimization_barrier((value,) + tuple(others))[0]


def spread_kernel(hidden, flags, *out):
    blk = lax.axis_index("blk")
    seq = hidden.shape[1]
    for step in range(PIECES):
        document = blk ^ step
        out[step][0:seq, :] = hidden[document]
        row = flags[pl.ds(document, 1), :]
        out[step][seq : seq + 16, 0:seq] = jnp.concatenate(
            [row, jnp.zeros((15, seq), f32)], axis=0
        ).astype(bf16)
        out[step][seq : seq + 16, seq:] = jnp.zeros((16, hidden.shape[2] - seq), bf16)


def spread(hidden, flags):
    documents, seq, width = hidden.shape
    outs = (shape((seq + 16, width), bf16),) * PIECES
    return run(spread_kernel, "spread_documents", 1, (hidden, flags), outs, (), 2)


def spread_plain_kernel(hidden, *out):
    blk = lax.axis_index("blk")
    for step in range(PIECES):
        out[step][...] = hidden[blk ^ step]


def spread_plain(hidden):
    outs = (shape(hidden.shape[1:], bf16),) * PIECES
    return run(spread_plain_kernel, "spread_grads", 1, (hidden,), outs, (), 2)


def move_pieces(pieces):
    own, *others = pieces
    return [own] + [swap(piece, "blk", step + 1) for step, piece in enumerate(others)]


def collect_kernel(own, near, far, both, out):
    blk = lax.axis_index("blk")
    out[blk] = own[...]
    out[blk ^ 1] = near[...]
    out[blk ^ 2] = far[0]
    out[blk ^ 3] = both[1]


def gather_documents(own, near, far):
    late = yield
    near = swap(near, "blk", 1)
    far = tie(swap(far, "blk", 2), *late)
    late = yield (far,)
    both = tie(swap(far, "blk", 1), *late)
    ins = (own, near, far, both)
    outs = (shape((PIECES,) + own.shape, bf16),)
    yield run(collect_kernel, "collect_documents", 0, ins, outs, (), 2)


def split_vectors(values):
    high = values.astype(bf16)
    return high, (values - high.astype(f32)).astype(bf16)


def sum_kernel(plan, emit, rows, counts, *refs):
    n_in, n_out, n_vectors = counts
    operands, made = refs[:n_in], refs[n_in:]
    kept, arrived = operands[0], operands[1 : n_in - n_vectors]

    def take(source, place):
        if isinstance(place, tuple):
            return source[place].astype(f32)
        return source[pl.ds(pl.multiple_of(place * rows, 16), rows), :].astype(f32)

    plans = plan(*place_bits())
    for which, places in enumerate(plans):
        for item, place in enumerate(places):
            other = [take(part, place) for part in arrived]
            other = other[0] if len(other) == 1 else jnp.concatenate(other, axis=0)
            value = take(kept, place) + other
            if emit is None:
                made[which][item * rows : (item + 1) * rows, :] = value.astype(bf16)
    if n_vectors:
        own, other = operands[n_in - 2], operands[n_in - 1]
        if other.dtype == f32:
            vectors = own[...] + other[...]
        else:
            start = other.shape[0] - 64
            high, low = other[start : start + 32, :], other[start + 32 : start + 64, :]
            vectors = own[...] + (high.astype(f32) + low.astype(f32))
        if emit is None:
            high, low = split_vectors(vectors)
            start = len(plans[0]) * rows
            made[0][start : start + 32, :] = high
            made[0][start + 32 : start + 64, :] = low
            made[2][...] = high.astype(f32) + low.astype(f32)
        else:
            emit_vectors(vectors, made[n_out - VECTORS :])
    if emit is not None:
        emit(value, made)


VECTORS = 11


def emit_vectors(vectors, made):
    half = D // 2
    for index, target in enumerate(made):
        for part in range(target.shape[0] // D):
            row = index + part
            target[part * D : part * D + half] = vectors[row : row + 1, :].reshape(half)
            target[part * D + half : part * D + D] = vectors[row + 16 : row + 17, :].reshape(half)


def sum_stage(name, kept, arrived, rows, plan, count, vectors=(), emit=None, outs=None):
    if outs is None:
        outs = (shape((count * rows + (64 if vectors else 0), LANES), bf16),)
        outs += (shape((count * rows, LANES), bf16),)
        if vectors:
            outs += (shape((32, LANES), f32),)
    elif vectors:
        outs = outs + (shape((D,), f32),) * (VECTORS - 1) + (shape((FF,), f32),)
    ins = (kept,) + tuple(arrived) + tuple(vectors)
    kernel = functools.partial(sum_kernel, plan, emit, rows, (len(ins), len(outs), len(vectors)))
    return run(kernel, name, 0, ins, outs, (), 4)


def reduce_tiles(sent, kept, emit, outs, vectors=None):
    rows = kept.shape[2]
    fine = lax.axis_size("dp") // 8

    late = yield tuple(sent)
    both = ()
    if vectors:
        both = (late[0], tie(swap(late[0], "blk", 1), *late))
    arrived = [tie(swap(part, "blk", 1), *late) for part in sent]

    def core_plan(core, y, b0, b1, b2):
        def places(mine_x, mine_y):
            return [
                (
                    core * mine_y + (1 - core) * u,
                    i * 4 + j * 2 + core * u + (1 - core) * mine_x,
                )
                for u in (0, 1)
                for i in (0, 1)
                for j in (0, 1)
            ]

        return places(1 - b0, 1 - y), places(b0, y)

    send, kept, *own = sum_stage("sum_core", kept, arrived, rows, core_plan, 8, both)
    late = yield (send,)
    got = tie(swap_turned(send, True), *late)

    def first_plan(core, y, b0, b1, b2):
        u = core * b0 + (1 - core) * y
        return [[v * 4 + item for item in range(4)] for v in (1 - u, u)]

    both = (own[0], got) if own else ()
    send, kept, *own = sum_stage("sum_first", kept, (got,), rows, first_plan, 4, both)
    late = yield (send,)
    got = tie(swap_turned(send, False), *late)

    def second_plan(core, y, b0, b1, b2):
        return [[i * 2 + j for i in (0, 1)] for j in (1 - b1, b1)]

    both = (own[0], got) if own else ()
    send, kept, *own = sum_stage("sum_second", kept, (got,), rows, second_plan, 2, both)
    late = yield (send,)
    got = tie(swap(send, "dp", 2 * fine), *late)

    def third_plan(core, y, b0, b1, b2):
        return [1 - b2], [b2]

    both = (own[0], got) if own else ()
    send, kept, *own = sum_stage("sum_third", kept, (got,), rows, third_plan, 1, both)
    late = yield (send,)
    got = tie(swap(send, "dp", 4 * fine), *late)

    def last_plan(core, y, b0, b1, b2):
        return ([0],)

    both = (own[0], got) if own else ()
    yield sum_stage("sum_last", kept, (got,), rows, last_plan, 1, both, emit, outs)


def emit_down(tile, made):
    made[0][...] = tile.T


def emit_up(tile, made):
    block = D // PIECES
    made[0][:, 0:LANES] = tile[0:96]
    made[0][:, LANES:] = tile[144:240]
    made[1][0:48, :] = tile[96:144, :block]
    made[1][48:96, :] = tile[96:144, block:]


def emit_pair(tile, made):
    block = D // PIECES
    made[0][...] = tile[0:96, :block]
    made[1][...] = tile[0:96, block:]
    made[2][0:48, :] = tile[96:144, :block]
    made[2][48:96, :] = tile[96:144, block:]


def finish(tile, axis):
    size = lax.axis_size("dp")
    fine = size // 8
    if fine == 1:
        return tile
    groups = [[index * fine + item for item in range(fine)] for index in range(8)]
    return lax.psum_scatter(
        tile, "dp", scatter_dimension=axis, axis_index_groups=groups, tiled=True
    )


def local(
    hidden_in,
    pad_mask,
    masked_flag,
    replaced_flag,
    mask_vector,
    replace_vector,
    w_query,
    b_query,
    w_key,
    w_value,
    b_value,
    w_out,
    b_out,
    gain_one,
    shift_one,
    w_up,
    b_up,
    w_down,
    b_down,
    gain_two,
    shift_two,
    out_grad,
):
    codes = (pad_mask + 2 * masked_flag + 4 * replaced_flag).astype(f32)
    spread_in = spread(hidden_in, codes)
    pieces = move_pieces(spread_in)
    grad_pieces = move_pieces(spread_plain(tie(out_grad, *spread_in)))
    vectors = (
        mask_vector,
        replace_vector,
        b_query,
        b_value,
        b_out,
        gain_one,
        shift_one,
        b_down,
        gain_two,
        shift_two,
        b_up,
    )
    (
        entries,
        queries,
        keyed,
        valued,
        context,
        key_bias,
        stats,
        hat_one,
        scale_one,
        normed_low,
        active,
        slope,
        hat_two,
        scale_two,
        flags,
        *hidden_out,
    ) = forward(pieces, vectors, w_query, w_key, w_value, w_out, w_up, w_down)
    grad_z_two, grad_dropped, vectors_two, kept, *sent = down_back(
        grad_pieces, hat_two, scale_two, active, gain_two
    )
    block = D // PIECES
    square = shape((D // 8, block), f32)
    down = reduce_tiles(sent, kept, emit_down, (shape((FF // 8, block), f32),))
    ties = next(down)
    grad_lifted, grad_b_up = lifted_back(tie(grad_dropped, *ties), w_down, slope)
    ties = down.send((grad_b_up,))
    hidden_back = gather_documents(*hidden_out)
    next(hidden_back)
    attention = (queries, keyed, valued, key_bias, stats)
    found = middle_back(
        1,
        gain_one,
        grad_lifted,
        w_up,
        tie(grad_z_two, *ties),
        hat_one,
        scale_one,
        w_out,
        context,
        normed_low,
        *attention,
    )
    grad_z_one, grad_attended, delta, vectors_one, _, kept, *sent = found[:-3]
    grads = found[-3:]
    up = reduce_tiles(sent, kept, emit_up, (shape((D // 8, D), f32), square))
    ties = next(up)
    ties = down.send(ties)
    ties += hidden_back.send(ties)
    attention += (grad_attended,)
    grads += attention_back(1, 4, *attention, tie(delta, *ties))
    ties = up.send((grads[3],))
    (hidden_out,) = hidden_back.send(ties)
    ties = down.send((hidden_out, *ties))
    grad_q, grad_k, grad_v, vectors_qv, kept, *sent = weights_back(
        5, 1, *attention, tie(delta, *ties), entries, *grads
    )
    pair = reduce_tiles(sent, kept, emit_pair, (square,) * 3, True)
    ties = next(pair)
    *grad_in, vectors = start_back(
        (w_query, w_key, w_value),
        tie(grad_z_one, *ties),
        flags,
        (vectors_two, vectors_one, grad_b_up, vectors_qv),
        (grad_q, grad_k, grad_v),
    )
    ties = up.send((vectors,))
    ties = pair.send((vectors, *ties))
    ties = down.send(ties)
    ties = up.send(ties)
    (grad_w_down,) = down.send(ties)
    ties = pair.send((grad_w_down,))
    own, near, far = grad_in
    grad_back = gather_documents(own, near, tie(far, *ties))
    next(grad_back)
    ties = up.send(ties)
    ties = pair.send(ties)
    ties = grad_back.send(ties)
    grad_w_up, grad_w_out = up.send(ties)
    ties = pair.send((grad_w_up,))
    (grad_in,) = grad_back.send(ties)
    grad_w_query, grad_w_key, grad_w_value, *vectors = pair.send((grad_in,))
    return (
        hidden_out,
        grad_in,
        vectors[0],
        vectors[1],
        finish(grad_w_query, 0),
        vectors[2],
        finish(grad_w_key, 0),
        finish(grad_w_value, 0),
        vectors[3],
        finish(grad_w_out, 0),
        vectors[9],
        vectors[7],
        vectors[8],
        finish(grad_w_up, 0),
        vectors[10],
        finish(grad_w_down, 0),
        vectors[6],
        vectors[4],
        vectors[5],
    )


def solution(mesh):
    replicated = (P(),) * 17
    placed = (P("dp", "blk", None),) + (P("dp", "blk"),) * 3 + replicated
    placed = placed + (P("dp", "blk", None),)
    tiles = P("dp", "blk")
    rows = P("dp", "blk", None)
    return jax.shard_map(
        local,
        mesh=mesh,
        in_specs=placed,
        out_specs=(
            rows,
            rows,
            P(),
            P(),
            tiles,
            P(),
            tiles,
            tiles,
            P(),
            tiles,
            P(),
            P(),
            P(),
            tiles,
            P(),
            tiles,
            P(),
            P(),
            P(),
        ),
        check_vma=False,
    )
```

```python
import functools

import jax
import jax.numpy as jnp
import numpy as np
from jax import lax
from jax.experimental import pallas as pl
from jax.experimental.pallas import tpu as pltpu
from jax.sharding import PartitionSpec as P

D = 768
HEADS = 12
HEAD_SIZE = 64
FF = 3072
PIECES = 4
MIB = 1024 * 1024

epsilon = 1e-05
log_two_e = 1.4426950408889634
query_scale = HEAD_SIZE ** (-0.5) * log_two_e
left_out = -1e30

f32 = jnp.float32
bf16 = jnp.bfloat16

VMEM = pl.BlockSpec(memory_space=pltpu.VMEM)


def cost(micros):
    return pl.CostEstimate(flops=int(micros * 4e9), bytes_accessed=1024, transcendentals=0)


def shape(dims, dtype):
    return jax.ShapeDtypeStruct(dims, dtype)


def dot(left_side, right_side):
    return jnp.dot(left_side, right_side, preferred_element_type=f32)


def dot_right_t(left_side, right_side):
    return lax.dot_general(
        left_side, right_side, (((1,), (1,)), ((), ())), preferred_element_type=f32
    )


def lane_half(rows, which):
    lane = lax.broadcasted_iota(jnp.int32, (rows, 2 * HEAD_SIZE), 1)
    return (lane < HEAD_SIZE) if which == 0 else (lane >= HEAD_SIZE)


def normal_cdf(values):
    bell = jnp.exp2(values * values * (-0.5 * log_two_e))
    t = 1.0 / (1.0 + jnp.abs(values) * (0.3275911 * 0.7071067811865476))
    poly = 0.5 * 1.061405429 * t + 0.5 * -1.453152027
    poly = poly * t + 0.5 * 1.421413741
    poly = poly * t + 0.5 * -0.284496736
    poly = poly * t + 0.5 * 0.254829592
    tail = poly * t * bell
    return jnp.where(values >= 0, 1.0 - tail, tail), bell


def norm(values):
    centred = values - jnp.mean(values, axis=-1, keepdims=True)
    spread = jnp.mean(centred * centred, axis=-1, keepdims=True)
    scale = lax.rsqrt(spread + epsilon)
    return centred * scale, scale


def norm_back(grad, hat, scale, gain):
    lifted = grad * gain
    mean_one = jnp.mean(lifted, axis=-1, keepdims=True)
    mean_two = jnp.mean(lifted * hat, axis=-1, keepdims=True)
    return scale * (lifted - mean_one - hat * mean_two)


def room(items, more):
    total = more * MIB
    for item in items:
        *lead, rows, lanes = (1,) + tuple(item.shape)
        size = (rows + 15) // 16 * 16 * ((lanes + 127) // 128 * 128)
        total += int(np.prod(lead)) * size * jnp.dtype(item.dtype).itemsize
    return min(total, 62 * MIB)


def run(kernel, name, micros, ins, outs, scratch=(), more=10):
    return pl.pallas_call(
        kernel,
        out_shape=outs,
        in_specs=[VMEM] * len(ins),
        out_specs=(VMEM,) * len(outs),
        scratch_shapes=[pltpu.VMEM(item.shape, item.dtype) for item in scratch],
        compiler_params=pltpu.CompilerParams(vmem_limit_bytes=room(scratch, more)),
        cost_estimate=cost(micros),
        name=name,
    )(*ins)


def back_shapes(rows):
    seq = rows // PIECES
    return (shape((seq, D), bf16),) * 2 + (shape((2, seq, D), bf16),)


def put_pieces(values, targets):
    seq = values.shape[0] // 2
    for item in (0, 1):
        target = targets[item] if len(targets) == 2 else targets[0].at[item]
        target[...] = values[item * seq : (item + 1) * seq, :]


def sums(values):
    return jnp.sum(values, axis=0, keepdims=True)


def place_bits():
    blk = lax.axis_index("blk")
    coarse = lax.axis_index("dp") // (lax.axis_size("dp") // 8)
    return blk % 2, blk // 2, coarse % 2, (coarse // 2) % 2, coarse // 4


def unpack_flags(codes):
    replaced = (codes >= 4).astype(f32)
    codes = codes - 4 * replaced
    masked = (codes >= 2).astype(f32)
    pad = codes - 2 * masked
    lane = lax.broadcasted_iota(jnp.int32, (codes.shape[0], 16), 1)
    return jnp.where(lane == 0, pad, jnp.where(lane == 1, masked, replaced))


def forward_kernel(*refs):
    vectors, refs = refs[:11], refs[11:]
    pieces, refs = refs[:PIECES], refs[PIECES:]
    w_query, w_key, w_value, w_out, w_up, w_down, *refs = refs
    made, refs = refs[:18], refs[18:]
    start, value_t, context_t, dropped = refs
    (
        entries,
        queries,
        keyed,
        valued,
        context,
        key_bias,
        stats,
        hat_one,
        scale_one,
        normed_low,
        active,
        slope,
        hat_two,
        scale_two,
        flags_out,
        *hidden_out,
    ) = made
    (
        mask_vector,
        replace_vector,
        b_query,
        b_value,
        b_out,
        gain_one,
        shift_one,
        b_down,
        gain_two,
        shift_two,
        b_up,
    ) = (vector[...].reshape(1, -1) for vector in vectors)
    seq = pieces[0].shape[0] - 16
    rows = PIECES * seq
    row_id = lax.broadcasted_iota(jnp.int32, (seq, seq), 0)
    col_id = lax.broadcasted_iota(jnp.int32, (seq, seq), 1)
    eye = (row_id == col_id).astype(bf16)
    for index, piece in enumerate(pieces):
        where = pl.ds(index * seq, seq)
        columns = dot_right_t(eye, piece[seq : seq + 16, 0:seq])
        columns = unpack_flags(columns[:, 0:1])
        flags_out[where, :] = columns
        key_bias[where, :] = jnp.where(
            lax.broadcasted_iota(jnp.int32, (seq, 128), 1) == 0,
            (1.0 - columns[:, 0:1]) * left_out,
            0.0,
        ).astype(bf16)
        rows_here = jnp.where(
            columns[:, 1:2] > 0, mask_vector, piece[0:seq, :].astype(f32)
        )
        rows_here = rows_here + columns[:, 2:3] * replace_vector
        start[where, :] = rows_here
        entries[where, :] = rows_here.astype(bf16)
    queries[...] = ((dot(entries[...], w_query[...]) + b_query) * query_scale).astype(bf16)
    keyed[...] = dot(entries[...], w_key[...]).astype(bf16)
    valued[...] = (dot(entries[...], w_value[...]) + b_value).astype(bf16)
    value_t[...] = valued[...].T

    ones_lane = (lax.broadcasted_iota(jnp.int32, (rows, 128), 1) == 0).astype(bf16)
    ones_rows = jnp.ones((16, rows), bf16)

    def head_scores(pair, which):
        columns = pl.ds(pl.multiple_of(pair * 128, 128), 128)
        query_pair = jnp.concatenate([queries[:, columns], ones_lane], axis=1)
        key_pair = keyed[:, columns]
        key_head = jnp.where(lane_half(rows, which), key_pair, jnp.zeros_like(key_pair))
        key_head = jnp.concatenate([key_head, key_bias[...]], axis=1)
        return dot_right_t(key_head, query_pair)

    together = 2

    def group_step(group, carry):
        first = group * together
        following = head_scores(first, 0)
        for index in range(2 * together):
            scores = following
            if index + 1 < 2 * together:
                following = head_scores(first + (index + 1) // 2, (index + 1) % 2)
            peak = jnp.max(scores, axis=0, keepdims=True)
            weights = jnp.exp2(scores - peak).astype(bf16)
            head = first * 2 + index
            head_rows = pl.ds(pl.multiple_of(head * HEAD_SIZE, HEAD_SIZE), HEAD_SIZE)
            values = jnp.concatenate([value_t[head_rows, :], ones_rows], axis=0)
            summed = dot(values, weights)
            total = summed[HEAD_SIZE : HEAD_SIZE + 1, :]
            context_t[head_rows, :] = (summed[:HEAD_SIZE, :] * (1.0 / total)).astype(bf16)
            stats[pl.ds(head, 1), :] = peak + jnp.log2(total)
        return carry

    stats[pl.ds(8, 8), :] = jnp.zeros((8, rows), f32)
    lax.fori_loop(0, HEADS // 2 // together, group_step, 0)
    context[...] = context_t[...].T
    half = rows // 2
    for index in range(2):
        where = pl.ds(index * half, half)
        branch = dot(context[where, :], w_out[...]) + b_out
        hat, scale = norm(start[where, :] + branch)
        hat_one[where, :] = hat
        scale_one[where, :] = scale
        normed_low[where, :] = (hat * gain_one + shift_one).astype(bf16)
    chunk = 256
    count = FF // chunk

    def lift(index):
        columns = slice(index * chunk, (index + 1) * chunk)
        return dot(normed_low[...], w_up[:, columns]) + b_up[:, columns]

    following = lift(0)
    for index in range(count):
        lifted = following
        if index + 1 < count:
            following = lift(index + 1)
        columns = pl.ds(index * chunk, chunk)
        cdf, bell = normal_cdf(lifted)
        act = (lifted * cdf).astype(bf16)
        active[:, columns] = act
        slope[:, columns] = (cdf + lifted * bell * 0.3989422804014327).astype(bf16)
        part = dot(act, w_down[columns, :])
        if index == 0:
            dropped[...] = part
        else:
            dropped[...] += part
    for index in range(2):
        where = pl.ds(index * half, half)
        normed = hat_one[where, :] * gain_one + shift_one
        hat, scale = norm(normed + dropped[where, :] + b_down)
        hat_two[where, :] = hat
        scale_two[where, :] = scale
        low = (hat * gain_two + shift_two).astype(bf16)
        put_pieces(low, hidden_out[index * 2 : index * 2 + 2])


def forward(pieces, vectors, *weights):
    rows = PIECES * (pieces[0].shape[0] - 16)
    ins = tuple(vectors) + tuple(pieces) + weights
    outs = (
        shape((rows, D), bf16),
        shape((rows, D), bf16),
        shape((rows, D), bf16),
        shape((rows, D), bf16),
        shape((rows, D), bf16),
        shape((rows, 128), bf16),
        shape((16, rows), f32),
        shape((rows, D), f32),
        shape((rows, 1), f32),
        shape((rows, D), bf16),
        shape((rows, FF), bf16),
        shape((rows, FF), bf16),
        shape((rows, D), f32),
        shape((rows, 1), f32),
        shape((rows, 16), f32),
    ) + back_shapes(rows)
    more = (
        shape((rows, D), f32),
        shape((D, rows), bf16),
        shape((D, rows), bf16),
        shape((rows, D), f32),
    )
    return run(forward_kernel, "forward_layer", 22, ins, outs, more)


LANES = 384
ROWS_DOWN = 192
ROWS_UP = 240
ROWS_PAIR = 144


PARTS_DOWN = (192,)
PARTS_UP = (80, 80, 80)
PARTS_PAIR = (80, 64)
WAYS_PAIR = (80, 64)


def tiles(parts):
    return tuple(shape((2, 8, rows, LANES), bf16) for rows in parts)


def put(parts, y, dp, first, value):
    low = 0
    for part in parts:
        high = low + part.shape[2]
        start, stop = max(first, low), min(first + value.shape[0], high)
        if start < stop:
            part[y, dp, start - low : stop - low] = value[start - first : stop - first]
        low = high


def halves_t(values, target):
    rows = values.shape[0]
    turned = values.T
    for dp in range(8):
        for half in range(2):
            low = dp * 96 + half * 48
            target[dp * 48 : dp * 48 + 48, half * rows : (half + 1) * rows] = turned[
                low : low + 48, :
            ]


def halves_wide(values, target):
    rows = values.shape[0]
    block = D // PIECES
    nothing = jnp.zeros((rows, block), bf16)
    for index in range(PIECES):
        piece = values[:, index * block : (index + 1) * block]
        wide = slice(index * LANES, (index + 1) * LANES)
        target[0:rows, wide] = jnp.concatenate([piece, nothing], axis=1)
        target[rows : 2 * rows, wide] = jnp.concatenate([nothing, piece], axis=1)


def down_kernel(*refs):
    gain, refs = refs[0], refs[1:]
    pieces, (hat_two, scale_two, active, *refs) = refs[:PIECES], refs[PIECES:]
    count = len(PARTS_DOWN)
    grad_z_two, grad_dropped, vectors, kept, *refs = refs
    sent, (grad_t,) = refs[:count], refs[count:]
    gain_two = gain[...].reshape(1, D)
    seq = pieces[0].shape[0]
    core = place_bits()[0]
    totals = [jnp.zeros((1, D), f32)] * 3
    for index, piece in enumerate(pieces):
        where = pl.ds(index * seq, seq)
        grad = piece[...].astype(f32)
        hat = hat_two[where, :]
        grad_z = norm_back(grad, hat, scale_two[where, :], gain_two)
        low = grad_z.astype(bf16)
        grad_z_two[where, :] = grad_z
        grad_dropped[where, :] = low
        terms = (grad * hat, grad, low.astype(f32))
        totals = [total + sums(term) for total, term in zip(totals, terms)]
    vectors[...] = jnp.concatenate(totals + [jnp.zeros((5, D), f32)], axis=0)
    block = D // PIECES
    grad_t[...] = grad_dropped[...].T
    order = [1 - core, 3 - core, core, 2 + core]
    left_side = jnp.concatenate(
        [grad_t[pl.ds(pl.multiple_of(index * block, block), block), :] for index in order], axis=0
    )
    for pair in range(4):
        part = dot(left_side, active[:, pl.ds(pair * D, D)]).astype(bf16)
        for dp in range(2):
            columns = slice(dp * LANES, dp * LANES + LANES)
            for y in range(2):
                put(sent, y, pair * 2 + dp, 0, part[y * block : (y + 1) * block, columns])
                kept[y, pair * 2 + dp] = part[(y + 2) * block : (y + 3) * block, columns]


def down_back(pieces, hat_two, scale_two, active, gain_two):
    rows = PIECES * pieces[0].shape[0]
    ins = (gain_two,) + tuple(pieces) + (hat_two, scale_two, active)
    outs = (
        shape((rows, D), f32),
        shape((rows, D), bf16),
        shape((8, D), f32),
        *tiles((ROWS_DOWN,)),
        *tiles(PARTS_DOWN),
    )
    more = (shape((D, rows), bf16),)
    return run(down_kernel, "down_back", 7, ins, outs, more)


def lifted_kernel(grad_dropped, w_down, slope, grad_lifted, grad_b_up):
    block = FF // PIECES
    for index in range(PIECES):
        columns = pl.ds(index * block, block)
        grad = dot_right_t(grad_dropped[...], w_down[columns, :])
        grad = (grad * slope[:, columns].astype(f32)).astype(bf16)
        grad_lifted[:, columns] = grad
        grad_b_up[:, columns] = sums(grad.astype(f32))


def lifted_back(grad_dropped, w_down, slope):
    rows = grad_dropped.shape[0]
    ins = (grad_dropped, w_down, slope)
    outs = (shape((rows, FF), bf16), shape((1, FF), f32))
    return run(lifted_kernel, "lifted_back", 5, ins, outs)


def middle_kernel(gain, *refs):
    inside, refs = refs[:8], refs[8:]
    grad_z_one, grad_attended, delta, vectors, grad_branch, kept, *refs = refs
    sent, (normed_t, context_t, wide) = refs[: len(PARTS_UP)], refs[len(PARTS_UP) :]
    grad_lifted, w_up, grad_z_two, hat_one, scale_one, w_out, context, normed_low = inside
    core = place_bits()[0]
    rows = grad_z_two.shape[0]
    half = rows // 2
    gain_one = gain[...].reshape(1, D)
    totals = [jnp.zeros((1, D), f32)] * 3
    head = lax.broadcasted_iota(jnp.int32, (16, D), 0)
    feature = lax.broadcasted_iota(jnp.int32, (16, D), 1)
    heads = (feature // HEAD_SIZE == head).astype(bf16)
    for index in range(2):
        where = pl.ds(index * half, half)
        grad = dot_right_t(grad_lifted[where, :], w_up[...])
        grad = grad_z_two[where, :] + grad
        hat = hat_one[where, :]
        grad_z = norm_back(grad, hat, scale_one[where, :], gain_one)
        low = grad_z.astype(bf16)
        grad_z_one[where, :] = grad_z
        grad_branch[where, :] = low
        terms = (grad * hat, grad, low.astype(f32))
        totals = [total + sums(term) for total, term in zip(totals, terms)]
        attended = dot_right_t(low, w_out[...])
        grad_attended[where, :] = attended.astype(bf16)
        products = attended * context[where, :].astype(f32)
        high = products.astype(bf16)
        rest = (products - high.astype(f32)).astype(bf16)
        delta[:, where] = dot_right_t(heads, high) + dot_right_t(heads, rest)
    vectors[...] = jnp.concatenate(totals + [jnp.zeros((5, D), f32)], axis=0)
    normed_t[...] = normed_low[...].T
    halves_wide(grad_branch[...], wide)
    halves_t(context[...], context_t)
    block = FF // PIECES
    for index, which in enumerate([1 - core, 3 - core, core, 2 + core]):
        columns = pl.ds(pl.multiple_of(which * block, block), block)
        part = dot(normed_t[...], grad_lifted[:, columns]).astype(bf16)
        columns = pl.ds(pl.multiple_of(which * LANES, LANES), LANES)
        extra = dot(context_t[...], wide[:, columns]).astype(bf16)
        target = (sent, (kept,))[index // 2]
        y = index % 2
        for dp in range(8):
            put(target, y, dp, 0, part[dp * 96 : dp * 96 + 96, 0:LANES])
            put(target, y, dp, 96, extra[dp * 48 : dp * 48 + 48, :])
            put(target, y, dp, 144, part[dp * 96 : dp * 96 + 96, LANES:])


def middle_back(*ins):
    rows = ins[1].shape[0]
    whole = shape((rows, D), bf16)
    outs = (
        shape((rows, D), f32),
        whole,
        shape((16, rows), f32),
        shape((8, D), f32),
        whole,
        *tiles((ROWS_UP,)),
        *tiles(PARTS_UP),
    )
    more = (
        shape((D, rows), bf16),
        shape((D // 2, 2 * rows), bf16),
        shape((2 * rows, 2 * D), bf16),
    )
    return run(middle_kernel, "middle_up_back", 10, ins, outs, more)


def attention_steps(first, pairs, inside, grads, base=0):
    queries, keyed, valued, key_bias, stats, grad_attended, delta = inside
    grad_q, grad_k, grad_v = grads
    rows = queries.shape[0]
    ones_lane = (lax.broadcasted_iota(jnp.int32, (rows, 128), 1) == 0).astype(bf16)
    low = lane_half(rows, 0)
    nothing = jnp.zeros((rows, 128), bf16)

    def products(head):
        pair, which = head // 2, head % 2
        columns = pl.ds(pair * 128, 128)
        own = lane_half(rows, which)
        query_wide = jnp.concatenate([queries[:, columns], ones_lane], axis=1)
        key_head = jnp.where(own, keyed[:, columns], nothing)
        key_head = jnp.concatenate([key_head, key_bias[...]], axis=1)
        value_head = jnp.where(own, valued[:, columns], nothing)
        return (
            dot_right_t(key_head, query_wide),
            dot_right_t(value_head, grad_attended[:, columns]),
        )

    following = products(2 * first)
    for index in range(pairs):
        pair = first + index
        columns = pl.ds(pair * 128, 128)
        target = pl.ds(base + index * 128, 128)
        query_pair = queries[:, columns]
        key_pair_t = keyed[:, columns].T
        grad_pair = grad_attended[:, columns]
        found = []
        for which in range(2):
            head = 2 * pair + which
            scores, grad_weights = following
            if head + 1 < 2 * (first + pairs):
                following = products(head + 1)
            here = pl.ds(head, 1)
            weights = jnp.exp2(scores - stats[here, :])
            grad_raw = (weights * (grad_weights - delta[here, :])).astype(bf16)
            grad_v_pair = dot(weights.astype(bf16), grad_pair)
            grad_k_pair = dot(grad_raw, query_pair)
            head_rows = slice(which * HEAD_SIZE, which * HEAD_SIZE + HEAD_SIZE)
            grad_q_t = dot(key_pair_t[head_rows, :], grad_raw)
            found.append((grad_q_t, grad_k_pair, grad_v_pair))
        grad_q_t = jnp.concatenate([found[0][0], found[1][0]], axis=0) * HEAD_SIZE ** (-0.5)
        grad_q[:, target] = grad_q_t.T.astype(bf16)
        grad_k_pair = jnp.where(low, found[0][1], found[1][1]) * (1.0 / log_two_e)
        grad_k[:, target] = grad_k_pair.astype(bf16)
        grad_v[:, target] = jnp.where(low, found[0][2], found[1][2]).astype(bf16)


def attention_kernel(first, pairs, *refs):
    attention_steps(first, pairs, refs[:7], refs[7:])


def attention_back(first, pairs, *ins):
    rows = ins[0].shape[0]
    outs = (shape((rows, pairs * 128), bf16),) * 3
    kernel = functools.partial(attention_kernel, first, pairs)
    return run(kernel, "attention_back", 0, ins, outs)


def weights_kernel(first, pairs, *refs):
    inside, (entries, *before), refs = refs[:7], refs[7:11], refs[11:]
    merged, (vectors, kept, *refs) = refs[:3], refs[3:]
    sent, refs = refs[: len(PARTS_PAIR)], refs[len(PARTS_PAIR) :]
    entries_t, entries_half, wide_qk, wide_v = refs
    core = place_bits()[0]
    for part, target in zip(before, merged):
        target[:, 0 : first * 128] = part[...]
    attention_steps(first, pairs, inside, merged, first * 128)
    turned = entries[...]
    entries_t[...] = turned.T
    halves_t(turned, entries_half)
    block = D // PIECES
    grad_q, grad_k, grad_v = merged
    for index in range(PIECES):
        piece = slice(index * block, (index + 1) * block)
        wide = slice(index * LANES, (index + 1) * LANES)
        wide_qk[:, wide] = jnp.concatenate([grad_q[:, piece], grad_k[:, piece]], axis=1)
    halves_wide(grad_v[...], wide_v)
    for index, which in enumerate([1 - core, 3 - core, core, 2 + core]):
        columns = pl.ds(pl.multiple_of(which * LANES, LANES), LANES)
        part = dot(entries_t[...], wide_qk[:, columns]).astype(bf16)
        extra = dot(entries_half[...], wide_v[:, columns]).astype(bf16)
        target = (sent, (kept,))[index // 2]
        y = index % 2
        for dp in range(8):
            put(target, y, dp, 0, part[dp * 96 : dp * 96 + 96, :])
            put(target, y, dp, 96, extra[dp * 48 : dp * 48 + 48, :])
    vectors[0:1, :] = sums(grad_q[...].astype(f32))
    vectors[1:2, :] = sums(grad_v[...].astype(f32))


def weights_back(first, pairs, *ins):
    rows = ins[0].shape[0]
    whole = shape((rows, D), bf16)
    outs = (whole,) * 3 + (shape((2, D), f32), *tiles((ROWS_PAIR,)), *tiles(PARTS_PAIR))
    more = (
        shape((D, rows), bf16),
        shape((D // 2, 2 * rows), bf16),
        shape((rows, 2 * D), bf16),
        shape((2 * rows, 2 * D), bf16),
    )
    kernel = functools.partial(weights_kernel, first, pairs)
    return run(kernel, "attention_weights_back", 2.2 * pairs + 4, ins, outs, more)


def start_kernel(*refs):
    w_query, w_key, w_value, grad_z_one, flags, two, one, b_up, late = refs[:9]
    grads, made = refs[9:12], refs[12:]
    *grad_in, vectors = made
    seq = grad_z_one.shape[0] // PIECES
    half = D // 2
    totals = [jnp.zeros((1, D), f32)] * 2
    for step in range(2):
        where = pl.ds(step * 2 * seq, 2 * seq)
        grad = grad_z_one[where, :]
        for value, weight in zip(grads, (w_query, w_key, w_value)):
            grad = grad + dot_right_t(value[where, :], weight[...])
        masked = flags[where, 1:2]
        replaced = flags[where, 2:3]
        terms = (grad * masked, grad * replaced)
        totals = [total + sums(term) for total, term in zip(totals, terms)]
        low = jnp.where(masked > 0, 0.0, grad).astype(bf16)
        put_pieces(low, grad_in[step * 2 : step * 2 + 2])
    rows = totals + [late[...], two[0:3, :], one[0:3, :]]
    rows += [b_up[:, index * D : (index + 1) * D] for index in range(FF // D)]
    rows = jnp.concatenate(rows + [jnp.zeros((2, D), f32)], axis=0)
    vectors[0:16, :] = rows[:, :half]
    vectors[16:32, :] = rows[:, half:]


def start_back(weights, grad_z_one, flags, vectors, grads):
    rows = grad_z_one.shape[0]
    ins = tuple(weights) + (grad_z_one, flags) + tuple(vectors) + tuple(grads)
    outs = (shape((rows // PIECES, D), bf16),) * PIECES + (shape((32, LANES), f32),)
    return run(start_kernel, "start_back", 0, ins, outs)


def swap(value, axis, bit):
    size = lax.axis_size(axis)
    return lax.ppermute(value, axis, [(i, i ^ bit) for i in range(size)])


def swap_turned(value, first):
    blks = lax.axis_size("blk")
    fine = lax.axis_size("dp") // 8
    pairs = []
    for dp in range(lax.axis_size("dp")):
        for blk in range(blks):
            along_dp = (blk % 2 == 0) == first
            other = (dp ^ fine) * blks + blk if along_dp else dp * blks + (blk ^ 2)
            pairs.append((dp * blks + blk, other))
    return lax.ppermute(value, ("dp", "blk"), pairs)


def tie(value, *others):
    return lax.optimization_barrier((value,) + tuple(others))[0]


def spread_kernel(hidden, flags, *out):
    blk = lax.axis_index("blk")
    seq = hidden.shape[1]
    for step in range(PIECES):
        document = blk ^ step
        out[step][0:seq, :] = hidden[document]
        row = flags[pl.ds(document, 1), :]
        out[step][seq : seq + 16, 0:seq] = jnp.concatenate(
            [row, jnp.zeros((15, seq), f32)], axis=0
        ).astype(bf16)
        out[step][seq : seq + 16, seq:] = jnp.zeros((16, hidden.shape[2] - seq), bf16)


def spread(hidden, flags):
    documents, seq, width = hidden.shape
    outs = (shape((seq + 16, width), bf16),) * PIECES
    return run(spread_kernel, "spread_documents", 1, (hidden, flags), outs, (), 2)


def spread_plain_kernel(hidden, *out):
    blk = lax.axis_index("blk")
    for step in range(PIECES):
        out[step][...] = hidden[blk ^ step]


def spread_plain(hidden):
    outs = (shape(hidden.shape[1:], bf16),) * PIECES
    return run(spread_plain_kernel, "spread_grads", 1, (hidden,), outs, (), 2)


def move_pieces(pieces):
    own, *others = pieces
    return [own] + [swap(piece, "blk", step + 1) for step, piece in enumerate(others)]


def collect_kernel(own, near, far, both, out):
    blk = lax.axis_index("blk")
    out[blk] = own[...]
    out[blk ^ 1] = near[...]
    out[blk ^ 2] = far[0]
    out[blk ^ 3] = both[1]


def collect_direct_kernel(*refs):
    blk = lax.axis_index("blk")
    for step in range(PIECES):
        refs[PIECES][blk ^ step] = refs[step][...]


def gather_direct(pieces, late):
    pieces = lax.optimization_barrier((*pieces, *late))[:PIECES]
    back = [swap(pieces[step], "blk", step) for step in range(1, PIECES)]
    late = yield
    ins = (pieces[0], *(tie(piece, *late) for piece in back))
    outs = (shape((PIECES,) + pieces[0].shape, bf16),)
    yield run(collect_direct_kernel, "collect_documents", 0, ins, outs, (), 2)[0]


def gather_documents(own, near, far):
    late = yield
    near = tie(swap(near, "blk", 1), *late)
    far = tie(swap(far, "blk", 2), *late)
    late = yield (near, far)
    both = tie(swap(far, "blk", 1), *late)
    ins = (own, near, far, both)
    outs = (shape((PIECES,) + own.shape, bf16),)
    yield run(collect_kernel, "collect_documents", 0, ins, outs, (), 2)


def split_vectors(values):
    high = values.astype(bf16)
    return high, (values - high.astype(f32)).astype(bf16)


def sum_kernel(plan, emit, split_in, split_out, wide, n_vectors, *refs):
    kept, *arrived = refs[: 1 + len(split_in)]
    vectors_in = refs[1 + len(split_in) : 1 + len(split_in) + n_vectors]
    made = refs[1 + len(split_in) + n_vectors :]
    rows = sum(split_in)

    def take(source, place, height):
        if isinstance(place, tuple):
            return source[place].astype(f32)
        where = pl.ds(pl.multiple_of(place * height, 16), height)
        return source[where, :].astype(f32)

    plans = plan(*place_bits())
    targets = (made[: len(split_out)], made[len(split_out) : len(split_out) + 1])
    for group, splits, places in zip(targets, (split_out, (rows,)), plans):
        for item, place in enumerate(places):
            other = [take(part, place, height) for part, height in zip(arrived, split_in)]
            other = other[0] if len(other) == 1 else jnp.concatenate(other, axis=0)
            value = take(kept, place, rows) + other
            low = 0
            if emit is None:
                for target, height in zip(group, splits):
                    part = value[low : low + height].astype(bf16)
                    target[item * height : (item + 1) * height, :] = part
                    low += height
    if n_vectors:
        own, other = vectors_in
        if other.dtype == f32:
            vectors = own[...] + other[...]
        else:
            tail = 64 if other.shape[0] % split_in[-1] == 64 % split_in[-1] else 32
            start = other.shape[0] - tail
            vectors = own[...] + other[start : start + 32, :].astype(f32)
            if tail == 64:
                vectors = vectors + other[start + 32 : start + 64, :].astype(f32)
        if emit is None:
            high, low = split_vectors(vectors)
            target = targets[0][-1]
            start = target.shape[0] - (64 if wide else 32)
            target[start : start + 32, :] = high
            kept_vectors = high.astype(f32)
            if wide:
                target[start + 32 : start + 64, :] = low
                kept_vectors = kept_vectors + low.astype(f32)
            made[-1][...] = kept_vectors
        else:
            emit_vectors(vectors, made[len(made) - VECTORS :])
    if emit is not None:
        emit(value, made)


VECTORS = 11


def emit_vectors(vectors, made):
    half = D // 2
    for index, target in enumerate(made):
        for part in range(target.shape[0] // D):
            row = index + part
            target[part * D : part * D + half] = vectors[row : row + 1, :].reshape(half)
            target[part * D + half : part * D + D] = vectors[row + 16 : row + 17, :].reshape(half)


def sum_stage(
    name,
    kept,
    arrived,
    rows,
    plan,
    count,
    vectors=(),
    emit=None,
    outs=None,
    wide=True,
    split_in=None,
    split_out=None,
):
    split_in = split_in or (rows,)
    split_out = split_out or (rows,)
    if outs is None:
        heights = [count * height for height in split_out]
        if vectors:
            heights[-1] += 64 if wide else 32
        outs = tuple(shape((height, LANES), bf16) for height in heights)
        outs += (shape((count * rows, LANES), bf16),)
        if vectors:
            outs += (shape((32, LANES), f32),)
    elif vectors:
        outs = outs + (shape((D,), f32),) * (VECTORS - 1) + (shape((FF,), f32),)
    ins = (kept,) + tuple(arrived) + tuple(vectors)
    kernel = functools.partial(sum_kernel, plan, emit, split_in, split_out, wide, len(vectors))
    return run(kernel, name, 0, ins, outs, (), 4)


def plan_core(core, y, b0, b1, b2):
    def places(mine_x, mine_y):
        return [
            (core * mine_y + (1 - core) * u, i * 4 + j * 2 + core * u + (1 - core) * mine_x)
            for u in (0, 1)
            for i in (0, 1)
            for j in (0, 1)
        ]

    return places(1 - b0, 1 - y), places(b0, y)


def plan_first(core, y, b0, b1, b2):
    u = core * b0 + (1 - core) * y
    return [[v * 4 + item for item in range(4)] for v in (1 - u, u)]


def plan_second(core, y, b0, b1, b2):
    return [[i * 2 + j for i in (0, 1)] for j in (1 - b1, b1)]


def plan_third(core, y, b0, b1, b2):
    return [1 - b2], [b2]


def plan_last(core, y, b0, b1, b2):
    return ([0],)


def finish_tiles(sends, kept, rows, emit, outs, own=()):
    fine = lax.axis_size("dp") // 8
    splits = WAYS_PAIR if len(sends) > 1 else (rows,)
    late = yield tuple(sends)
    got = [tie(swap_turned(send, False), *late) for send in sends]
    both = (own[0], got[-1]) if own else ()
    made = sum_stage(
        "sum_second",
        kept,
        got,
        rows,
        plan_second,
        2,
        both,
        wide=False,
        split_in=splits,
        split_out=splits,
    )
    sends, (kept, *own) = made[: len(splits)], made[len(splits) :]
    late = yield tuple(sends)
    got = [tie(swap(send, "dp", 2 * fine), *late) for send in sends]
    both = (own[0], got[-1]) if own else ()
    send, kept, *own = sum_stage(
        "sum_third", kept, got, rows, plan_third, 1, both, wide=False, split_in=splits
    )
    late = yield (send,)
    got = tie(swap(send, "dp", 4 * fine), *late)
    both = (own[0], got) if own else ()
    yield sum_stage("sum_last", kept, (got,), rows, plan_last, 1, both, emit, outs)


def reduce_tiles(sent, kept, splits, emit, outs):
    rows = sum(splits)
    late = yield tuple(sent)
    got = [tie(swap(part, "blk", 1), *late) for part in sent]
    send, kept = sum_stage("sum_core", kept, got, rows, plan_core, 8, split_in=splits)
    late = yield (send,)
    got = tie(swap_turned(send, True), *late)
    send, kept = sum_stage("sum_first", kept, (got,), rows, plan_first, 4)
    yield from finish_tiles((send,), kept, rows, emit, outs)


def reduce_pair(sent, kept, emit, outs):
    late = yield tuple(sent)
    both = (late[0], tie(swap(late[0], "blk", 1), *late))
    got = [tie(swap(part, "blk", 1), *late) for part in sent]
    *sends, kept, own = sum_stage(
        "sum_core",
        kept,
        got,
        ROWS_PAIR,
        plan_core,
        8,
        both,
        split_in=PARTS_PAIR,
        split_out=WAYS_PAIR,
    )
    late = yield tuple(sends)
    got = [tie(swap_turned(send, True), *late) for send in sends]
    both = (own, got[-1])
    *sends, kept, own = sum_stage(
        "sum_first",
        kept,
        got,
        ROWS_PAIR,
        plan_first,
        4,
        both,
        split_in=WAYS_PAIR,
        split_out=WAYS_PAIR,
    )
    yield from finish_tiles(sends, kept, ROWS_PAIR, emit, outs, (own,))


def emit_down(tile, made):
    made[0][...] = tile.T


def emit_up(tile, made):
    block = D // PIECES
    made[0][:, 0:LANES] = tile[0:96]
    made[0][:, LANES:] = tile[144:240]
    made[1][0:48, :] = tile[96:144, :block]
    made[1][48:96, :] = tile[96:144, block:]


def emit_pair(tile, made):
    block = D // PIECES
    made[0][...] = tile[0:96, :block]
    made[1][...] = tile[0:96, block:]
    made[2][0:48, :] = tile[96:144, :block]
    made[2][48:96, :] = tile[96:144, block:]


def finish(tile, axis):
    size = lax.axis_size("dp")
    fine = size // 8
    if fine == 1:
        return tile
    groups = [[index * fine + item for item in range(fine)] for index in range(8)]
    return lax.psum_scatter(
        tile, "dp", scatter_dimension=axis, axis_index_groups=groups, tiled=True
    )


def local(
    hidden_in,
    pad_mask,
    masked_flag,
    replaced_flag,
    mask_vector,
    replace_vector,
    w_query,
    b_query,
    w_key,
    w_value,
    b_value,
    w_out,
    b_out,
    gain_one,
    shift_one,
    w_up,
    b_up,
    w_down,
    b_down,
    gain_two,
    shift_two,
    out_grad,
):
    codes = (pad_mask + 2 * masked_flag + 4 * replaced_flag).astype(f32)
    spread_in = spread(hidden_in, codes)
    pieces = move_pieces(spread_in)
    grad_pieces = move_pieces(spread_plain(tie(out_grad, *spread_in)))
    vectors = (
        mask_vector,
        replace_vector,
        b_query,
        b_value,
        b_out,
        gain_one,
        shift_one,
        b_down,
        gain_two,
        shift_two,
        b_up,
    )
    (
        entries,
        queries,
        keyed,
        valued,
        context,
        key_bias,
        stats,
        hat_one,
        scale_one,
        normed_low,
        active,
        slope,
        hat_two,
        scale_two,
        flags,
        *hidden_out,
    ) = forward(pieces, vectors, w_query, w_key, w_value, w_out, w_up, w_down)
    grad_z_two, grad_dropped, vectors_two, kept, *sent = down_back(
        grad_pieces, hat_two, scale_two, active, gain_two
    )
    block = D // PIECES
    square = shape((D // 8, block), f32)
    outs = (shape((FF // 8, block), f32),)
    down = reduce_tiles(sent, kept, PARTS_DOWN, emit_down, outs)
    ties = next(down)
    grad_lifted, grad_b_up = lifted_back(tie(grad_dropped, *ties), w_down, slope)
    ties = down.send((grad_b_up,))
    hidden_back = gather_documents(*hidden_out)
    next(hidden_back)
    attention = (queries, keyed, valued, key_bias, stats)
    grad_z_one, grad_attended, delta, vectors_one, _, kept, *sent = middle_back(
        gain_one,
        grad_lifted,
        w_up,
        tie(grad_z_two, *ties),
        hat_one,
        scale_one,
        w_out,
        context,
        normed_low,
    )
    ties = hidden_back.send((delta,))
    sent = lax.optimization_barrier((*sent, *ties))[: len(sent)]
    up = reduce_tiles(sent, kept, PARTS_UP, emit_up, (shape((D // 8, D), f32), square))
    ties = next(up)
    attention += (grad_attended,)
    grads = attention_back(0, 3, *attention, tie(delta, *ties))
    ties = down.send((grads[0],))
    ties = up.send(ties)
    (hidden_out,) = hidden_back.send(ties)
    grad_q, grad_k, grad_v, vectors_qv, kept, *sent = weights_back(
        3, 3, *attention, tie(delta, hidden_out, *ties), entries, *grads
    )
    ties = down.send((vectors_qv,))
    sent = lax.optimization_barrier((*sent, *ties))[: len(sent)]
    pair = reduce_pair(sent, kept, emit_pair, (square,) * 3)
    ties = next(pair)
    *grad_in, vectors = start_back(
        (w_query, w_key, w_value),
        tie(grad_z_one, *ties),
        flags,
        (vectors_two, vectors_one, grad_b_up, vectors_qv),
        (grad_q, grad_k, grad_v),
    )
    ties = down.send((vectors,))
    ties = up.send(ties)
    ties = pair.send((vectors, *ties))
    (grad_w_down,) = down.send(ties)
    ties = up.send((grad_w_down,))
    ties = pair.send(ties)
    ties = up.send(ties)
    ties = pair.send(ties)
    grad_back = gather_direct(grad_in, ties)
    next(grad_back)
    grad_w_up, grad_w_out = up.send(ties)
    ties = pair.send((grad_w_up,))
    grad_in = grad_back.send(ties)
    grad_w_query, grad_w_key, grad_w_value, *vectors = pair.send((grad_in,))
    return (
        hidden_out,
        grad_in,
        vectors[0],
        vectors[1],
        finish(grad_w_query, 0),
        vectors[2],
        finish(grad_w_key, 0),
        finish(grad_w_value, 0),
        vectors[3],
        finish(grad_w_out, 0),
        vectors[9],
        vectors[7],
        vectors[8],
        finish(grad_w_up, 0),
        vectors[10],
        finish(grad_w_down, 0),
        vectors[6],
        vectors[4],
        vectors[5],
    )


def solution(mesh):
    replicated = (P(),) * 17
    placed = (P("dp", "blk", None),) + (P("dp", "blk"),) * 3 + replicated
    placed = placed + (P("dp", "blk", None),)
    tiles = P("dp", "blk")
    rows = P("dp", "blk", None)
    return jax.shard_map(
        local,
        mesh=mesh,
        in_specs=placed,
        out_specs=(
            rows,
            rows,
            P(),
            P(),
            tiles,
            P(),
            tiles,
            tiles,
            P(),
            tiles,
            P(),
            P(),
            P(),
            tiles,
            P(),
            tiles,
            P(),
            P(),
            P(),
        ),
        check_vma=False,
    )
```

```python
import functools

import jax
import jax.numpy as jnp
import numpy as np
from jax import lax
from jax.experimental import pallas as pl
from jax.experimental.pallas import tpu as pltpu
from jax.sharding import PartitionSpec as P

D = 768
HEADS = 12
HEAD_SIZE = 64
FF = 3072
PIECES = 4
MIB = 1024 * 1024

epsilon = 1e-05
log_two_e = 1.4426950408889634
query_scale = HEAD_SIZE ** (-0.5) * log_two_e
left_out = -1e30

f32 = jnp.float32
bf16 = jnp.bfloat16

VMEM = pl.BlockSpec(memory_space=pltpu.VMEM)


def cost(micros):
    return pl.CostEstimate(flops=int(micros * 4e9), bytes_accessed=1024, transcendentals=0)


def shape(dims, dtype):
    return jax.ShapeDtypeStruct(dims, dtype)


def dot(left_side, right_side):
    return jnp.dot(left_side, right_side, preferred_element_type=f32)


def dot_right_t(left_side, right_side):
    return lax.dot_general(
        left_side, right_side, (((1,), (1,)), ((), ())), preferred_element_type=f32
    )


def lane_half(rows, which):
    lane = lax.broadcasted_iota(jnp.int32, (rows, 2 * HEAD_SIZE), 1)
    return (lane < HEAD_SIZE) if which == 0 else (lane >= HEAD_SIZE)


def normal_cdf(values):
    bell = jnp.exp2(values * values * (-0.5 * log_two_e))
    t = 1.0 / (1.0 + jnp.abs(values) * (0.3275911 * 0.7071067811865476))
    poly = 0.5 * 1.061405429 * t + 0.5 * -1.453152027
    poly = poly * t + 0.5 * 1.421413741
    poly = poly * t + 0.5 * -0.284496736
    poly = poly * t + 0.5 * 0.254829592
    tail = poly * t * bell
    return jnp.where(values >= 0, 1.0 - tail, tail), bell


def norm(values):
    centred = values - jnp.mean(values, axis=-1, keepdims=True)
    spread = jnp.mean(centred * centred, axis=-1, keepdims=True)
    scale = lax.rsqrt(spread + epsilon)
    return centred * scale, scale


def norm_back(grad, hat, scale, gain):
    lifted = grad * gain
    mean_one = jnp.mean(lifted, axis=-1, keepdims=True)
    mean_two = jnp.mean(lifted * hat, axis=-1, keepdims=True)
    return scale * (lifted - mean_one - hat * mean_two)


def room(items, more):
    total = more * MIB
    for item in items:
        *lead, rows, lanes = (1,) + tuple(item.shape)
        size = (rows + 15) // 16 * 16 * ((lanes + 127) // 128 * 128)
        total += int(np.prod(lead)) * size * jnp.dtype(item.dtype).itemsize
    return min(total, 62 * MIB)


def run(kernel, name, micros, ins, outs, scratch=(), more=10):
    return pl.pallas_call(
        kernel,
        out_shape=outs,
        in_specs=[VMEM] * len(ins),
        out_specs=(VMEM,) * len(outs),
        scratch_shapes=[pltpu.VMEM(item.shape, item.dtype) for item in scratch],
        compiler_params=pltpu.CompilerParams(vmem_limit_bytes=room(scratch, more)),
        cost_estimate=cost(micros),
        name=name,
    )(*ins)


def back_shapes(rows):
    seq = rows // PIECES
    return (shape((seq, D), bf16),) * 2 + (shape((2, seq, D), bf16),)


def put_pieces(values, targets):
    seq = values.shape[0] // 2
    for item in (0, 1):
        target = targets[item] if len(targets) == 2 else targets[0].at[item]
        target[...] = values[item * seq : (item + 1) * seq, :]


def sums(values):
    return jnp.sum(values, axis=0, keepdims=True)


def place_bits():
    blk = lax.axis_index("blk")
    coarse = lax.axis_index("dp") // (lax.axis_size("dp") // 8)
    return blk % 2, blk // 2, coarse % 2, (coarse // 2) % 2, coarse // 4


def unpack_flags(codes):
    replaced = (codes >= 4).astype(f32)
    codes = codes - 4 * replaced
    masked = (codes >= 2).astype(f32)
    pad = codes - 2 * masked
    lane = lax.broadcasted_iota(jnp.int32, (codes.shape[0], 16), 1)
    return jnp.where(lane == 0, pad, jnp.where(lane == 1, masked, replaced))


def forward_kernel(*refs):
    vectors, refs = refs[:11], refs[11:]
    pieces, refs = refs[:PIECES], refs[PIECES:]
    w_query, w_key, w_value, w_out, w_up, w_down, *refs = refs
    made, refs = refs[:18], refs[18:]
    start, value_t, context_t, dropped = refs
    (
        entries,
        queries,
        keyed,
        valued,
        context,
        key_bias,
        stats,
        hat_one,
        scale_one,
        normed_low,
        active,
        slope,
        hat_two,
        scale_two,
        flags_out,
        *hidden_out,
    ) = made
    (
        mask_vector,
        replace_vector,
        b_query,
        b_value,
        b_out,
        gain_one,
        shift_one,
        b_down,
        gain_two,
        shift_two,
        b_up,
    ) = (vector[...].reshape(1, -1) for vector in vectors)
    seq = pieces[0].shape[0] - 16
    rows = PIECES * seq
    row_id = lax.broadcasted_iota(jnp.int32, (seq, seq), 0)
    col_id = lax.broadcasted_iota(jnp.int32, (seq, seq), 1)
    eye = (row_id == col_id).astype(bf16)
    for index, piece in enumerate(pieces):
        where = pl.ds(index * seq, seq)
        columns = dot_right_t(eye, piece[seq : seq + 16, 0:seq])
        columns = unpack_flags(columns[:, 0:1])
        flags_out[where, :] = columns
        key_bias[where, :] = jnp.where(
            lax.broadcasted_iota(jnp.int32, (seq, 128), 1) == 0,
            (1.0 - columns[:, 0:1]) * left_out,
            0.0,
        ).astype(bf16)
        rows_here = jnp.where(
            columns[:, 1:2] > 0, mask_vector, piece[0:seq, :].astype(f32)
        )
        rows_here = rows_here + columns[:, 2:3] * replace_vector
        start[where, :] = rows_here
        entries[where, :] = rows_here.astype(bf16)
    queries[...] = ((dot(entries[...], w_query[...]) + b_query) * query_scale).astype(bf16)
    keyed[...] = dot(entries[...], w_key[...]).astype(bf16)
    valued[...] = (dot(entries[...], w_value[...]) + b_value).astype(bf16)
    value_t[...] = valued[...].T

    ones_lane = (lax.broadcasted_iota(jnp.int32, (rows, 128), 1) == 0).astype(bf16)
    ones_rows = jnp.ones((16, rows), bf16)

    def head_scores(pair, which):
        columns = pl.ds(pl.multiple_of(pair * 128, 128), 128)
        query_pair = jnp.concatenate([queries[:, columns], ones_lane], axis=1)
        key_pair = keyed[:, columns]
        key_head = jnp.where(lane_half(rows, which), key_pair, jnp.zeros_like(key_pair))
        key_head = jnp.concatenate([key_head, key_bias[...]], axis=1)
        return dot_right_t(key_head, query_pair)

    together = 2

    def group_step(group, carry):
        first = group * together
        following = head_scores(first, 0)
        for index in range(2 * together):
            scores = following
            if index + 1 < 2 * together:
                following = head_scores(first + (index + 1) // 2, (index + 1) % 2)
            peak = jnp.max(scores, axis=0, keepdims=True)
            weights = jnp.exp2(scores - peak).astype(bf16)
            head = first * 2 + index
            head_rows = pl.ds(pl.multiple_of(head * HEAD_SIZE, HEAD_SIZE), HEAD_SIZE)
            values = jnp.concatenate([value_t[head_rows, :], ones_rows], axis=0)
            summed = dot(values, weights)
            total = summed[HEAD_SIZE : HEAD_SIZE + 1, :]
            context_t[head_rows, :] = (summed[:HEAD_SIZE, :] * (1.0 / total)).astype(bf16)
            stats[pl.ds(head, 1), :] = peak + jnp.log2(total)
        return carry

    stats[pl.ds(8, 8), :] = jnp.zeros((8, rows), f32)
    lax.fori_loop(0, HEADS // 2 // together, group_step, 0)
    context[...] = context_t[...].T
    half = rows // 2
    for index in range(2):
        where = pl.ds(index * half, half)
        branch = dot(context[where, :], w_out[...]) + b_out
        hat, scale = norm(start[where, :] + branch)
        hat_one[where, :] = hat
        scale_one[where, :] = scale
        normed_low[where, :] = (hat * gain_one + shift_one).astype(bf16)
    chunk = 256
    count = FF // chunk

    def lift(index):
        columns = slice(index * chunk, (index + 1) * chunk)
        return dot(normed_low[...], w_up[:, columns]) + b_up[:, columns]

    following = lift(0)
    for index in range(count):
        lifted = following
        if index + 1 < count:
            following = lift(index + 1)
        columns = pl.ds(index * chunk, chunk)
        cdf, bell = normal_cdf(lifted)
        act = (lifted * cdf).astype(bf16)
        active[:, columns] = act
        slope[:, columns] = (cdf + lifted * bell * 0.3989422804014327).astype(bf16)
        part = dot(act, w_down[columns, :])
        if index == 0:
            dropped[...] = part
        else:
            dropped[...] += part
    for index in range(2):
        where = pl.ds(index * half, half)
        normed = hat_one[where, :] * gain_one + shift_one
        hat, scale = norm(normed + dropped[where, :] + b_down)
        hat_two[where, :] = hat
        scale_two[where, :] = scale
        low = (hat * gain_two + shift_two).astype(bf16)
        put_pieces(low, hidden_out[index * 2 : index * 2 + 2])


def forward(pieces, vectors, *weights):
    rows = PIECES * (pieces[0].shape[0] - 16)
    ins = tuple(vectors) + tuple(pieces) + weights
    outs = (
        shape((rows, D), bf16),
        shape((rows, D), bf16),
        shape((rows, D), bf16),
        shape((rows, D), bf16),
        shape((rows, D), bf16),
        shape((rows, 128), bf16),
        shape((16, rows), f32),
        shape((rows, D), f32),
        shape((rows, 1), f32),
        shape((rows, D), bf16),
        shape((rows, FF), bf16),
        shape((rows, FF), bf16),
        shape((rows, D), f32),
        shape((rows, 1), f32),
        shape((rows, 16), f32),
    ) + back_shapes(rows)
    more = (
        shape((rows, D), f32),
        shape((D, rows), bf16),
        shape((D, rows), bf16),
        shape((rows, D), f32),
    )
    return run(forward_kernel, "forward_layer", 22, ins, outs, more)


LANES = 384
ROWS_DOWN = 192
ROWS_UP = 240
ROWS_PAIR = 144
PAIRS_FIRST = 2


PARTS_DOWN = (192,)
PARTS_UP = (80, 80, 80)
PARTS_PAIR = (80, 64)
WAYS_PAIR = (80, 64)


def tiles(parts):
    return tuple(shape((2, 8, rows, LANES), bf16) for rows in parts)


def put(parts, y, dp, first, value):
    low = 0
    for part in parts:
        high = low + part.shape[2]
        start, stop = max(first, low), min(first + value.shape[0], high)
        if start < stop:
            part[y, dp, start - low : stop - low] = value[start - first : stop - first]
        low = high


def halves_t(values, target):
    rows = values.shape[0]
    turned = values.T
    for dp in range(8):
        for half in range(2):
            low = dp * 96 + half * 48
            target[dp * 48 : dp * 48 + 48, half * rows : (half + 1) * rows] = turned[
                low : low + 48, :
            ]


def halves_wide(values, target):
    rows = values.shape[0]
    block = D // PIECES
    nothing = jnp.zeros((rows, block), bf16)
    for index in range(PIECES):
        piece = values[:, index * block : (index + 1) * block]
        wide = slice(index * LANES, (index + 1) * LANES)
        target[0:rows, wide] = jnp.concatenate([piece, nothing], axis=1)
        target[rows : 2 * rows, wide] = jnp.concatenate([nothing, piece], axis=1)


def down_tiles(left_side, active, target):
    block = D // PIECES
    for pair in range(4):
        part = dot(left_side, active[:, pl.ds(pair * D, D)]).astype(bf16)
        for dp in range(2):
            columns = slice(dp * LANES, dp * LANES + LANES)
            for y in range(2):
                put(target, y, pair * 2 + dp, 0, part[y * block : (y + 1) * block, columns])


def down_kernel(*refs):
    gain, refs = refs[0], refs[1:]
    pieces, (hat_two, scale_two, active, *refs) = refs[:PIECES], refs[PIECES:]
    count = len(PARTS_DOWN)
    grad_z_two, grad_dropped, vectors, left_kept, *refs = refs
    sent, (grad_t,) = refs[:count], refs[count:]
    gain_two = gain[...].reshape(1, D)
    seq = pieces[0].shape[0]
    core = place_bits()[0]
    totals = [jnp.zeros((1, D), f32)] * 3
    for index, piece in enumerate(pieces):
        where = pl.ds(index * seq, seq)
        grad = piece[...].astype(f32)
        hat = hat_two[where, :]
        grad_z = norm_back(grad, hat, scale_two[where, :], gain_two)
        low = grad_z.astype(bf16)
        grad_z_two[where, :] = grad_z
        grad_dropped[where, :] = low
        terms = (grad * hat, grad, low.astype(f32))
        totals = [total + sums(term) for total, term in zip(totals, terms)]
    vectors[...] = jnp.concatenate(totals + [jnp.zeros((5, D), f32)], axis=0)
    block = D // PIECES
    grad_t[...] = grad_dropped[...].T

    def rows_of(order):
        return jnp.concatenate(
            [grad_t[pl.ds(pl.multiple_of(index * block, block), block), :] for index in order],
            axis=0,
        )

    left_kept[...] = rows_of([core, 2 + core])
    down_tiles(rows_of([1 - core, 3 - core]), active, sent)


def down_back(pieces, hat_two, scale_two, active, gain_two):
    rows = PIECES * pieces[0].shape[0]
    ins = (gain_two,) + tuple(pieces) + (hat_two, scale_two, active)
    outs = (
        shape((rows, D), f32),
        shape((rows, D), bf16),
        shape((8, D), f32),
        shape((D // 2, rows), bf16),
        *tiles(PARTS_DOWN),
    )
    more = (shape((D, rows), bf16),)
    return run(down_kernel, "down_back", 7, ins, outs, more)


def lifted_kernel(grad_dropped, w_down, slope, left_kept, active, grad_lifted, grad_b_up, kept):
    block = FF // PIECES
    for index in range(PIECES):
        columns = pl.ds(index * block, block)
        grad = dot_right_t(grad_dropped[...], w_down[columns, :])
        grad = (grad * slope[:, columns].astype(f32)).astype(bf16)
        grad_lifted[:, columns] = grad
        grad_b_up[:, columns] = sums(grad.astype(f32))
    down_tiles(left_kept[...], active, (kept,))


def lifted_back(grad_dropped, w_down, slope, left_kept, active):
    rows = grad_dropped.shape[0]
    ins = (grad_dropped, w_down, slope, left_kept, active)
    outs = (shape((rows, FF), bf16), shape((1, FF), f32), *tiles((ROWS_DOWN,)))
    return run(lifted_kernel, "lifted_back", 5, ins, outs)


def up_tiles(order, normed_t, grad_lifted, context_t, wide, target):
    block = FF // PIECES
    for y, which in enumerate(order):
        columns = pl.ds(pl.multiple_of(which * block, block), block)
        part = dot(normed_t[...], grad_lifted[:, columns]).astype(bf16)
        columns = pl.ds(pl.multiple_of(which * LANES, LANES), LANES)
        extra = dot(context_t[...], wide[:, columns]).astype(bf16)
        for dp in range(8):
            put(target, y, dp, 0, part[dp * 96 : dp * 96 + 96, 0:LANES])
            put(target, y, dp, 96, extra[dp * 48 : dp * 48 + 48, :])
            put(target, y, dp, 144, part[dp * 96 : dp * 96 + 96, LANES:])


def middle_kernel(gain, *refs):
    grad_lifted, w_up, grad_z_two, hat_one, scale_one, context, normed_low, *refs = refs
    grad_z_one, vectors, grad_branch, normed_t, context_t, wide, *sent = refs
    core = place_bits()[0]
    rows = grad_z_two.shape[0]
    half = rows // 2
    gain_one = gain[...].reshape(1, D)
    totals = [jnp.zeros((1, D), f32)] * 3
    normed_t[...] = normed_low[...].T
    halves_t(context[...], context_t)
    for index in range(2):
        where = pl.ds(index * half, half)
        grad = grad_z_two[where, :] + dot_right_t(grad_lifted[where, :], w_up[...])
        hat = hat_one[where, :]
        grad_z = norm_back(grad, hat, scale_one[where, :], gain_one)
        low = grad_z.astype(bf16)
        grad_z_one[where, :] = grad_z
        grad_branch[where, :] = low
        terms = (grad * hat, grad, low.astype(f32))
        totals = [total + sums(term) for total, term in zip(totals, terms)]
    vectors[...] = jnp.concatenate(totals + [jnp.zeros((5, D), f32)], axis=0)
    halves_wide(grad_branch[...], wide)
    up_tiles([1 - core, 3 - core], normed_t, grad_lifted, context_t, wide, sent)


def middle_back(*ins):
    rows = ins[1].shape[0]
    outs = (
        shape((rows, D), f32),
        shape((8, D), f32),
        shape((rows, D), bf16),
        shape((D, rows), bf16),
        shape((D // 2, 2 * rows), bf16),
        shape((2 * rows, 2 * D), bf16),
        *tiles(PARTS_UP),
    )
    return run(middle_kernel, "middle_up_back", 10, ins, outs)


def attention_steps(first, pairs, inside, grads, base=0):
    queries, keyed, valued, key_bias, stats, grad_attended, delta = inside
    grad_q, grad_k, grad_v = grads
    rows = queries.shape[0]
    ones_lane = (lax.broadcasted_iota(jnp.int32, (rows, 128), 1) == 0).astype(bf16)
    low = lane_half(rows, 0)
    nothing = jnp.zeros((rows, 128), bf16)

    def products(head):
        pair, which = head // 2, head % 2
        columns = pl.ds(pair * 128, 128)
        own = lane_half(rows, which)
        query_wide = jnp.concatenate([queries[:, columns], ones_lane], axis=1)
        key_head = jnp.where(own, keyed[:, columns], nothing)
        key_head = jnp.concatenate([key_head, key_bias[...]], axis=1)
        value_head = jnp.where(own, valued[:, columns], nothing)
        return (
            dot_right_t(key_head, query_wide),
            dot_right_t(value_head, grad_attended[:, columns]),
        )

    following = products(2 * first)
    for index in range(pairs):
        pair = first + index
        columns = pl.ds(pair * 128, 128)
        target = pl.ds(base + index * 128, 128)
        query_pair = queries[:, columns]
        key_pair_t = keyed[:, columns].T
        grad_pair = grad_attended[:, columns]
        found = []
        for which in range(2):
            head = 2 * pair + which
            scores, grad_weights = following
            if head + 1 < 2 * (first + pairs):
                following = products(head + 1)
            here = pl.ds(head, 1)
            weights = jnp.exp2(scores - stats[here, :])
            grad_raw = (weights * (grad_weights - delta[here, :])).astype(bf16)
            grad_v_pair = dot(weights.astype(bf16), grad_pair)
            grad_k_pair = dot(grad_raw, query_pair)
            head_rows = slice(which * HEAD_SIZE, which * HEAD_SIZE + HEAD_SIZE)
            grad_q_t = dot(key_pair_t[head_rows, :], grad_raw)
            found.append((grad_q_t, grad_k_pair, grad_v_pair))
        grad_q_t = jnp.concatenate([found[0][0], found[1][0]], axis=0) * HEAD_SIZE ** (-0.5)
        grad_q[:, target] = grad_q_t.T.astype(bf16)
        grad_k_pair = jnp.where(low, found[0][1], found[1][1]) * (1.0 / log_two_e)
        grad_k[:, target] = grad_k_pair.astype(bf16)
        grad_v[:, target] = jnp.where(low, found[0][2], found[1][2]).astype(bf16)


def attention_kernel(first, pairs, *refs):
    inside, refs = refs[:5], refs[5:]
    grad_branch, w_out, context, normed_t, grad_lifted, context_t, wide, *refs = refs
    grad_attended, delta, *grads, kept = refs
    rows = grad_branch.shape[0]
    half = rows // 2
    core = place_bits()[0]
    head = lax.broadcasted_iota(jnp.int32, (16, D), 0)
    feature = lax.broadcasted_iota(jnp.int32, (16, D), 1)
    heads = (feature // HEAD_SIZE == head).astype(bf16)
    for index in range(2):
        where = pl.ds(index * half, half)
        attended = dot_right_t(grad_branch[where, :], w_out[...])
        grad_attended[where, :] = attended.astype(bf16)
        products = attended * context[where, :].astype(f32)
        high = products.astype(bf16)
        rest = (products - high.astype(f32)).astype(bf16)
        delta[:, where] = dot_right_t(heads, high) + dot_right_t(heads, rest)
    attention_steps(first, pairs, (*inside, grad_attended, delta), grads)
    up_tiles([core, 2 + core], normed_t, grad_lifted, context_t, wide, (kept,))


def attention_back(first, pairs, *ins):
    rows = ins[0].shape[0]
    outs = (shape((rows, D), bf16), shape((16, rows), f32))
    outs += (shape((rows, pairs * 128), bf16),) * 3 + tiles((ROWS_UP,))
    kernel = functools.partial(attention_kernel, first, pairs)
    return run(kernel, "attention_back", 0, ins, outs)


def weights_kernel(first, pairs, *refs):
    inside, (entries, *before), refs = refs[:7], refs[7:11], refs[11:]
    merged, (vectors, kept, *refs) = refs[:3], refs[3:]
    sent, refs = refs[: len(PARTS_PAIR)], refs[len(PARTS_PAIR) :]
    entries_t, entries_half, wide_qk, wide_v = refs
    core = place_bits()[0]
    for part, target in zip(before, merged):
        target[:, 0 : first * 128] = part[...]
    attention_steps(first, pairs, inside, merged, first * 128)
    turned = entries[...]
    entries_t[...] = turned.T
    halves_t(turned, entries_half)
    block = D // PIECES
    grad_q, grad_k, grad_v = merged
    for index in range(PIECES):
        piece = slice(index * block, (index + 1) * block)
        wide = slice(index * LANES, (index + 1) * LANES)
        wide_qk[:, wide] = jnp.concatenate([grad_q[:, piece], grad_k[:, piece]], axis=1)
    halves_wide(grad_v[...], wide_v)
    for index, which in enumerate([1 - core, 3 - core, core, 2 + core]):
        columns = pl.ds(pl.multiple_of(which * LANES, LANES), LANES)
        part = dot(entries_t[...], wide_qk[:, columns]).astype(bf16)
        extra = dot(entries_half[...], wide_v[:, columns]).astype(bf16)
        target = (sent, (kept,))[index // 2]
        y = index % 2
        for dp in range(8):
            put(target, y, dp, 0, part[dp * 96 : dp * 96 + 96, :])
            put(target, y, dp, 96, extra[dp * 48 : dp * 48 + 48, :])
    vectors[0:1, :] = sums(grad_q[...].astype(f32))
    vectors[1:2, :] = sums(grad_v[...].astype(f32))


def weights_back(first, pairs, *ins):
    rows = ins[0].shape[0]
    whole = shape((rows, D), bf16)
    outs = (whole,) * 3 + (shape((2, D), f32), *tiles((ROWS_PAIR,)), *tiles(PARTS_PAIR))
    more = (
        shape((D, rows), bf16),
        shape((D // 2, 2 * rows), bf16),
        shape((rows, 2 * D), bf16),
        shape((2 * rows, 2 * D), bf16),
    )
    kernel = functools.partial(weights_kernel, first, pairs)
    return run(kernel, "attention_weights_back", 2.2 * pairs + 4, ins, outs, more)


def start_kernel(*refs):
    w_query, w_key, w_value, grad_z_one, flags, two, one, b_up, late = refs[:9]
    grads, made = refs[9:12], refs[12:]
    *grad_in, vectors = made
    seq = grad_z_one.shape[0] // PIECES
    half = D // 2
    totals = [jnp.zeros((1, D), f32)] * 2
    for step in range(2):
        where = pl.ds(step * 2 * seq, 2 * seq)
        grad = grad_z_one[where, :]
        for value, weight in zip(grads, (w_query, w_key, w_value)):
            grad = grad + dot_right_t(value[where, :], weight[...])
        masked = flags[where, 1:2]
        replaced = flags[where, 2:3]
        terms = (grad * masked, grad * replaced)
        totals = [total + sums(term) for total, term in zip(totals, terms)]
        low = jnp.where(masked > 0, 0.0, grad).astype(bf16)
        put_pieces(low, grad_in[step * 2 : step * 2 + 2])
    rows = totals + [late[...], two[0:3, :], one[0:3, :]]
    rows += [b_up[:, index * D : (index + 1) * D] for index in range(FF // D)]
    rows = jnp.concatenate(rows + [jnp.zeros((2, D), f32)], axis=0)
    vectors[0:16, :] = rows[:, :half]
    vectors[16:32, :] = rows[:, half:]


def start_back(weights, grad_z_one, flags, vectors, grads):
    rows = grad_z_one.shape[0]
    ins = tuple(weights) + (grad_z_one, flags) + tuple(vectors) + tuple(grads)
    outs = (shape((rows // PIECES, D), bf16),) * PIECES + (shape((32, LANES), f32),)
    return run(start_kernel, "start_back", 0, ins, outs)


def swap(value, axis, bit):
    size = lax.axis_size(axis)
    return lax.ppermute(value, axis, [(i, i ^ bit) for i in range(size)])


def swap_turned(value, first):
    blks = lax.axis_size("blk")
    fine = lax.axis_size("dp") // 8
    pairs = []
    for dp in range(lax.axis_size("dp")):
        for blk in range(blks):
            along_dp = (blk % 2 == 0) == first
            other = (dp ^ fine) * blks + blk if along_dp else dp * blks + (blk ^ 2)
            pairs.append((dp * blks + blk, other))
    return lax.ppermute(value, ("dp", "blk"), pairs)


def swap_line(value, first):
    blks = lax.axis_size("blk")
    fine = lax.axis_size("dp") // 8
    pairs = []
    for dp in range(lax.axis_size("dp")):
        for blk in range(blks):
            near = (blk % 2 == 0) == first
            bits = 2 if near else (6 if first else 4)
            pairs.append((dp * blks + blk, (dp ^ (bits * fine)) * blks + blk))
    return lax.ppermute(value, ("dp", "blk"), pairs)


def tie(value, *others):
    return lax.optimization_barrier((value,) + tuple(others))[0]


def spread_kernel(hidden, flags, *out):
    blk = lax.axis_index("blk")
    seq = hidden.shape[1]
    for step in range(PIECES):
        document = blk ^ step
        out[step][0:seq, :] = hidden[document]
        row = flags[pl.ds(document, 1), :]
        out[step][seq : seq + 16, 0:seq] = jnp.concatenate(
            [row, jnp.zeros((15, seq), f32)], axis=0
        ).astype(bf16)
        out[step][seq : seq + 16, seq:] = jnp.zeros((16, hidden.shape[2] - seq), bf16)


def spread(hidden, flags):
    documents, seq, width = hidden.shape
    outs = (shape((seq + 16, width), bf16),) * PIECES
    return run(spread_kernel, "spread_documents", 1, (hidden, flags), outs, (), 2)


def spread_plain_kernel(hidden, *out):
    blk = lax.axis_index("blk")
    for step in range(PIECES):
        out[step][...] = hidden[blk ^ step]


def spread_plain(hidden):
    outs = (shape(hidden.shape[1:], bf16),) * PIECES
    return run(spread_plain_kernel, "spread_grads", 1, (hidden,), outs, (), 2)


def move_pieces(pieces):
    own, *others = pieces
    return [own] + [swap(piece, "blk", step + 1) for step, piece in enumerate(others)]


def collect_kernel(own, near, far, both, out):
    blk = lax.axis_index("blk")
    out[blk] = own[...]
    out[blk ^ 1] = near[...]
    out[blk ^ 2] = far[0]
    out[blk ^ 3] = both[1]


def collect_direct_kernel(*refs):
    blk = lax.axis_index("blk")
    for step in range(PIECES):
        refs[PIECES][blk ^ step] = refs[step][...]


def gather_direct(pieces, late):
    pieces = lax.optimization_barrier((*pieces, *late))[:PIECES]
    back = [swap(pieces[step], "blk", step) for step in range(2, PIECES)]
    late = yield
    back = [swap(tie(pieces[1], *late), "blk", 1)] + back
    late = yield late
    ins = (pieces[0], *(tie(piece, *late) for piece in back))
    outs = (shape((PIECES,) + pieces[0].shape, bf16),)
    yield run(collect_direct_kernel, "collect_documents", 0, ins, outs, (), 2)[0]


def gather_documents(own, near, far):
    late = yield
    near = tie(swap(near, "blk", 1), *late)
    far = tie(swap(far, "blk", 2), *late)
    late = yield (near, far)
    both = tie(swap(far, "blk", 1), *late)
    ins = (own, near, far, both)
    outs = (shape((PIECES,) + own.shape, bf16),)
    yield run(collect_kernel, "collect_documents", 0, ins, outs, (), 2)


def split_vectors(values):
    high = values.astype(bf16)
    return high, (values - high.astype(f32)).astype(bf16)


def sum_kernel(plan, emit, split_in, split_out, wide, n_vectors, *refs):
    kept, *arrived = refs[: 1 + len(split_in)]
    vectors_in = refs[1 + len(split_in) : 1 + len(split_in) + n_vectors]
    made = refs[1 + len(split_in) + n_vectors :]
    rows = sum(split_in)

    def take(source, place, height):
        if isinstance(place, tuple):
            return source[place].astype(f32)
        where = pl.ds(pl.multiple_of(place * height, 16), height)
        return source[where, :].astype(f32)

    plans = plan(*place_bits())
    targets = (made[: len(split_out)], made[len(split_out) : len(split_out) + 1])
    for group, splits, places in zip(targets, (split_out, (rows,)), plans):
        for item, place in enumerate(places):
            other = [take(part, place, height) for part, height in zip(arrived, split_in)]
            other = other[0] if len(other) == 1 else jnp.concatenate(other, axis=0)
            value = take(kept, place, rows) + other
            low = 0
            if emit is None:
                for target, height in zip(group, splits):
                    part = value[low : low + height].astype(bf16)
                    target[item * height : (item + 1) * height, :] = part
                    low += height
    if n_vectors:
        own, other = vectors_in
        if other.dtype == f32:
            vectors = own[...] + other[...]
        else:
            tail = 64 if other.shape[0] % split_in[-1] == 64 % split_in[-1] else 32
            start = other.shape[0] - tail
            vectors = own[...] + other[start : start + 32, :].astype(f32)
            if tail == 64:
                vectors = vectors + other[start + 32 : start + 64, :].astype(f32)
        if emit is None:
            high, low = split_vectors(vectors)
            target = targets[0][-1]
            start = target.shape[0] - (64 if wide else 32)
            target[start : start + 32, :] = high
            kept_vectors = high.astype(f32)
            if wide:
                target[start + 32 : start + 64, :] = low
                kept_vectors = kept_vectors + low.astype(f32)
            made[-1][...] = kept_vectors
        else:
            emit_vectors(vectors, made[len(made) - VECTORS :])
    if emit is not None:
        emit(value, made)


VECTORS = 11


def emit_vectors(vectors, made):
    half = D // 2
    for index, target in enumerate(made):
        for part in range(target.shape[0] // D):
            row = index + part
            target[part * D : part * D + half] = vectors[row : row + 1, :].reshape(half)
            target[part * D + half : part * D + D] = vectors[row + 16 : row + 17, :].reshape(half)


def sum_stage(
    name,
    kept,
    arrived,
    rows,
    plan,
    count,
    vectors=(),
    emit=None,
    outs=None,
    wide=True,
    split_in=None,
    split_out=None,
):
    split_in = split_in or (rows,)
    split_out = split_out or (rows,)
    if outs is None:
        heights = [count * height for height in split_out]
        if vectors:
            heights[-1] += 64 if wide else 32
        outs = tuple(shape((height, LANES), bf16) for height in heights)
        outs += (shape((count * rows, LANES), bf16),)
        if vectors:
            outs += (shape((32, LANES), f32),)
    elif vectors:
        outs = outs + (shape((D,), f32),) * (VECTORS - 1) + (shape((FF,), f32),)
    ins = (kept,) + tuple(arrived) + tuple(vectors)
    kernel = functools.partial(sum_kernel, plan, emit, split_in, split_out, wide, len(vectors))
    return run(kernel, name, 0, ins, outs, (), 4)


def plan_core(core, y, b0, b1, b2):
    def places(mine_x, mine_y):
        return [
            (core * mine_y + (1 - core) * u, i * 4 + j * 2 + core * u + (1 - core) * mine_x)
            for u in (0, 1)
            for i in (0, 1)
            for j in (0, 1)
        ]

    return places(1 - b0, 1 - y), places(b0, y)


def plan_first(core, y, b0, b1, b2):
    u = core * b0 + (1 - core) * y
    return [[v * 4 + item for item in range(4)] for v in (1 - u, u)]


def plan_second(core, y, b0, b1, b2):
    def places(low, high):
        return [core * (high * 2 + u) + (1 - core) * (u * 2 + low) for u in (0, 1)]

    return places(1 - b1, 1 - b2), places(b1, b2)


def plan_third(core, y, b0, b1, b2):
    u = core * b1 + (1 - core) * b2
    return [1 - u], [u]


def plan_last(core, y, b0, b1, b2):
    return ([0],)


def finish_tiles(sends, kept, rows, emit, outs, own=()):
    splits = WAYS_PAIR if len(sends) > 1 else (rows,)
    late = yield tuple(sends)
    got = [tie(swap_turned(send, False), *late) for send in sends]
    both = (own[0], got[-1]) if own else ()
    made = sum_stage(
        "sum_second",
        kept,
        got,
        rows,
        plan_second,
        2,
        both,
        split_in=splits,
        split_out=splits,
    )
    sends, (kept, *own) = made[: len(splits)], made[len(splits) :]
    late = yield tuple(sends)
    got = [tie(swap_line(send, True), *late) for send in sends]
    both = (own[0], got[-1]) if own else ()
    send, kept, *own = sum_stage(
        "sum_third", kept, got, rows, plan_third, 1, both, split_in=splits
    )
    late = yield (send,)
    got = tie(swap_line(send, False), *late)
    both = (own[0], got) if own else ()
    yield sum_stage("sum_last", kept, (got,), rows, plan_last, 1, both, emit, outs)


def reduce_tiles(sent, kept, splits, emit, outs):
    rows = sum(splits)
    late = yield tuple(sent)
    got = [tie(swap(part, "blk", 1), *late) for part in sent]
    send, kept = sum_stage("sum_core", kept[0], got, rows, plan_core, 8, split_in=splits)
    late = yield (send,)
    got = tie(swap_turned(send, True), *late)
    send, kept = sum_stage("sum_first", kept, (got,), rows, plan_first, 4)
    yield from finish_tiles((send,), kept, rows, emit, outs)


def reduce_pair(sent, kept, emit, outs):
    late = yield tuple(sent)
    both = (late[0], tie(swap(late[0], "blk", 1), *late))
    got = [tie(swap(part, "blk", 1), *late) for part in sent]
    *sends, kept, own = sum_stage(
        "sum_core",
        kept,
        got,
        ROWS_PAIR,
        plan_core,
        8,
        both,
        split_in=PARTS_PAIR,
        split_out=WAYS_PAIR,
    )
    late = yield tuple(sends)
    got = [tie(swap_turned(send, True), *late) for send in sends]
    both = (own, got[-1])
    *sends, kept, own = sum_stage(
        "sum_first",
        kept,
        got,
        ROWS_PAIR,
        plan_first,
        4,
        both,
        split_in=WAYS_PAIR,
        split_out=WAYS_PAIR,
    )
    yield from finish_tiles(sends, kept, ROWS_PAIR, emit, outs, (own,))


def emit_down(tile, made):
    made[0][...] = tile.T


def emit_up(tile, made):
    block = D // PIECES
    made[0][:, 0:LANES] = tile[0:96]
    made[0][:, LANES:] = tile[144:240]
    made[1][0:48, :] = tile[96:144, :block]
    made[1][48:96, :] = tile[96:144, block:]


def emit_pair(tile, made):
    block = D // PIECES
    made[0][...] = tile[0:96, :block]
    made[1][...] = tile[0:96, block:]
    made[2][0:48, :] = tile[96:144, :block]
    made[2][48:96, :] = tile[96:144, block:]


def finish_vectors(vectors):
    size = lax.axis_size("dp")
    fine = size // 8
    if fine == 1:
        return vectors
    groups = [[index * fine + item for item in range(fine)] for index in range(8)]
    return lax.psum(tuple(vectors), "dp", axis_index_groups=groups)


def finish(tile, axis):
    size = lax.axis_size("dp")
    fine = size // 8
    if fine == 1:
        return tile
    groups = [[index * fine + item for item in range(fine)] for index in range(8)]
    return lax.psum_scatter(
        tile, "dp", scatter_dimension=axis, axis_index_groups=groups, tiled=True
    )


def local(
    hidden_in,
    pad_mask,
    masked_flag,
    replaced_flag,
    mask_vector,
    replace_vector,
    w_query,
    b_query,
    w_key,
    w_value,
    b_value,
    w_out,
    b_out,
    gain_one,
    shift_one,
    w_up,
    b_up,
    w_down,
    b_down,
    gain_two,
    shift_two,
    out_grad,
):
    codes = (pad_mask + 2 * masked_flag + 4 * replaced_flag).astype(f32)
    spread_in = spread(hidden_in, codes)
    pieces = move_pieces(spread_in)
    grad_pieces = move_pieces(spread_plain(tie(out_grad, *spread_in)))
    vectors = (
        mask_vector,
        replace_vector,
        b_query,
        b_value,
        b_out,
        gain_one,
        shift_one,
        b_down,
        gain_two,
        shift_two,
        b_up,
    )
    (
        entries,
        queries,
        keyed,
        valued,
        context,
        key_bias,
        stats,
        hat_one,
        scale_one,
        normed_low,
        active,
        slope,
        hat_two,
        scale_two,
        flags,
        *hidden_out,
    ) = forward(pieces, vectors, w_query, w_key, w_value, w_out, w_up, w_down)
    grad_z_two, grad_dropped, vectors_two, left_kept, *sent = down_back(
        grad_pieces, hat_two, scale_two, active, gain_two
    )
    block = D // PIECES
    square = shape((D // 8, block), f32)
    outs = (shape((FF // 8, block), f32),)
    kept_down, kept_up = [], []
    down = reduce_tiles(sent, kept_down, PARTS_DOWN, emit_down, outs)
    ties = next(down)
    grad_lifted, grad_b_up, kept = lifted_back(
        tie(grad_dropped, *ties), w_down, slope, left_kept, active
    )
    kept_down.append(kept)
    ties = down.send((grad_b_up,))
    hidden_back = gather_documents(*hidden_out)
    next(hidden_back)
    grad_z_one, vectors_one, grad_branch, normed_t, context_t, wide, *sent = middle_back(
        gain_one,
        grad_lifted,
        w_up,
        tie(grad_z_two, *ties),
        hat_one,
        scale_one,
        context,
        normed_low,
    )
    ties = hidden_back.send((vectors_one,))
    sent = lax.optimization_barrier((*sent, *ties))[: len(sent)]
    outs = (shape((D // 8, D), f32), square)
    up = reduce_tiles(sent, kept_up, PARTS_UP, emit_up, outs)
    ties = next(up)
    attention = (queries, keyed, valued, key_bias, stats)
    grad_attended, delta, *grads, kept = attention_back(
        0,
        PAIRS_FIRST,
        *attention,
        tie(grad_branch, *ties),
        w_out,
        context,
        normed_t,
        grad_lifted,
        context_t,
        wide,
    )
    kept_up.append(kept)
    attention += (grad_attended,)
    ties = down.send((grads[0],))
    ties = up.send(ties)
    (hidden_out,) = hidden_back.send(ties)
    grad_q, grad_k, grad_v, vectors_qv, kept, *sent = weights_back(
        PAIRS_FIRST,
        HEADS // 2 - PAIRS_FIRST,
        *attention,
        tie(delta, hidden_out, *ties),
        entries,
        *grads,
    )
    ties = down.send((vectors_qv,))
    sent = lax.optimization_barrier((*sent, *ties))[: len(sent)]
    pair = reduce_pair(sent, kept, emit_pair, (square,) * 3)
    ties = next(pair)
    *grad_in, vectors = start_back(
        (w_query, w_key, w_value),
        tie(grad_z_one, *ties),
        flags,
        (vectors_two, vectors_one, grad_b_up, vectors_qv),
        (grad_q, grad_k, grad_v),
    )
    ties = down.send((vectors,))
    ties = up.send(ties)
    (grad_w_down,) = down.send(ties)
    ties = pair.send((vectors, grad_w_down))
    ties = up.send(ties)
    ties = pair.send(ties)
    ties = up.send(ties)
    ties = pair.send(ties)
    grad_back = gather_direct(grad_in, ties)
    next(grad_back)
    grad_w_up, grad_w_out = up.send(ties)
    ties = grad_back.send((grad_w_up,))
    ties = pair.send(ties)
    grad_in = grad_back.send(ties)
    grad_w_query, grad_w_key, grad_w_value, *vectors = pair.send((grad_in,))
    vectors = finish_vectors(vectors)
    return (
        hidden_out,
        grad_in,
        vectors[0],
        vectors[1],
        finish(grad_w_query, 0),
        vectors[2],
        finish(grad_w_key, 0),
        finish(grad_w_value, 0),
        vectors[3],
        finish(grad_w_out, 0),
        vectors[9],
        vectors[7],
        vectors[8],
        finish(grad_w_up, 0),
        vectors[10],
        finish(grad_w_down, 0),
        vectors[6],
        vectors[4],
        vectors[5],
    )


def solution(mesh):
    replicated = (P(),) * 17
    placed = (P("dp", "blk", None),) + (P("dp", "blk"),) * 3 + replicated
    placed = placed + (P("dp", "blk", None),)
    tiles = P("dp", "blk")
    rows = P("dp", "blk", None)
    return jax.shard_map(
        local,
        mesh=mesh,
        in_specs=placed,
        out_specs=(
            rows,
            rows,
            P(),
            P(),
            tiles,
            P(),
            tiles,
            tiles,
            P(),
            tiles,
            P(),
            P(),
            P(),
            tiles,
            P(),
            tiles,
            P(),
            P(),
            P(),
        ),
        check_vma=False,
    )
```

```python
import functools

import jax
import jax.numpy as jnp
import numpy as np
from jax import lax
from jax.experimental import pallas as pl
from jax.experimental.pallas import tpu as pltpu
from jax.sharding import PartitionSpec as P

D = 768
HEADS = 12
HEAD_SIZE = 64
FF = 3072
PIECES = 4
MIB = 1024 * 1024

epsilon = 1e-05
log_two_e = 1.4426950408889634
query_scale = HEAD_SIZE ** (-0.5) * log_two_e
left_out = -1e30

f32 = jnp.float32
bf16 = jnp.bfloat16

VMEM = pl.BlockSpec(memory_space=pltpu.VMEM)


def cost(micros):
    return pl.CostEstimate(flops=int(micros * 4e9), bytes_accessed=1024, transcendentals=0)


def shape(dims, dtype):
    return jax.ShapeDtypeStruct(dims, dtype)


def dot(left_side, right_side):
    return jnp.dot(left_side, right_side, preferred_element_type=f32)


def dot_right_t(left_side, right_side):
    return lax.dot_general(
        left_side, right_side, (((1,), (1,)), ((), ())), preferred_element_type=f32
    )


def lane_half(rows, which):
    lane = lax.broadcasted_iota(jnp.int32, (rows, 2 * HEAD_SIZE), 1)
    return (lane < HEAD_SIZE) if which == 0 else (lane >= HEAD_SIZE)


def normal_cdf(values):
    bell = jnp.exp2(values * values * (-0.5 * log_two_e))
    t = 1.0 / (1.0 + jnp.abs(values) * (0.3275911 * 0.7071067811865476))
    poly = 0.5 * 1.061405429 * t + 0.5 * -1.453152027
    poly = poly * t + 0.5 * 1.421413741
    poly = poly * t + 0.5 * -0.284496736
    poly = poly * t + 0.5 * 0.254829592
    tail = poly * t * bell
    return jnp.where(values >= 0, 1.0 - tail, tail), bell


def norm(values):
    centred = values - jnp.mean(values, axis=-1, keepdims=True)
    spread = jnp.mean(centred * centred, axis=-1, keepdims=True)
    scale = lax.rsqrt(spread + epsilon)
    return centred * scale, scale


def norm_back(grad, hat, scale, gain):
    lifted = grad * gain
    mean_one = jnp.mean(lifted, axis=-1, keepdims=True)
    mean_two = jnp.mean(lifted * hat, axis=-1, keepdims=True)
    return scale * (lifted - mean_one - hat * mean_two)


def room(items, more):
    total = more * MIB
    for item in items:
        *lead, rows, lanes = (1,) + tuple(item.shape)
        size = (rows + 15) // 16 * 16 * ((lanes + 127) // 128 * 128)
        total += int(np.prod(lead)) * size * jnp.dtype(item.dtype).itemsize
    return min(total, 62 * MIB)


def run(kernel, name, micros, ins, outs, scratch=(), more=10, aliases=None):
    return pl.pallas_call(
        kernel,
        out_shape=outs,
        in_specs=[VMEM] * len(ins),
        out_specs=(VMEM,) * len(outs),
        scratch_shapes=[pltpu.VMEM(item.shape, item.dtype) for item in scratch],
        compiler_params=pltpu.CompilerParams(vmem_limit_bytes=room(scratch, more)),
        cost_estimate=cost(micros),
        input_output_aliases=aliases or {},
        name=name,
    )(*ins)


def back_shapes(rows):
    seq = rows // PIECES
    return (shape((seq, D), bf16),) * 2 + (shape((2, seq, D), bf16),)


def put_pieces(values, targets):
    seq = values.shape[0] // 2
    for item in (0, 1):
        target = targets[item] if len(targets) == 2 else targets[0].at[item]
        target[...] = values[item * seq : (item + 1) * seq, :]


def sums(values):
    return jnp.sum(values, axis=0, keepdims=True)


def place_bits():
    blk = lax.axis_index("blk")
    coarse = lax.axis_index("dp") // (lax.axis_size("dp") // 8)
    return blk % 2, blk // 2, coarse % 2, (coarse // 2) % 2, coarse // 4


def unpack_flags(codes):
    replaced = (codes >= 4).astype(f32)
    codes = codes - 4 * replaced
    masked = (codes >= 2).astype(f32)
    pad = codes - 2 * masked
    lane = lax.broadcasted_iota(jnp.int32, (codes.shape[0], 16), 1)
    return jnp.where(lane == 0, pad, jnp.where(lane == 1, masked, replaced))


def project(pieces, vectors, weights, made, low):
    mask_vector, replace_vector, b_query, b_value = (item[...].reshape(1, D) for item in vectors)
    w_query, w_key, w_value = weights
    start, entries, queries, keyed, valued, key_bias, flags_out = made
    seq = pieces[0].shape[0] - 16
    row_id = lax.broadcasted_iota(jnp.int32, (seq, seq), 0)
    col_id = lax.broadcasted_iota(jnp.int32, (seq, seq), 1)
    eye = (row_id == col_id).astype(bf16)
    for index, piece in enumerate(pieces):
        where = pl.ds(low + index * seq, seq)
        columns = dot_right_t(eye, piece[seq : seq + 16, 0:seq])
        columns = unpack_flags(columns[:, 0:1])
        flags_out[where, :] = columns
        key_bias[where, :] = jnp.where(
            lax.broadcasted_iota(jnp.int32, (seq, 128), 1) == 0,
            (1.0 - columns[:, 0:1]) * left_out,
            0.0,
        ).astype(bf16)
        rows_here = jnp.where(columns[:, 1:2] > 0, mask_vector, piece[0:seq, :].astype(f32))
        rows_here = rows_here + columns[:, 2:3] * replace_vector
        start[where, :] = rows_here
        entries[where, :] = rows_here.astype(bf16)
    where = pl.ds(low, len(pieces) * seq)
    rows = entries[where, :]
    queries[where, :] = ((dot(rows, w_query[...]) + b_query) * query_scale).astype(bf16)
    keyed[where, :] = dot(rows, w_key[...]).astype(bf16)
    valued[where, :] = (dot(rows, w_value[...]) + b_value).astype(bf16)


EARLY = 3


def early_kernel(*refs):
    vectors, refs = refs[:4], refs[4:]
    pieces, weights, made = refs[:EARLY], refs[EARLY : EARLY + 3], refs[EARLY + 3 :]
    project(pieces, vectors, weights, made, 0)


def early(pieces, vectors, weights):
    rows = PIECES * (pieces[0].shape[0] - 16)
    whole = shape((rows, D), bf16)
    outs = (shape((rows, D), f32), whole, whole, whole, whole)
    outs += (shape((rows, 128), bf16), shape((rows, 16), f32))
    ins = (*vectors, *pieces, *weights)
    return run(early_kernel, "project_early", 3, ins, outs)


def forward_kernel(*refs):
    vectors, refs = refs[:11], refs[11:]
    before, (piece, *refs) = refs[:7], refs[7:]
    w_query, w_key, w_value, w_out, w_up, w_down, *refs = refs
    made, refs = refs[:18], refs[18:]
    value_t, context_t, dropped = refs
    (
        entries,
        queries,
        keyed,
        valued,
        context,
        key_bias,
        stats,
        hat_one,
        scale_one,
        normed_low,
        active,
        slope,
        hat_two,
        scale_two,
        flags_out,
        *hidden_out,
    ) = made
    (
        mask_vector,
        replace_vector,
        b_query,
        b_value,
        b_out,
        gain_one,
        shift_one,
        b_down,
        gain_two,
        shift_two,
        b_up,
    ) = (vector[...].reshape(1, -1) for vector in vectors)
    seq = piece.shape[0] - 16
    rows = PIECES * seq
    ready = EARLY * seq
    start = hat_one
    here = (start, entries, queries, keyed, valued, key_bias, flags_out)
    for source, target in zip(before, here):
        target[0:ready, :] = source[0:ready, :]
    project((piece,), vectors[:4], (w_query, w_key, w_value), here, ready)
    value_t[...] = valued[...].T
    ones_lane = (lax.broadcasted_iota(jnp.int32, (rows, 128), 1) == 0).astype(bf16)
    ones_rows = jnp.ones((16, rows), bf16)

    def head_scores(pair, which):
        columns = pl.ds(pl.multiple_of(pair * 128, 128), 128)
        query_pair = jnp.concatenate([queries[:, columns], ones_lane], axis=1)
        key_pair = keyed[:, columns]
        key_head = jnp.where(lane_half(rows, which), key_pair, jnp.zeros_like(key_pair))
        key_head = jnp.concatenate([key_head, key_bias[...]], axis=1)
        return dot_right_t(key_head, query_pair)

    together = 2

    def group_step(group, carry):
        first = group * together
        following = head_scores(first, 0)
        for index in range(2 * together):
            scores = following
            if index + 1 < 2 * together:
                following = head_scores(first + (index + 1) // 2, (index + 1) % 2)
            peak = jnp.max(scores, axis=0, keepdims=True)
            weights = jnp.exp2(scores - peak).astype(bf16)
            head = first * 2 + index
            head_rows = pl.ds(pl.multiple_of(head * HEAD_SIZE, HEAD_SIZE), HEAD_SIZE)
            values = jnp.concatenate([value_t[head_rows, :], ones_rows], axis=0)
            summed = dot(values, weights)
            total = summed[HEAD_SIZE : HEAD_SIZE + 1, :]
            context_t[head_rows, :] = (summed[:HEAD_SIZE, :] * (1.0 / total)).astype(bf16)
            stats[pl.ds(head, 1), :] = peak + jnp.log2(total)
        return carry

    stats[pl.ds(8, 8), :] = jnp.zeros((8, rows), f32)
    lax.fori_loop(0, HEADS // 2 // together, group_step, 0)
    context[...] = context_t[...].T
    half = rows // 2
    for index in range(2):
        where = pl.ds(index * half, half)
        branch = dot(context[where, :], w_out[...]) + b_out
        hat, scale = norm(start[where, :] + branch)
        hat_one[where, :] = hat
        scale_one[where, :] = scale
        normed_low[where, :] = (hat * gain_one + shift_one).astype(bf16)
    chunk = 256
    count = FF // chunk

    def lift(index):
        columns = slice(index * chunk, (index + 1) * chunk)
        return dot(normed_low[...], w_up[:, columns]) + b_up[:, columns]

    following = lift(0)
    for index in range(count):
        lifted = following
        if index + 1 < count:
            following = lift(index + 1)
        columns = pl.ds(index * chunk, chunk)
        cdf, bell = normal_cdf(lifted)
        act = (lifted * cdf).astype(bf16)
        active[:, columns] = act
        slope[:, columns] = (cdf + lifted * bell * 0.3989422804014327).astype(bf16)
        part = dot(act, w_down[columns, :])
        if index == 0:
            dropped[...] = part
        else:
            dropped[...] += part
    for index in range(2):
        where = pl.ds(index * half, half)
        normed = hat_one[where, :] * gain_one + shift_one
        hat, scale = norm(normed + dropped[where, :] + b_down)
        hat_two[where, :] = hat
        scale_two[where, :] = scale
        low = (hat * gain_two + shift_two).astype(bf16)
        put_pieces(low, hidden_out[index * 2 : index * 2 + 2])


def forward(pieces, vectors, *weights):
    rows = PIECES * (pieces[0].shape[0] - 16)
    before = early(pieces[:EARLY], vectors[:4], weights[:3])
    ins = tuple(vectors) + tuple(before) + (pieces[EARLY],) + weights
    outs = (
        shape((rows, D), bf16),
        shape((rows, D), bf16),
        shape((rows, D), bf16),
        shape((rows, D), bf16),
        shape((rows, D), bf16),
        shape((rows, 128), bf16),
        shape((16, rows), f32),
        shape((rows, D), f32),
        shape((rows, 1), f32),
        shape((rows, D), bf16),
        shape((rows, FF), bf16),
        shape((rows, FF), bf16),
        shape((rows, D), f32),
        shape((rows, 1), f32),
        shape((rows, 16), f32),
    ) + back_shapes(rows)
    more = (
        shape((D, rows), bf16),
        shape((D, rows), bf16),
        shape((rows, D), f32),
    )
    first = len(vectors)
    aliases = {first + item: place for item, place in enumerate((7, 0, 1, 2, 3, 5, 14))}
    return run(forward_kernel, "forward_layer", 22, ins, outs, more, aliases=aliases)


LANES = 384
ROWS_DOWN = 192
ROWS_UP = 240
ROWS_PAIR = 144
PAIRS_FIRST = 2


PARTS_DOWN = (192,)
PARTS_UP = (80, 80, 80)
PARTS_PAIR = (80, 64)
WAYS_PAIR = (80, 64)


def tiles(parts):
    return tuple(shape((2, 8, rows, LANES), bf16) for rows in parts)


def put(parts, y, dp, first, value):
    low = 0
    for part in parts:
        high = low + part.shape[2]
        start, stop = max(first, low), min(first + value.shape[0], high)
        if start < stop:
            part[y, dp, start - low : stop - low] = value[start - first : stop - first]
        low = high


def halves_t(values, target):
    rows = values.shape[0]
    turned = values.T
    for dp in range(8):
        for half in range(2):
            low = dp * 96 + half * 48
            target[dp * 48 : dp * 48 + 48, half * rows : (half + 1) * rows] = turned[
                low : low + 48, :
            ]


def halves_wide(values, target):
    rows = values.shape[0]
    block = D // PIECES
    nothing = jnp.zeros((rows, block), bf16)
    for index in range(PIECES):
        piece = values[:, index * block : (index + 1) * block]
        wide = slice(index * LANES, (index + 1) * LANES)
        target[0:rows, wide] = jnp.concatenate([piece, nothing], axis=1)
        target[rows : 2 * rows, wide] = jnp.concatenate([nothing, piece], axis=1)


def down_tiles(left_side, active, target):
    block = D // PIECES
    for pair in range(4):
        part = dot(left_side, active[:, pl.ds(pair * D, D)]).astype(bf16)
        for dp in range(2):
            columns = slice(dp * LANES, dp * LANES + LANES)
            for y in range(2):
                put(target, y, pair * 2 + dp, 0, part[y * block : (y + 1) * block, columns])


def down_kernel(*refs):
    gain, refs = refs[0], refs[1:]
    pieces, (hat_two, scale_two, active, *refs) = refs[:PIECES], refs[PIECES:]
    count = len(PARTS_DOWN)
    grad_z_two, grad_dropped, vectors, left_kept, *refs = refs
    sent, (grad_t,) = refs[:count], refs[count:]
    gain_two = gain[...].reshape(1, D)
    seq = pieces[0].shape[0]
    core = place_bits()[0]
    totals = [jnp.zeros((1, D), f32)] * 3
    for index, piece in enumerate(pieces):
        where = pl.ds(index * seq, seq)
        grad = piece[...].astype(f32)
        hat = hat_two[where, :]
        grad_z = norm_back(grad, hat, scale_two[where, :], gain_two)
        low = grad_z.astype(bf16)
        grad_z_two[where, :] = grad_z
        grad_dropped[where, :] = low
        terms = (grad * hat, grad, low.astype(f32))
        totals = [total + sums(term) for total, term in zip(totals, terms)]
    vectors[...] = jnp.concatenate(totals + [jnp.zeros((5, D), f32)], axis=0)
    block = D // PIECES
    grad_t[...] = grad_dropped[...].T

    def rows_of(order):
        return jnp.concatenate(
            [grad_t[pl.ds(pl.multiple_of(index * block, block), block), :] for index in order],
            axis=0,
        )

    left_kept[...] = rows_of([core, 2 + core])
    down_tiles(rows_of([1 - core, 3 - core]), active, sent)


def down_back(pieces, hat_two, scale_two, active, gain_two):
    rows = PIECES * pieces[0].shape[0]
    ins = (gain_two,) + tuple(pieces) + (hat_two, scale_two, active)
    outs = (
        shape((rows, D), f32),
        shape((rows, D), bf16),
        shape((8, D), f32),
        shape((D // 2, rows), bf16),
        *tiles(PARTS_DOWN),
    )
    more = (shape((D, rows), bf16),)
    return run(down_kernel, "down_back", 7, ins, outs, more)


def lifted_kernel(grad_dropped, w_down, slope, left_kept, active, grad_lifted, grad_b_up, kept):
    block = FF // PIECES
    for index in range(PIECES):
        columns = pl.ds(index * block, block)
        grad = dot_right_t(grad_dropped[...], w_down[columns, :])
        grad = (grad * slope[:, columns].astype(f32)).astype(bf16)
        grad_lifted[:, columns] = grad
        grad_b_up[:, columns] = sums(grad.astype(f32))
    down_tiles(left_kept[...], active, (kept,))


def lifted_back(grad_dropped, w_down, slope, left_kept, active):
    rows = grad_dropped.shape[0]
    ins = (grad_dropped, w_down, slope, left_kept, active)
    outs = (shape((rows, FF), bf16), shape((1, FF), f32), *tiles((ROWS_DOWN,)))
    return run(lifted_kernel, "lifted_back", 5, ins, outs)


def up_tiles(order, normed_t, grad_lifted, context_t, wide, target):
    block = FF // PIECES
    for y, which in enumerate(order):
        columns = pl.ds(pl.multiple_of(which * block, block), block)
        part = dot(normed_t[...], grad_lifted[:, columns]).astype(bf16)
        columns = pl.ds(pl.multiple_of(which * LANES, LANES), LANES)
        extra = dot(context_t[...], wide[:, columns]).astype(bf16)
        for dp in range(8):
            put(target, y, dp, 0, part[dp * 96 : dp * 96 + 96, 0:LANES])
            put(target, y, dp, 96, extra[dp * 48 : dp * 48 + 48, :])
            put(target, y, dp, 144, part[dp * 96 : dp * 96 + 96, LANES:])


def middle_kernel(gain, *refs):
    grad_lifted, w_up, grad_z_two, hat_one, scale_one, context, normed_low, *refs = refs
    grad_z_one, vectors, grad_branch, normed_t, context_t, wide, *sent = refs
    core = place_bits()[0]
    rows = grad_z_two.shape[0]
    half = rows // 2
    gain_one = gain[...].reshape(1, D)
    totals = [jnp.zeros((1, D), f32)] * 3
    normed_t[...] = normed_low[...].T
    halves_t(context[...], context_t)
    for index in range(2):
        where = pl.ds(index * half, half)
        grad = grad_z_two[where, :] + dot_right_t(grad_lifted[where, :], w_up[...])
        hat = hat_one[where, :]
        grad_z = norm_back(grad, hat, scale_one[where, :], gain_one)
        low = grad_z.astype(bf16)
        grad_z_one[where, :] = grad_z
        grad_branch[where, :] = low
        terms = (grad * hat, grad, low.astype(f32))
        totals = [total + sums(term) for total, term in zip(totals, terms)]
    vectors[...] = jnp.concatenate(totals + [jnp.zeros((5, D), f32)], axis=0)
    halves_wide(grad_branch[...], wide)
    up_tiles([1 - core, 3 - core], normed_t, grad_lifted, context_t, wide, sent)


def middle_back(*ins):
    rows = ins[1].shape[0]
    outs = (
        shape((rows, D), f32),
        shape((8, D), f32),
        shape((rows, D), bf16),
        shape((D, rows), bf16),
        shape((D // 2, 2 * rows), bf16),
        shape((2 * rows, 2 * D), bf16),
        *tiles(PARTS_UP),
    )
    return run(middle_kernel, "middle_up_back", 10, ins, outs)


def attention_steps(first, pairs, inside, grads, base=0):
    queries, keyed, valued, key_bias, stats, grad_attended, delta = inside
    grad_q, grad_k, grad_v = grads
    rows = queries.shape[0]
    ones_lane = (lax.broadcasted_iota(jnp.int32, (rows, 128), 1) == 0).astype(bf16)
    low = lane_half(rows, 0)
    nothing = jnp.zeros((rows, 128), bf16)

    def products(head):
        pair, which = head // 2, head % 2
        columns = pl.ds(pair * 128, 128)
        own = lane_half(rows, which)
        query_wide = jnp.concatenate([queries[:, columns], ones_lane], axis=1)
        key_head = jnp.where(own, keyed[:, columns], nothing)
        key_head = jnp.concatenate([key_head, key_bias[...]], axis=1)
        value_head = jnp.where(own, valued[:, columns], nothing)
        return (
            dot_right_t(key_head, query_wide),
            dot_right_t(value_head, grad_attended[:, columns]),
        )

    following = products(2 * first)
    for index in range(pairs):
        pair = first + index
        columns = pl.ds(pair * 128, 128)
        target = pl.ds(base + index * 128, 128)
        query_pair = queries[:, columns]
        key_pair_t = keyed[:, columns].T
        grad_pair = grad_attended[:, columns]
        found = []
        for which in range(2):
            head = 2 * pair + which
            scores, grad_weights = following
            if head + 1 < 2 * (first + pairs):
                following = products(head + 1)
            here = pl.ds(head, 1)
            weights = jnp.exp2(scores - stats[here, :])
            grad_raw = (weights * (grad_weights - delta[here, :])).astype(bf16)
            grad_v_pair = dot(weights.astype(bf16), grad_pair)
            grad_k_pair = dot(grad_raw, query_pair)
            head_rows = slice(which * HEAD_SIZE, which * HEAD_SIZE + HEAD_SIZE)
            grad_q_t = dot(key_pair_t[head_rows, :], grad_raw)
            found.append((grad_q_t, grad_k_pair, grad_v_pair))
        grad_q_t = jnp.concatenate([found[0][0], found[1][0]], axis=0) * HEAD_SIZE ** (-0.5)
        grad_q[:, target] = grad_q_t.T.astype(bf16)
        grad_k_pair = jnp.where(low, found[0][1], found[1][1]) * (1.0 / log_two_e)
        grad_k[:, target] = grad_k_pair.astype(bf16)
        grad_v[:, target] = jnp.where(low, found[0][2], found[1][2]).astype(bf16)


def attention_kernel(first, pairs, *refs):
    inside, refs = refs[:5], refs[5:]
    grad_branch, w_out, context, normed_t, grad_lifted, context_t, wide, *refs = refs
    grad_attended, delta, *grads, kept = refs
    rows = grad_branch.shape[0]
    half = rows // 2
    core = place_bits()[0]
    head = lax.broadcasted_iota(jnp.int32, (16, D), 0)
    feature = lax.broadcasted_iota(jnp.int32, (16, D), 1)
    heads = (feature // HEAD_SIZE == head).astype(bf16)
    for index in range(2):
        where = pl.ds(index * half, half)
        attended = dot_right_t(grad_branch[where, :], w_out[...])
        grad_attended[where, :] = attended.astype(bf16)
        products = attended * context[where, :].astype(f32)
        high = products.astype(bf16)
        rest = (products - high.astype(f32)).astype(bf16)
        delta[:, where] = dot_right_t(heads, high) + dot_right_t(heads, rest)
    attention_steps(first, pairs, (*inside, grad_attended, delta), grads)
    up_tiles([core, 2 + core], normed_t, grad_lifted, context_t, wide, (kept,))


def attention_back(first, pairs, *ins):
    rows = ins[0].shape[0]
    outs = (shape((rows, D), bf16), shape((16, rows), f32))
    outs += (shape((rows, pairs * 128), bf16),) * 3 + tiles((ROWS_UP,))
    kernel = functools.partial(attention_kernel, first, pairs)
    return run(kernel, "attention_back", 0, ins, outs)


def weights_kernel(first, pairs, *refs):
    inside, (entries, *before), refs = refs[:7], refs[7:11], refs[11:]
    merged, (vectors, kept, *refs) = refs[:3], refs[3:]
    sent, refs = refs[: len(PARTS_PAIR)], refs[len(PARTS_PAIR) :]
    entries_t, entries_half, wide_qk, wide_v = refs
    core = place_bits()[0]
    for part, target in zip(before, merged):
        target[:, 0 : first * 128] = part[...]
    attention_steps(first, pairs, inside, merged, first * 128)
    turned = entries[...]
    entries_t[...] = turned.T
    halves_t(turned, entries_half)
    block = D // PIECES
    grad_q, grad_k, grad_v = merged
    for index in range(PIECES):
        piece = slice(index * block, (index + 1) * block)
        wide = slice(index * LANES, (index + 1) * LANES)
        wide_qk[:, wide] = jnp.concatenate([grad_q[:, piece], grad_k[:, piece]], axis=1)
    halves_wide(grad_v[...], wide_v)
    for index, which in enumerate([1 - core, 3 - core, core, 2 + core]):
        columns = pl.ds(pl.multiple_of(which * LANES, LANES), LANES)
        part = dot(entries_t[...], wide_qk[:, columns]).astype(bf16)
        extra = dot(entries_half[...], wide_v[:, columns]).astype(bf16)
        target = (sent, (kept,))[index // 2]
        y = index % 2
        for dp in range(8):
            put(target, y, dp, 0, part[dp * 96 : dp * 96 + 96, :])
            put(target, y, dp, 96, extra[dp * 48 : dp * 48 + 48, :])
    vectors[0:1, :] = sums(grad_q[...].astype(f32))
    vectors[1:2, :] = sums(grad_v[...].astype(f32))


def weights_back(first, pairs, *ins):
    rows = ins[0].shape[0]
    whole = shape((rows, D), bf16)
    outs = (whole,) * 3 + (shape((2, D), f32), *tiles((ROWS_PAIR,)), *tiles(PARTS_PAIR))
    more = (
        shape((D, rows), bf16),
        shape((D // 2, 2 * rows), bf16),
        shape((rows, 2 * D), bf16),
        shape((2 * rows, 2 * D), bf16),
    )
    kernel = functools.partial(weights_kernel, first, pairs)
    return run(kernel, "attention_weights_back", 2.2 * pairs + 4, ins, outs, more)


def start_kernel(*refs):
    w_query, w_key, w_value, grad_z_one, flags, two, one, b_up, late = refs[:9]
    grads, made = refs[9:12], refs[12:]
    *grad_in, vectors = made
    seq = grad_z_one.shape[0] // PIECES
    half = D // 2
    totals = [jnp.zeros((1, D), f32)] * 2
    for step in range(2):
        where = pl.ds(step * 2 * seq, 2 * seq)
        grad = grad_z_one[where, :]
        for value, weight in zip(grads, (w_query, w_key, w_value)):
            grad = grad + dot_right_t(value[where, :], weight[...])
        masked = flags[where, 1:2]
        replaced = flags[where, 2:3]
        terms = (grad * masked, grad * replaced)
        totals = [total + sums(term) for total, term in zip(totals, terms)]
        low = jnp.where(masked > 0, 0.0, grad).astype(bf16)
        put_pieces(low, grad_in[step * 2 : step * 2 + 2])
    rows = totals + [late[...], two[0:3, :], one[0:3, :]]
    rows += [b_up[:, index * D : (index + 1) * D] for index in range(FF // D)]
    rows = jnp.concatenate(rows + [jnp.zeros((2, D), f32)], axis=0)
    vectors[0:16, :] = rows[:, :half]
    vectors[16:32, :] = rows[:, half:]


def start_back(weights, grad_z_one, flags, vectors, grads):
    rows = grad_z_one.shape[0]
    ins = tuple(weights) + (grad_z_one, flags) + tuple(vectors) + tuple(grads)
    outs = (shape((rows // PIECES, D), bf16),) * PIECES + (shape((32, LANES), f32),)
    return run(start_kernel, "start_back", 0, ins, outs)


def swap(value, axis, bit):
    size = lax.axis_size(axis)
    return lax.ppermute(value, axis, [(i, i ^ bit) for i in range(size)])


def swap_turned(value, first):
    blks = lax.axis_size("blk")
    fine = lax.axis_size("dp") // 8
    pairs = []
    for dp in range(lax.axis_size("dp")):
        for blk in range(blks):
            along_dp = (blk % 2 == 0) == first
            other = (dp ^ fine) * blks + blk if along_dp else dp * blks + (blk ^ 2)
            pairs.append((dp * blks + blk, other))
    return lax.ppermute(value, ("dp", "blk"), pairs)


def swap_line(value, first):
    blks = lax.axis_size("blk")
    fine = lax.axis_size("dp") // 8
    pairs = []
    for dp in range(lax.axis_size("dp")):
        for blk in range(blks):
            near = (blk % 2 == 0) == first
            bits = 2 if near else (6 if first else 4)
            pairs.append((dp * blks + blk, (dp ^ (bits * fine)) * blks + blk))
    return lax.ppermute(value, ("dp", "blk"), pairs)


def tie(value, *others):
    return lax.optimization_barrier((value,) + tuple(others))[0]


def spread_kernel(hidden, flags, *out):
    blk = lax.axis_index("blk")
    seq = hidden.shape[1]
    for step in range(PIECES):
        document = blk ^ step
        out[step][0:seq, :] = hidden[document]
        row = flags[pl.ds(document, 1), :]
        out[step][seq : seq + 16, 0:seq] = jnp.concatenate(
            [row, jnp.zeros((15, seq), f32)], axis=0
        ).astype(bf16)
        out[step][seq : seq + 16, seq:] = jnp.zeros((16, hidden.shape[2] - seq), bf16)


def spread(hidden, flags):
    documents, seq, width = hidden.shape
    outs = (shape((seq + 16, width), bf16),) * PIECES
    return run(spread_kernel, "spread_documents", 1, (hidden, flags), outs, (), 2)


def spread_plain_kernel(hidden, *out):
    blk = lax.axis_index("blk")
    for step in range(PIECES):
        out[step][...] = hidden[blk ^ step]


def spread_plain(hidden):
    outs = (shape(hidden.shape[1:], bf16),) * PIECES
    return run(spread_plain_kernel, "spread_grads", 1, (hidden,), outs, (), 2)


def move_pieces(pieces):
    own, *others = pieces
    return [own] + [swap(piece, "blk", step + 1) for step, piece in enumerate(others)]


def collect_kernel(own, near, far, both, out):
    blk = lax.axis_index("blk")
    out[blk] = own[...]
    out[blk ^ 1] = near[...]
    out[blk ^ 2] = far[0]
    out[blk ^ 3] = both[1]


def collect_direct_kernel(*refs):
    blk = lax.axis_index("blk")
    for step in range(PIECES):
        refs[PIECES][blk ^ step] = refs[step][...]


def gather_direct(pieces, late):
    pieces = lax.optimization_barrier((*pieces, *late))[:PIECES]
    back = [swap(pieces[step], "blk", step) for step in range(2, PIECES)]
    late = yield
    back = [swap(tie(pieces[1], *late), "blk", 1)] + back
    late = yield late
    ins = (pieces[0], *(tie(piece, *late) for piece in back))
    outs = (shape((PIECES,) + pieces[0].shape, bf16),)
    yield run(collect_direct_kernel, "collect_documents", 0, ins, outs, (), 2)[0]


def gather_documents(own, near, far):
    late = yield
    near = tie(swap(near, "blk", 1), *late)
    far = tie(swap(far, "blk", 2), *late)
    late = yield (near, far)
    both = tie(swap(far, "blk", 1), *late)
    ins = (own, near, far, both)
    outs = (shape((PIECES,) + own.shape, bf16),)
    yield run(collect_kernel, "collect_documents", 0, ins, outs, (), 2)


def split_vectors(values):
    high = values.astype(bf16)
    return high, (values - high.astype(f32)).astype(bf16)


def sum_kernel(plan, emit, split_in, split_out, wide, n_vectors, *refs):
    kept, *arrived = refs[: 1 + len(split_in)]
    vectors_in = refs[1 + len(split_in) : 1 + len(split_in) + n_vectors]
    made = refs[1 + len(split_in) + n_vectors :]
    rows = sum(split_in)

    def take(source, place, height):
        if isinstance(place, tuple):
            return source[place].astype(f32)
        where = pl.ds(pl.multiple_of(place * height, 16), height)
        return source[where, :].astype(f32)

    plans = plan(*place_bits())
    targets = (made[: len(split_out)], made[len(split_out) : len(split_out) + 1])
    for group, splits, places in zip(targets, (split_out, (rows,)), plans):
        for item, place in enumerate(places):
            other = [take(part, place, height) for part, height in zip(arrived, split_in)]
            other = other[0] if len(other) == 1 else jnp.concatenate(other, axis=0)
            value = take(kept, place, rows) + other
            low = 0
            if emit is None:
                for target, height in zip(group, splits):
                    part = value[low : low + height].astype(bf16)
                    target[item * height : (item + 1) * height, :] = part
                    low += height
    if n_vectors:
        own, other = vectors_in
        if other.dtype == f32:
            vectors = own[...] + other[...]
        else:
            tail = 64 if other.shape[0] % split_in[-1] == 64 % split_in[-1] else 32
            start = other.shape[0] - tail
            vectors = own[...] + other[start : start + 32, :].astype(f32)
            if tail == 64:
                vectors = vectors + other[start + 32 : start + 64, :].astype(f32)
        if emit is None:
            high, low = split_vectors(vectors)
            target = targets[0][-1]
            start = target.shape[0] - (64 if wide else 32)
            target[start : start + 32, :] = high
            kept_vectors = high.astype(f32)
            if wide:
                target[start + 32 : start + 64, :] = low
                kept_vectors = kept_vectors + low.astype(f32)
            made[-1][...] = kept_vectors
        else:
            emit_vectors(vectors, made[len(made) - VECTORS :])
    if emit is not None:
        emit(value, made)


VECTORS = 11


def emit_vectors(vectors, made):
    half = D // 2
    for index, target in enumerate(made):
        for part in range(target.shape[0] // D):
            row = index + part
            target[part * D : part * D + half] = vectors[row : row + 1, :].reshape(half)
            target[part * D + half : part * D + D] = vectors[row + 16 : row + 17, :].reshape(half)


def sum_stage(
    name,
    kept,
    arrived,
    rows,
    plan,
    count,
    vectors=(),
    emit=None,
    outs=None,
    wide=True,
    split_in=None,
    split_out=None,
):
    split_in = split_in or (rows,)
    split_out = split_out or (rows,)
    if outs is None:
        heights = [count * height for height in split_out]
        if vectors:
            heights[-1] += 64 if wide else 32
        outs = tuple(shape((height, LANES), bf16) for height in heights)
        outs += (shape((count * rows, LANES), bf16),)
        if vectors:
            outs += (shape((32, LANES), f32),)
    elif vectors:
        outs = outs + (shape((D,), f32),) * (VECTORS - 1) + (shape((FF,), f32),)
    ins = (kept,) + tuple(arrived) + tuple(vectors)
    kernel = functools.partial(sum_kernel, plan, emit, split_in, split_out, wide, len(vectors))
    return run(kernel, name, 0, ins, outs, (), 4)


def plan_core(core, y, b0, b1, b2):
    def places(mine_x, mine_y):
        return [
            (core * mine_y + (1 - core) * u, i * 4 + j * 2 + core * u + (1 - core) * mine_x)
            for u in (0, 1)
            for i in (0, 1)
            for j in (0, 1)
        ]

    return places(1 - b0, 1 - y), places(b0, y)


def plan_first(core, y, b0, b1, b2):
    u = core * b0 + (1 - core) * y
    return [[v * 4 + item for item in range(4)] for v in (1 - u, u)]


def plan_second(core, y, b0, b1, b2):
    def places(low, high):
        return [core * (high * 2 + u) + (1 - core) * (u * 2 + low) for u in (0, 1)]

    return places(1 - b1, 1 - b2), places(b1, b2)


def plan_third(core, y, b0, b1, b2):
    u = core * b1 + (1 - core) * b2
    return [1 - u], [u]


def plan_last(core, y, b0, b1, b2):
    return ([0],)


def finish_tiles(sends, kept, rows, emit, outs, own=()):
    splits = WAYS_PAIR if len(sends) > 1 else (rows,)
    late = yield tuple(sends)
    got = [tie(swap_turned(send, False), *late) for send in sends]
    both = (own[0], got[-1]) if own else ()
    made = sum_stage(
        "sum_second",
        kept,
        got,
        rows,
        plan_second,
        2,
        both,
        split_in=splits,
        split_out=splits,
    )
    sends, (kept, *own) = made[: len(splits)], made[len(splits) :]
    late = yield tuple(sends)
    got = [tie(swap_line(send, True), *late) for send in sends]
    both = (own[0], got[-1]) if own else ()
    send, kept, *own = sum_stage(
        "sum_third", kept, got, rows, plan_third, 1, both, split_in=splits
    )
    late = yield (send,)
    got = tie(swap_line(send, False), *late)
    both = (own[0], got) if own else ()
    yield sum_stage("sum_last", kept, (got,), rows, plan_last, 1, both, emit, outs)


def reduce_tiles(sent, kept, splits, emit, outs):
    rows = sum(splits)
    late = yield tuple(sent)
    got = [tie(swap(part, "blk", 1), *late) for part in sent]
    send, kept = sum_stage("sum_core", kept[0], got, rows, plan_core, 8, split_in=splits)
    late = yield (send,)
    got = tie(swap_turned(send, True), *late)
    send, kept = sum_stage("sum_first", kept, (got,), rows, plan_first, 4)
    yield from finish_tiles((send,), kept, rows, emit, outs)


def reduce_pair(sent, kept, emit, outs):
    late = yield tuple(sent)
    both = (late[0], tie(swap(late[0], "blk", 1), *late))
    got = [tie(swap(part, "blk", 1), *late) for part in sent]
    *sends, kept, own = sum_stage(
        "sum_core",
        kept,
        got,
        ROWS_PAIR,
        plan_core,
        8,
        both,
        split_in=PARTS_PAIR,
        split_out=WAYS_PAIR,
    )
    late = yield tuple(sends)
    got = [tie(swap_turned(send, True), *late) for send in sends]
    both = (own, got[-1])
    *sends, kept, own = sum_stage(
        "sum_first",
        kept,
        got,
        ROWS_PAIR,
        plan_first,
        4,
        both,
        split_in=WAYS_PAIR,
        split_out=WAYS_PAIR,
    )
    yield from finish_tiles(sends, kept, ROWS_PAIR, emit, outs, (own,))


def emit_down(tile, made):
    made[0][...] = tile.T


def emit_up(tile, made):
    block = D // PIECES
    made[0][:, 0:LANES] = tile[0:96]
    made[0][:, LANES:] = tile[144:240]
    made[1][0:48, :] = tile[96:144, :block]
    made[1][48:96, :] = tile[96:144, block:]


def emit_pair(tile, made):
    block = D // PIECES
    made[0][...] = tile[0:96, :block]
    made[1][...] = tile[0:96, block:]
    made[2][0:48, :] = tile[96:144, :block]
    made[2][48:96, :] = tile[96:144, block:]


def finish_vectors(vectors):
    size = lax.axis_size("dp")
    fine = size // 8
    if fine == 1:
        return vectors
    groups = [[index * fine + item for item in range(fine)] for index in range(8)]
    return lax.psum(tuple(vectors), "dp", axis_index_groups=groups)


def finish(tile, axis):
    size = lax.axis_size("dp")
    fine = size // 8
    if fine == 1:
        return tile
    groups = [[index * fine + item for item in range(fine)] for index in range(8)]
    return lax.psum_scatter(
        tile, "dp", scatter_dimension=axis, axis_index_groups=groups, tiled=True
    )


def local(
    hidden_in,
    pad_mask,
    masked_flag,
    replaced_flag,
    mask_vector,
    replace_vector,
    w_query,
    b_query,
    w_key,
    w_value,
    b_value,
    w_out,
    b_out,
    gain_one,
    shift_one,
    w_up,
    b_up,
    w_down,
    b_down,
    gain_two,
    shift_two,
    out_grad,
):
    codes = (pad_mask + 2 * masked_flag + 4 * replaced_flag).astype(f32)
    spread_in = spread(hidden_in, codes)
    pieces = move_pieces(spread_in)
    grad_pieces = move_pieces(spread_plain(tie(out_grad, *spread_in)))
    vectors = (
        mask_vector,
        replace_vector,
        b_query,
        b_value,
        b_out,
        gain_one,
        shift_one,
        b_down,
        gain_two,
        shift_two,
        b_up,
    )
    (
        entries,
        queries,
        keyed,
        valued,
        context,
        key_bias,
        stats,
        hat_one,
        scale_one,
        normed_low,
        active,
        slope,
        hat_two,
        scale_two,
        flags,
        *hidden_out,
    ) = forward(pieces, vectors, w_query, w_key, w_value, w_out, w_up, w_down)
    grad_z_two, grad_dropped, vectors_two, left_kept, *sent = down_back(
        grad_pieces, hat_two, scale_two, active, gain_two
    )
    block = D // PIECES
    square = shape((D // 8, block), f32)
    outs = (shape((FF // 8, block), f32),)
    kept_down, kept_up = [], []
    down = reduce_tiles(sent, kept_down, PARTS_DOWN, emit_down, outs)
    ties = next(down)
    grad_lifted, grad_b_up, kept = lifted_back(
        tie(grad_dropped, *ties), w_down, slope, left_kept, active
    )
    kept_down.append(kept)
    ties = down.send((grad_b_up,))
    hidden_back = gather_documents(*hidden_out)
    next(hidden_back)
    grad_z_one, vectors_one, grad_branch, normed_t, context_t, wide, *sent = middle_back(
        gain_one,
        grad_lifted,
        w_up,
        tie(grad_z_two, *ties),
        hat_one,
        scale_one,
        context,
        normed_low,
    )
    ties = hidden_back.send((vectors_one,))
    sent = lax.optimization_barrier((*sent, *ties))[: len(sent)]
    outs = (shape((D // 8, D), f32), square)
    up = reduce_tiles(sent, kept_up, PARTS_UP, emit_up, outs)
    ties = next(up)
    attention = (queries, keyed, valued, key_bias, stats)
    grad_attended, delta, *grads, kept = attention_back(
        0,
        PAIRS_FIRST,
        *attention,
        tie(grad_branch, *ties),
        w_out,
        context,
        normed_t,
        grad_lifted,
        context_t,
        wide,
    )
    kept_up.append(kept)
    attention += (grad_attended,)
    ties = down.send((grads[0],))
    ties = up.send(ties)
    (hidden_out,) = hidden_back.send(ties)
    grad_q, grad_k, grad_v, vectors_qv, kept, *sent = weights_back(
        PAIRS_FIRST,
        HEADS // 2 - PAIRS_FIRST,
        *attention,
        tie(delta, hidden_out, *ties),
        entries,
        *grads,
    )
    ties = down.send((vectors_qv,))
    sent = lax.optimization_barrier((*sent, *ties))[: len(sent)]
    pair = reduce_pair(sent, kept, emit_pair, (square,) * 3)
    ties = next(pair)
    *grad_in, vectors = start_back(
        (w_query, w_key, w_value),
        tie(grad_z_one, *ties),
        flags,
        (vectors_two, vectors_one, grad_b_up, vectors_qv),
        (grad_q, grad_k, grad_v),
    )
    ties = down.send((vectors,))
    ties = up.send(ties)
    (grad_w_down,) = down.send(ties)
    ties = pair.send((vectors, grad_w_down))
    ties = up.send(ties)
    ties = pair.send(ties)
    ties = up.send(ties)
    ties = pair.send(ties)
    grad_back = gather_direct(grad_in, ties)
    next(grad_back)
    grad_w_up, grad_w_out = up.send(ties)
    ties = grad_back.send((grad_w_up,))
    ties = pair.send(ties)
    grad_in = grad_back.send(ties)
    grad_w_query, grad_w_key, grad_w_value, *vectors = pair.send((grad_in,))
    vectors = finish_vectors(vectors)
    return (
        hidden_out,
        grad_in,
        vectors[0],
        vectors[1],
        finish(grad_w_query, 0),
        vectors[2],
        finish(grad_w_key, 0),
        finish(grad_w_value, 0),
        vectors[3],
        finish(grad_w_out, 0),
        vectors[9],
        vectors[7],
        vectors[8],
        finish(grad_w_up, 0),
        vectors[10],
        finish(grad_w_down, 0),
        vectors[6],
        vectors[4],
        vectors[5],
    )


def solution(mesh):
    replicated = (P(),) * 17
    placed = (P("dp", "blk", None),) + (P("dp", "blk"),) * 3 + replicated
    placed = placed + (P("dp", "blk", None),)
    tiles = P("dp", "blk")
    rows = P("dp", "blk", None)
    return jax.shard_map(
        local,
        mesh=mesh,
        in_specs=placed,
        out_specs=(
            rows,
            rows,
            P(),
            P(),
            tiles,
            P(),
            tiles,
            tiles,
            P(),
            tiles,
            P(),
            P(),
            P(),
            tiles,
            P(),
            tiles,
            P(),
            P(),
            P(),
        ),
        check_vma=False,
    )
```
